256 devices in a mesh: grp: 8 (over x, core), row: 4 (over y), col: 8 (over z).
Axes of the slice: x: 4, y: 4, z: 8, core: 2. Of those that a mesh axis runs over, the one named last changes fastest.
Arguments:
- amplitudes: bfloat16 [8, 2048, 4608], P('grp', ('row', 'col')), may hold values from -6 to 6
- integrals: bfloat16 [8, 4608, 12288], P('grp', None, ('row', 'col')), may hold values from -0.0546875 to 0.0546875
- block_tiles: int32 [8], replicated, may hold values from 1 to 36, 96 in all
- assign: int32 [8], replicated, may hold values from 0 to 7, each once
Outputs:
- residual: float32 [2048, 12288], P('grp', ('row', 'col'))
The draws below stay inside these ranges and needn't reach their ends.
Inputs may be any that keep to these rules, and one draw needn't show every extreme that they name: `block_tiles`: the entries sum to 96; the largest is exactly 36. Each block b is held in slot assign[b]; the slots form a permutation, and consecutive slots belong to one group in the order of grp.
All inputs are finite; a program needn't handle non-finite values.
Results may differ from the reference program's by a relative error of at most 0.0003.
Values may be sent and summed in bfloat16 or wider, within the bound.
No kernel may reach another device: no remote copies, remote signals or barrier semaphores. Data moves between devices by JAX's collectives and lax.ppermute only.
A program may use at most 128 MiB of HBM per device.

```python
import math
import jax
import jax.numpy as jnp
import numpy as np

NBLK = 8
TP = 128
TILES = 96
ROWS = 2048
CAP = 36


def levels(key, extent, pieces, smallest, high):
    gain, own = 1.0, jax.random.fold_in(key, 6)
    for position, blocks in pieces:
        draws = jnp.exp(jax.random.uniform(jax.random.fold_in(own, position), (blocks,), jnp.float32, smallest / len(pieces), high / len(pieces)))
        gain = gain * jnp.repeat(draws, extent[position] // blocks).reshape([-1 if axis == position else 1 for axis in range(len(extent))])
    return gain


def split_up(amount, total, bound, slope):
    weights = [(1 << 20) // math.isqrt(rank ** slope) + 1 for rank in range(2, amount + 1)]
    spare, given = total - bound - (amount - 1), [1] * (amount - 1)
    while spare > 0:
        free = [i for i in range(amount - 1) if given[i] < bound]
        mass, budget = sum([weights[i] for i in free]), spare
        for i in free:
            extra = min(bound - given[i], max(1, budget * weights[i] // mass), spare)
            given[i] = given[i] + extra
            spare = spare - extra
    return np.array([bound] + given)


def ragged(key, count, total, bound, skew):
    if count == 2:
        one = jax.random.randint(key, (), max(1, total - bound), min(bound, total - 1) + 1)
        return jnp.stack([one, total - one])
    sizes = jnp.asarray(split_up(count, total, bound, skew), jnp.int32)
    twos = (count - 1) // 2
    source_of, taker = sizes[1:1 + 2 * twos:2], sizes[2:2 + 2 * twos:2]
    room = jnp.minimum(source_of - 1, bound - taker)
    shifted = jax.random.randint(jax.random.fold_in(key, 1), (twos,), 0, 1 << 20) % (room + 1)
    sizes = sizes.at[1:1 + 2 * twos:2].set(source_of - shifted).at[2:2 + 2 * twos:2].set(taker + shifted)
    return sizes[jax.random.permutation(jax.random.fold_in(key, 2), count)]


def normal_values(stream_key, shape, width, bound, split=(), kind=jnp.bfloat16):
    drawn = jax.random.normal(stream_key, shape, jnp.float32) * width
    if len(split) > 0:
        drawn = levels(stream_key, shape, split, -0.22, 0.18) * drawn
    return jnp.clip(drawn, min=-bound, max=bound).astype(kind)


def setup_inputs(seed: int = 0) -> dict:
    splits = jax.random.split(jax.random.key(seed), 5)
    return {
        "amplitudes": normal_values(splits[0], (NBLK, ROWS, CAP * TP), 1.0, 6.0, ((0, 8), (1, 32))),
        "integrals": normal_values(splits[1], (NBLK, CAP * TP, TILES * TP), (TILES * TP) ** -0.5, 0.0546875, ((0, 8), (2, 32))),
        "block_tiles": ragged(splits[2], NBLK, TILES, CAP, 2).astype(jnp.int32),
        "assign": jax.random.permutation(splits[3], NBLK).astype(jnp.int32),
    }


def reference(amplitudes, integrals, block_tiles, assign):
    columns = jnp.arange(CAP * TP, dtype=jnp.int32)
    total = jnp.zeros((ROWS, TILES * TP), jnp.float32)
    for block in range(NBLK):
        live = columns < block_tiles[block] * TP
        masked = jnp.where(live[None, :], amplitudes[block], jnp.zeros((), jnp.bfloat16)).astype(jnp.bfloat16)
        held = integrals[assign[block]]
        total = total + jnp.dot(masked, held, preferred_element_type=jnp.float32)
    return total
```

```python
import functools

import jax
import jax.numpy as jnp
from jax import lax
from jax.experimental import pallas as pl
from jax.experimental.pallas import tpu as pltpu
from jax.sharding import PartitionSpec as P

TP = 128
ANY = pl.BlockSpec(memory_space=pl.ANY)
SMEM = pl.BlockSpec(memory_space=pltpu.SMEM)
VMEM = pl.BlockSpec(memory_space=pltpu.VMEM)


def balance(tiles_ref, assign_ref, held_ref, block_ref, groups):
    for b in range(groups):
        held_ref[assign_ref[b]] = tiles_ref[b]
        block_ref[assign_ref[b]] = b
    chips = groups // 2
    held = [held_ref[s] for s in range(groups)]
    total = [held[2 * x] + held[2 * x + 1] for x in range(chips)]
    share = 0
    for x in range(chips):
        share = share + total[x]
    share = share // chips
    running, prefix = 0, []
    for x in range(chips):
        running = running + total[x] - share
        prefix.append(running)
    high = functools.reduce(jnp.maximum, prefix)
    low = functools.reduce(jnp.minimum, prefix)
    middle = lax.shift_right_arithmetic(high + low, jnp.int32(1))
    flow = [p - middle for p in prefix]
    right = [jnp.maximum(flow[x], 0) for x in range(chips)]
    left = [jnp.maximum(-flow[(x - 1) % chips], 0) for x in range(chips)]
    return held, total, right, left


def half(n, core):
    first = lax.shift_right_arithmetic(n + 1, jnp.int32(1))
    if isinstance(core, int):
        return (0, first) if core == 0 else (first, n - first)
    return jnp.where(core == 0, 0, first), jnp.where(core == 0, first, n - first)


def pick(values, index):
    out = values[0]
    for i in range(1, len(values)):
        out = jnp.where(index == i, values[i], out)
    return out


def plan(x, core, total, right, left, own):
    chips = len(total)
    if isinstance(x, int):
        xl, xr = (x - 1) % chips, (x + 1) % chips
        from_left, from_right = right[xl], left[xr]
        left_first, kept_first = total[xl] - right[xl], left[x]
    else:
        xl, xr = lax.rem(x + chips - 1, chips), lax.rem(x + 1, chips)
        from_left, from_right = pick(right, xl), pick(left, xr)
        left_first, kept_first = pick(total, xl) - from_left, pick(left, x)
    l0, nl = half(from_left, core)
    r0, nr = half(from_right, core)
    first = own - half(from_left, 0)[1] - half(from_right, 0)[1]
    k0 = core * first if isinstance(core, int) else jnp.where(core == 0, 0, first)
    return (xl, left_first + l0, nl), (xr, r0, nr), (x, kept_first + k0, own - nl - nr)


def pack_amplitudes(groups, own, tiles_ref, assign_ref, src_ref, out_ref, held_ref, block_ref):
    held, total, right, left = balance(tiles_ref, assign_ref, held_ref, block_ref, groups)
    blocks = [block_ref[s] for s in range(groups)]
    for g in range(groups):
        place = 0
        for chip, start, count in plan(g // 2, g % 2, total, right, left, own):
            n0 = jnp.clip(held[2 * chip] - start, 0, count)
            second = jnp.maximum(start - held[2 * chip], 0)
            for block, tile, many in ((blocks[2 * chip], start, n0), (blocks[2 * chip + 1], second, count - n0)):

                def move(i, carry, block=block, tile=tile, place=place):
                    into = pl.ds(pl.multiple_of((place + i) * TP, TP), TP)
                    out_ref[g, :, into] = src_ref[block, :, pl.ds(pl.multiple_of((tile + i) * TP, TP), TP)]
                    return carry

                lax.fori_loop(0, many, move, 0)
                place = place + many


def tile_rows(index):
    return pl.ds(pl.multiple_of(index * TP, TP), TP)


def send_tiles(groups, own, tiles_ref, assign_ref, mine_ref, other_ref, right_ref, left_ref, held_ref, block_ref, sems):
    held, total, right, left = balance(tiles_ref, assign_ref, held_ref, block_ref, groups)
    group = lax.axis_index("grp")
    x, core = lax.div(group, 2), lax.rem(group, 2)
    border = pick(held[0::2], x)
    go_right, go_left = pick(right, x), pick(left, x)
    r0, nr = half(go_right, core)
    l0, nl = half(go_left, core)
    jobs = []
    for way, (ref, start, count) in enumerate(((right_ref, pick(total, x) - go_right + r0, nr), (left_ref, l0, nl))):
        for i in range(own):
            tile = start + i
            upper = (tile >= border).astype(jnp.int32)
            row = tile - upper * border
            for source, here in ((mine_ref, upper == core), (other_ref, upper != core)):
                jobs.append((jnp.logical_and(i < count, here), source, row, ref, i, way * own + i))
    run_copies(jobs, sems)


def run_copies(jobs, sems):
    for go, source, row, ref, i, sem in jobs:

        @pl.when(go)
        def _():
            pltpu.make_async_copy(source.at[tile_rows(row)], ref.at[pl.ds(i * TP, TP)], sems.at[sem]).start()

    for go, source, row, ref, i, sem in jobs:

        @pl.when(go)
        def _():
            pltpu.make_async_copy(source.at[tile_rows(row)], ref.at[pl.ds(i * TP, TP)], sems.at[sem]).wait()


def join_tiles(groups, own, tiles_ref, assign_ref, mine_ref, other_ref, fl_ref, fr_ref, out_ref, held_ref, block_ref, sems):
    held, total, right, left = balance(tiles_ref, assign_ref, held_ref, block_ref, groups)
    group = lax.axis_index("grp")
    x, core = lax.div(group, 2), lax.rem(group, 2)
    border = pick(held[0::2], x)
    (_, _, nl), (_, _, nr), (_, start, _) = plan(x, core, total, right, left, own)
    jobs = []
    for i in range(own):
        jobs.append((i < nl, fl_ref, i, out_ref, i, i))
        jobs.append((jnp.logical_and(i >= nl, i < nl + nr), fr_ref, jnp.maximum(i - nl, 0), out_ref, i, i))
        tile = jnp.maximum(start + i - nl - nr, 0)
        upper = (tile >= border).astype(jnp.int32)
        row = tile - upper * border
        kept = i >= nl + nr
        jobs.append((jnp.logical_and(kept, upper == core), mine_ref, row, out_ref, i, i))
        jobs.append((jnp.logical_and(kept, upper != core), other_ref, row, out_ref, i, i))
    run_copies(jobs, sems)


def body(amplitudes, integrals, block_tiles, assign):
    groups = assign.shape[0]
    chips = groups // 2
    _, rows, cap = amplitudes.shape
    cols = integrals.shape[2]
    own = 12
    wide = own * TP
    small = [pltpu.SMEM((groups,), jnp.int32)] * 2
    swap = [(g, g ^ 1) for g in range(groups)]
    up = [(g, (g + 2) % groups) for g in range(groups)]
    down = [(g, (g - 2) % groups) for g in range(groups)]

    mine = integrals[0]
    other = lax.ppermute(mine, "grp", swap)
    moved = lax.all_to_all(amplitudes[0].reshape(groups, rows // groups, cap), "grp", 0, 0, tiled=True)
    packed = pl.pallas_call(
        functools.partial(pack_amplitudes, groups, own),
        out_shape=jax.ShapeDtypeStruct((groups, rows // groups, wide), jnp.bfloat16),
        in_specs=[SMEM, SMEM, VMEM],
        out_specs=VMEM,
        scratch_shapes=small,
    )(block_tiles, assign, moved)
    piece = lax.all_to_all(packed, "grp", 0, 0, tiled=True).reshape(rows, wide)
    whole = lax.all_gather(piece, ("row", "col"), axis=0, tiled=True)

    sends = jax.ShapeDtypeStruct((wide, cols), jnp.bfloat16)
    to_right, to_left = pl.pallas_call(
        functools.partial(send_tiles, groups, own),
        out_shape=(sends, sends),
        in_specs=[SMEM, SMEM, ANY, ANY],
        out_specs=(ANY, ANY),
        scratch_shapes=small + [pltpu.SemaphoreType.DMA((2 * own,))],
    )(block_tiles, assign, mine, other)
    from_left = lax.ppermute(to_right, "grp", up)
    from_right = lax.ppermute(to_left, "grp", down)
    held = pl.pallas_call(
        functools.partial(join_tiles, groups, own),
        out_shape=sends,
        in_specs=[SMEM, SMEM, ANY, ANY, ANY, ANY],
        out_specs=ANY,
        scratch_shapes=small + [pltpu.SemaphoreType.DMA((own,))],
    )(block_tiles, assign, mine, other, from_left, from_right)

    partial_sum = jnp.dot(whole, held, preferred_element_type=jnp.float32)
    return lax.psum_scatter(partial_sum, "grp", scatter_dimension=0, tiled=True)


def solution(mesh):
    in_specs = (P("grp", ("row", "col"), None), P("grp", None, ("row", "col")), P(), P())
    out_specs = P("grp", ("row", "col"))
    return jax.shard_map(body, mesh=mesh, in_specs=in_specs, out_specs=out_specs, check_vma=False)
```

```python
import functools

import jax
import jax.numpy as jnp
from jax import lax
from jax.experimental import pallas as pl
from jax.experimental.pallas import tpu as pltpu
from jax.sharding import PartitionSpec as P

TP = 128
ANY = pl.BlockSpec(memory_space=pl.ANY)
SMEM = pl.BlockSpec(memory_space=pltpu.SMEM)
VMEM = pl.BlockSpec(memory_space=pltpu.VMEM)


def balance(tiles_ref, assign_ref, held_ref, block_ref, groups):
    for b in range(groups):
        held_ref[assign_ref[b]] = tiles_ref[b]
        block_ref[assign_ref[b]] = b
    chips = groups // 2
    held = [held_ref[s] for s in range(groups)]
    total = [held[2 * x] + held[2 * x + 1] for x in range(chips)]
    share = 0
    for x in range(chips):
        share = share + total[x]
    share = share // chips
    running, prefix = 0, []
    for x in range(chips):
        running = running + total[x] - share
        prefix.append(running)
    high = functools.reduce(jnp.maximum, prefix)
    low = functools.reduce(jnp.minimum, prefix)
    middle = lax.shift_right_arithmetic(high + low, jnp.int32(1))
    flow = [p - middle for p in prefix]
    right = [jnp.maximum(flow[x], 0) for x in range(chips)]
    left = [jnp.maximum(-flow[(x - 1) % chips], 0) for x in range(chips)]
    return held, total, right, left


def half(n, core):
    first = lax.shift_right_arithmetic(n + 1, jnp.int32(1))
    if isinstance(core, int):
        return (0, first) if core == 0 else (first, n - first)
    return jnp.where(core == 0, 0, first), jnp.where(core == 0, first, n - first)


def pick(values, index):
    out = values[0]
    for i in range(1, len(values)):
        out = jnp.where(index == i, values[i], out)
    return out


def plan(x, core, total, right, left, own):
    chips = len(total)
    if isinstance(x, int):
        xl, xr = (x - 1) % chips, (x + 1) % chips
        from_left, from_right = right[xl], left[xr]
        left_first, kept_first = total[xl] - right[xl], left[x]
    else:
        xl, xr = lax.rem(x + chips - 1, chips), lax.rem(x + 1, chips)
        from_left, from_right = pick(right, xl), pick(left, xr)
        left_first, kept_first = pick(total, xl) - from_left, pick(left, x)
    l0, nl = half(from_left, core)
    r0, nr = half(from_right, core)
    first = own - half(from_left, 0)[1] - half(from_right, 0)[1]
    k0 = core * first if isinstance(core, int) else jnp.where(core == 0, 0, first)
    return (xl, left_first + l0, nl), (xr, r0, nr), (x, kept_first + k0, own - nl - nr)


def pack_amplitudes(groups, own, tiles_ref, assign_ref, src_ref, out_ref, held_ref, block_ref):
    held, total, right, left = balance(tiles_ref, assign_ref, held_ref, block_ref, groups)
    blocks = [block_ref[s] for s in range(groups)]
    for g in range(groups):
        place = 0
        for chip, start, count in plan(g // 2, g % 2, total, right, left, own):
            n0 = jnp.clip(held[2 * chip] - start, 0, count)
            second = jnp.maximum(start - held[2 * chip], 0)
            for block, tile, many in ((blocks[2 * chip], start, n0), (blocks[2 * chip + 1], second, count - n0)):

                def move(i, carry, block=block, tile=tile, place=place):
                    into = pl.ds(pl.multiple_of((place + i) * TP, TP), TP)
                    out_ref[g, :, into] = src_ref[block, :, pl.ds(pl.multiple_of((tile + i) * TP, TP), TP)]
                    return carry

                lax.fori_loop(0, many, move, 0)
                place = place + many


def tile_rows(index):
    return pl.ds(pl.multiple_of(index * TP, TP), TP)


def copy_run(border, core, start, count, mine_ref, other_ref, out_ref, place):
    lower = jnp.clip(border - start, 0, count)
    for upper, tile, many, at in ((0, start, lower, place), (1, jnp.maximum(start - border, 0), count - lower, place + lower)):
        for source, here in ((mine_ref, core == upper), (other_ref, core != upper)):

            def move(i, carry, source=source, tile=tile, at=at):
                out_ref[tile_rows(at + i), :] = source[tile_rows(tile + i), :]
                return carry

            lax.fori_loop(0, jnp.where(here, many, 0), move, 0)


def send_tiles(groups, own, tiles_ref, assign_ref, mine_ref, other_ref, right_ref, left_ref, held_ref, block_ref):
    held, total, right, left = balance(tiles_ref, assign_ref, held_ref, block_ref, groups)
    group = lax.axis_index("grp")
    x, core = lax.div(group, 2), lax.rem(group, 2)
    border = pick(held[0::2], x)
    go_right, go_left = pick(right, x), pick(left, x)
    r0, nr = half(go_right, core)
    l0, nl = half(go_left, core)
    copy_run(border, core, pick(total, x) - go_right + r0, nr, mine_ref, other_ref, right_ref, 0)
    copy_run(border, core, l0, nl, mine_ref, other_ref, left_ref, 0)


def join_tiles(groups, own, tiles_ref, assign_ref, mine_ref, other_ref, fl_ref, fr_ref, out_ref, held_ref, block_ref):
    held, total, right, left = balance(tiles_ref, assign_ref, held_ref, block_ref, groups)
    group = lax.axis_index("grp")
    x, core = lax.div(group, 2), lax.rem(group, 2)
    border = pick(held[0::2], x)
    (_, _, nl), (_, _, nr), (_, start, count) = plan(x, core, total, right, left, own)
    for source, many, place in ((fl_ref, nl, 0), (fr_ref, nr, nl)):

        def move(i, carry, source=source, place=place):
            out_ref[tile_rows(place + i), :] = source[tile_rows(i), :]
            return carry

        lax.fori_loop(0, many, move, 0)
    copy_run(border, core, start, count, mine_ref, other_ref, out_ref, nl + nr)


def multiply(ny, nz, rows, *refs):
    zs, ys, (b_ref, keep_ref, send_ref) = refs[:ny], refs[ny : ny + nz], refs[ny + nz :]
    group, y, z = lax.axis_index("grp"), lax.axis_index("row"), lax.axis_index("col")
    x, core = lax.div(group, 2), lax.rem(group, 2)
    wide = zs[0].shape[1]
    part = rows * nz // 2
    for r in range(ny):
        d = lax.rem(y + r - x + ny, ny)
        out = jnp.dot(zs[r][...], b_ref[:wide, :], preferred_element_type=jnp.float32)
        keep_ref[d] = jnp.where(core == 0, out[:part], out[part:])
        send_ref[d] = jnp.where(core == 0, out[part:], out[:part])
    for r in range(nz):
        at = lax.rem(z + r, nz)
        side = lax.div(at, nz // 2)
        into = pl.ds(pl.multiple_of(lax.rem(at, nz // 2) * rows, rows), rows)
        out = jnp.dot(ys[r][...], b_ref[wide:, :], preferred_element_type=jnp.float32)
        for ref, here in ((keep_ref, side == core), (send_ref, side != core)):

            @pl.when(here)
            def _(ref=ref, out=out):
                for q in range(ny):
                    d = lax.rem(q - x + ny, ny)
                    ref[d, into, :] += out[q * rows : (q + 1) * rows]


def steps(n):
    return [(i, (i + 1) % n) for i in range(n)], [(i, (i - 1) % n) for i in range(n)]


def ring(block, axis, n):
    up, down = steps(n)
    out = [block] * n
    a = b = block
    for s in range(1, n // 2):
        a, b = lax.ppermute(a, axis, up), lax.ppermute(b, axis, down)
        out[n - s], out[s] = a, b
    h = block.shape[0] // 2
    ta, tb = lax.ppermute(a[:h], axis, up), lax.ppermute(b[h:], axis, down)
    out[n // 2] = jnp.concatenate([ta, tb], axis=0)
    return out


def body(amplitudes, integrals, block_tiles, assign):
    groups = assign.shape[0]
    _, rows, cap = amplitudes.shape
    cols = integrals.shape[2]
    ny, nz = lax.axis_size("row"), lax.axis_size("col")
    own = 12
    wide = own * TP
    split = 7 * TP
    small = [pltpu.SMEM((groups,), jnp.int32)] * 2
    swap = [(g, g ^ 1) for g in range(groups)]
    up = [(g, (g + 2) % groups) for g in range(groups)]
    down = [(g, (g - 2) % groups) for g in range(groups)]
    limit = pltpu.CompilerParams(vmem_limit_bytes=24 * 2**20)

    mine = integrals[0]
    other = lax.ppermute(mine, "grp", swap)
    moved = lax.all_to_all(amplitudes[0].reshape(groups, rows // groups, cap), "grp", 0, 0, tiled=True)
    packed = pl.pallas_call(
        functools.partial(pack_amplitudes, groups, own),
        out_shape=jax.ShapeDtypeStruct((groups, rows // groups, wide), jnp.bfloat16),
        in_specs=[SMEM, SMEM, VMEM],
        out_specs=VMEM,
        scratch_shapes=small,
    )(block_tiles, assign, moved)
    piece = lax.all_to_all(packed, "grp", 0, 0, tiled=True).reshape(rows, wide)

    sends = jax.ShapeDtypeStruct((wide, cols), jnp.bfloat16)
    to_right, to_left = pl.pallas_call(
        functools.partial(send_tiles, groups, own),
        out_shape=(sends, sends),
        in_specs=[SMEM, SMEM, VMEM, VMEM],
        out_specs=(VMEM, VMEM),
        scratch_shapes=small,
        compiler_params=limit,
    )(block_tiles, assign, mine, other)
    from_left = lax.ppermute(to_right, "grp", up)
    from_right = lax.ppermute(to_left, "grp", down)
    held = pl.pallas_call(
        functools.partial(join_tiles, groups, own),
        out_shape=sends,
        in_specs=[SMEM, SMEM, VMEM, VMEM, VMEM, VMEM],
        out_specs=VMEM,
        scratch_shapes=small,
        compiler_params=limit,
    )(block_tiles, assign, mine, other, from_left, from_right)

    y_line = lax.all_gather(piece[:, split:], "row", axis=0, tiled=True)
    z_line = lax.all_gather(piece[:, :split], "col", axis=0, tiled=True)
    zs = ring(z_line, "row", ny)
    ys = ring(y_line, "col", nz)
    half_rows = rows * nz // 2
    kept = jax.ShapeDtypeStruct((ny, half_rows, cols), jnp.float32)
    keep, send = pl.pallas_call(
        functools.partial(multiply, ny, nz, rows),
        out_shape=(kept, kept),
        in_specs=[VMEM] * (ny + nz + 1),
        out_specs=(VMEM, VMEM),
        compiler_params=pltpu.CompilerParams(vmem_limit_bytes=32 * 2**20),
    )(*zs, *ys, held)

    p = keep + lax.ppermute(send, "grp", swap)
    h = half_rows // 2
    a = lax.ppermute(jnp.concatenate([p[2, :h], p[1, h:]]), "grp", up)
    b = lax.ppermute(jnp.concatenate([p[2, h:], p[3, :h]]), "grp", down)
    a2 = lax.ppermute(p[1, :h] + a[:h], "grp", up)
    b2 = lax.ppermute(p[3, h:] + b[:h], "grp", down)
    return p[0] + jnp.concatenate([a2, a[h:]]) + jnp.concatenate([b[h:], b2])


def solution(mesh):
    in_specs = (P("grp", ("row", "col"), None), P("grp", None, ("row", "col")), P(), P())
    out_specs = P("grp", ("row", "col"))
    return jax.shard_map(body, mesh=mesh, in_specs=in_specs, out_specs=out_specs, check_vma=False)
```

```python
import functools

import jax
import jax.numpy as jnp
from jax import lax
from jax.experimental import pallas as pl
from jax.experimental.pallas import tpu as pltpu
from jax.sharding import PartitionSpec as P

TP = 128
ANY = pl.BlockSpec(memory_space=pl.ANY)
SMEM = pl.BlockSpec(memory_space=pltpu.SMEM)
VMEM = pl.BlockSpec(memory_space=pltpu.VMEM)


def balance(tiles_ref, assign_ref, held_ref, block_ref, groups):
    for b in range(groups):
        held_ref[assign_ref[b]] = tiles_ref[b]
        block_ref[assign_ref[b]] = b
    chips = groups // 2
    held = [held_ref[s] for s in range(groups)]
    total = [held[2 * x] + held[2 * x + 1] for x in range(chips)]
    share = 0
    for x in range(chips):
        share = share + total[x]
    share = share // chips
    running, prefix = 0, []
    for x in range(chips):
        running = running + total[x] - share
        prefix.append(running)
    high = functools.reduce(jnp.maximum, prefix)
    low = functools.reduce(jnp.minimum, prefix)
    middle = lax.shift_right_arithmetic(high + low, jnp.int32(1))
    flow = [p - middle for p in prefix]
    right = [jnp.maximum(flow[x], 0) for x in range(chips)]
    left = [jnp.maximum(-flow[(x - 1) % chips], 0) for x in range(chips)]
    return held, total, right, left


def half(n, core):
    first = lax.shift_right_arithmetic(n + 1, jnp.int32(1))
    if isinstance(core, int):
        return (0, first) if core == 0 else (first, n - first)
    return jnp.where(core == 0, 0, first), jnp.where(core == 0, first, n - first)


def pick(values, index):
    out = values[0]
    for i in range(1, len(values)):
        out = jnp.where(index == i, values[i], out)
    return out


def plan(x, core, total, right, left, own):
    chips = len(total)
    if isinstance(x, int):
        xl, xr = (x - 1) % chips, (x + 1) % chips
        from_left, from_right = right[xl], left[xr]
        left_first, kept_first = total[xl] - right[xl], left[x]
    else:
        xl, xr = lax.rem(x + chips - 1, chips), lax.rem(x + 1, chips)
        from_left, from_right = pick(right, xl), pick(left, xr)
        left_first, kept_first = pick(total, xl) - from_left, pick(left, x)
    l0, nl = half(from_left, core)
    r0, nr = half(from_right, core)
    first = own - half(from_left, 0)[1] - half(from_right, 0)[1]
    k0 = core * first if isinstance(core, int) else jnp.where(core == 0, 0, first)
    return (xl, left_first + l0, nl), (xr, r0, nr), (x, kept_first + k0, own - nl - nr)


def pack_amplitudes(groups, own, tiles_ref, assign_ref, src_ref, out_ref, held_ref, block_ref):
    held, total, right, left = balance(tiles_ref, assign_ref, held_ref, block_ref, groups)
    blocks = [block_ref[s] for s in range(groups)]
    group = lax.axis_index("grp")
    x, core = lax.div(group, 2), lax.rem(group, 2)
    chips = groups // 2
    for g in range(groups):
        place = lax.rem(g // 2 - x + chips, chips) * own
        side = jnp.where(core == g % 2, 0, 1)
        for chip, start, count in plan(g // 2, g % 2, total, right, left, own):
            n0 = jnp.clip(held[2 * chip] - start, 0, count)
            second = jnp.maximum(start - held[2 * chip], 0)
            for block, tile, many in ((blocks[2 * chip], start, n0), (blocks[2 * chip + 1], second, count - n0)):

                def move(i, carry, block=block, tile=tile, place=place):
                    into = pl.ds(pl.multiple_of((place + i) * TP, TP), TP)
                    out_ref[side, :, into] = src_ref[block, :, pl.ds(pl.multiple_of((tile + i) * TP, TP), TP)]
                    return carry

                lax.fori_loop(0, many, move, 0)
                place = place + many


def tile_rows(index):
    return pl.ds(pl.multiple_of(index * TP, TP), TP)


def copy_run(border, core, start, count, mine_ref, other_ref, out_ref, place):
    lower = jnp.clip(border - start, 0, count)
    for upper, tile, many, at in ((0, start, lower, place), (1, jnp.maximum(start - border, 0), count - lower, place + lower)):
        for source, here in ((mine_ref, core == upper), (other_ref, core != upper)):

            def move(i, carry, source=source, tile=tile, at=at):
                out_ref[tile_rows(at + i), :] = source[tile_rows(tile + i), :]
                return carry

            lax.fori_loop(0, jnp.where(here, many, 0), move, 0)


def send_tiles(groups, own, tiles_ref, assign_ref, mine_ref, other_ref, right_ref, left_ref, held_ref, block_ref):
    held, total, right, left = balance(tiles_ref, assign_ref, held_ref, block_ref, groups)
    group = lax.axis_index("grp")
    x, core = lax.div(group, 2), lax.rem(group, 2)
    border = pick(held[0::2], x)
    go_right, go_left = pick(right, x), pick(left, x)
    r0, nr = half(go_right, core)
    l0, nl = half(go_left, core)
    copy_run(border, core, pick(total, x) - go_right + r0, nr, mine_ref, other_ref, right_ref, 0)
    copy_run(border, core, l0, nl, mine_ref, other_ref, left_ref, 0)


def join_tiles(groups, own, tiles_ref, assign_ref, mine_ref, other_ref, fl_ref, fr_ref, out_ref, held_ref, block_ref):
    held, total, right, left = balance(tiles_ref, assign_ref, held_ref, block_ref, groups)
    group = lax.axis_index("grp")
    x, core = lax.div(group, 2), lax.rem(group, 2)
    border = pick(held[0::2], x)
    (_, _, nl), (_, _, nr), (_, start, count) = plan(x, core, total, right, left, own)
    for source, many, place in ((fl_ref, nl, 0), (fr_ref, nr, nl)):

        def move(i, carry, source=source, place=place):
            out_ref[tile_rows(place + i), :] = source[tile_rows(i), :]
            return carry

        lax.fori_loop(0, many, move, 0)
    copy_run(border, core, start, count, mine_ref, other_ref, out_ref, nl + nr)


def multiply(ny, nz, *refs):
    zs, ys, (b0, b1, b2, b3, b4, out_ref, za_ref, ya_ref) = refs[:ny], refs[ny : ny + nz], refs[ny + nz :]
    group, y, z = lax.axis_index("grp"), lax.axis_index("row"), lax.axis_index("col")
    core = lax.rem(group, 2)
    zrows, zwide = zs[0].shape
    yrows = ys[0].shape[0]
    rows = yrows // ny
    for r in range(ny):
        za_ref[r * zrows : (r + 1) * zrows, :] = zs[r][...]
    for r in range(nz):
        ya_ref[r * yrows : (r + 1) * yrows, :] = ys[r][...]

    def runs(a_ref, parts):
        at, out = 0, None
        for part in parts:
            term = jnp.dot(a_ref[:, at : at + part.shape[0]], part[...], preferred_element_type=jnp.float32)
            out = term if out is None else out + term
            at += part.shape[0]
        return out

    cut = zwide - b0.shape[0] - b1.shape[0]
    out = runs(za_ref, (b0, b1, b2.at[:cut]))
    for r in range(ny):
        at_y = lax.rem(y + r, ny)
        for q in range(nz):
            at = lax.rem(z + q, nz)
            side = jnp.where(lax.div(at, nz // 2) == core, 0, 1)
            first = r * zrows + q * rows
            out_ref[side, at_y, lax.rem(at, nz // 2)] = out[first : first + rows]
    out = runs(ya_ref, (b2.at[cut:], b3, b4))
    for q in range(nz):
        at = lax.rem(z + q, nz)
        side = jnp.where(lax.div(at, nz // 2) == core, 0, 1)
        for r in range(ny):
            first = q * yrows + r * rows
            out_ref[side, r, lax.rem(at, nz // 2)] += out[first : first + rows]


def steps(n):
    return [(i, (i + 1) % n) for i in range(n)], [(i, (i - 1) % n) for i in range(n)]


def ring(block, axis, up, down, half_way):
    n = len(up) if axis != "grp" else len(up) // 2
    out = [block] * n
    a = b = block
    for s in range(1, n // 2):
        a, b = lax.ppermute(a, axis, up), lax.ppermute(b, axis, down)
        out[n - s], out[s] = a, b
    h = block.shape[0] // 2
    ta, tb = lax.ppermute(a[:h], axis, up), lax.ppermute(b[h:], axis, down)
    out[n // 2] = (ta, tb) if half_way else jnp.concatenate([ta, tb], axis=0)
    return out


def body(amplitudes, integrals, block_tiles, assign):
    groups = assign.shape[0]
    chips = groups // 2
    _, rows, cap = amplitudes.shape
    cols = integrals.shape[2]
    ny, nz = lax.axis_size("row"), lax.axis_size("col")
    own = 12
    wide = own * TP
    split = 28 * TP
    octet = rows // groups
    small = [pltpu.SMEM((groups,), jnp.int32)] * 2
    swap = [(g, g ^ 1) for g in range(groups)]
    up = [(g, (g + 2) % groups) for g in range(groups)]
    down = [(g, (g - 2) % groups) for g in range(groups)]
    limit = pltpu.CompilerParams(vmem_limit_bytes=24 * 2**20)
    core = lax.rem(lax.axis_index("grp"), 2)

    mine = integrals[0]
    other = lax.ppermute(mine, "grp", swap)
    moved = lax.all_to_all(amplitudes[0].reshape(groups, octet, cap), "grp", 0, 0, tiled=True)
    packed = pl.pallas_call(
        functools.partial(pack_amplitudes, groups, own),
        out_shape=jax.ShapeDtypeStruct((2, octet, chips * wide), jnp.bfloat16),
        in_specs=[SMEM, SMEM, VMEM],
        out_specs=VMEM,
        scratch_shapes=small,
    )(block_tiles, assign, moved)

    sends = jax.ShapeDtypeStruct((wide, cols), jnp.bfloat16)
    to_right, to_left = pl.pallas_call(
        functools.partial(send_tiles, groups, own),
        out_shape=(sends, sends),
        in_specs=[SMEM, SMEM, VMEM, VMEM],
        out_specs=(VMEM, VMEM),
        scratch_shapes=small,
        compiler_params=limit,
    )(block_tiles, assign, mine, other)
    packed, to_right, to_left = lax.optimization_barrier((packed, to_right, to_left))
    from_left = lax.ppermute(to_right, "grp", up)
    from_right = lax.ppermute(to_left, "grp", down)

    theirs = lax.ppermute(packed[1], "grp", swap)
    piece = jnp.where(core == 0, jnp.concatenate([packed[0], theirs]), jnp.concatenate([theirs, packed[0]]))
    y_line = lax.all_gather(piece[:, split:], "row", axis=0, tiled=True)
    z_line = jnp.concatenate(ring(piece[:, :split], "col", *steps(nz), False))

    held = pl.pallas_call(
        functools.partial(join_tiles, groups, own),
        out_shape=sends,
        in_specs=[SMEM, SMEM, VMEM, VMEM, VMEM, VMEM],
        out_specs=VMEM,
        scratch_shapes=small,
        compiler_params=limit,
    )(block_tiles, assign, mine, other, from_left, from_right)
    y_line, z_line, held = lax.optimization_barrier((y_line, z_line, held))

    zs = ring(z_line, "row", *steps(ny), False)
    ys = ring(y_line, "col", *steps(nz), False)
    b0, b1, (b2, b3), b4 = ring(held, "grp", up, down, True)
    sums = pl.pallas_call(
        functools.partial(multiply, ny, nz),
        out_shape=jax.ShapeDtypeStruct((2, ny, nz // 2, 2 * octet, cols), jnp.float32),
        in_specs=[VMEM] * (ny + nz + 5),
        out_specs=VMEM,
        scratch_shapes=[
            pltpu.VMEM((2 * octet * ny * nz, split), jnp.bfloat16),
            pltpu.VMEM((2 * octet * ny * nz, chips * wide - split), jnp.bfloat16),
        ],
        compiler_params=pltpu.CompilerParams(vmem_limit_bytes=40 * 2**20),
    )(*zs, *ys, b0, b1, b2, b3, b4)

    done = sums[0] + lax.ppermute(sums[1], "grp", swap)
    lines = [[2 * x + c for x in range(chips)] for c in range(2)]
    got = lax.all_to_all(done, "grp", 0, 0, axis_index_groups=lines, tiled=True)
    return got.transpose(1, 0, 2, 3).reshape(nz // 2 * chips * 2 * octet, cols)


def solution(mesh):
    in_specs = (P("grp", ("row", "col"), None), P("grp", None, ("row", "col")), P(), P())
    out_specs = P("grp", ("row", "col"))
    return jax.shard_map(body, mesh=mesh, in_specs=in_specs, out_specs=out_specs, check_vma=False)
```

```python
import functools

import jax
import jax.numpy as jnp
from jax import lax
from jax.experimental import pallas as pl
from jax.experimental.pallas import tpu as pltpu
from jax.sharding import PartitionSpec as P

TP = 128
ANY = pl.BlockSpec(memory_space=pl.ANY)
SMEM = pl.BlockSpec(memory_space=pltpu.SMEM)
VMEM = pl.BlockSpec(memory_space=pltpu.VMEM)


def balance(tiles_ref, assign_ref, held_ref, block_ref, groups):
    for b in range(groups):
        held_ref[assign_ref[b]] = tiles_ref[b]
        block_ref[assign_ref[b]] = b
    chips = groups // 2
    held = [held_ref[s] for s in range(groups)]
    total = [held[2 * x] + held[2 * x + 1] for x in range(chips)]
    share = 0
    for x in range(chips):
        share = share + total[x]
    share = share // chips
    running, prefix = 0, []
    for x in range(chips):
        running = running + total[x] - share
        prefix.append(running)
    high = functools.reduce(jnp.maximum, prefix)
    low = functools.reduce(jnp.minimum, prefix)
    middle = lax.shift_right_arithmetic(high + low, jnp.int32(1))
    flow = [p - middle for p in prefix]
    right = [jnp.maximum(flow[x], 0) for x in range(chips)]
    left = [jnp.maximum(-flow[(x - 1) % chips], 0) for x in range(chips)]
    return held, total, right, left


def half(n, core):
    first = lax.shift_right_arithmetic(n + 1, jnp.int32(1))
    if isinstance(core, int):
        return (0, first) if core == 0 else (first, n - first)
    return jnp.where(core == 0, 0, first), jnp.where(core == 0, first, n - first)


def pick(values, index):
    out = values[0]
    for i in range(1, len(values)):
        out = jnp.where(index == i, values[i], out)
    return out


def plan(x, core, total, right, left, own):
    chips = len(total)
    if isinstance(x, int):
        xl, xr = (x - 1) % chips, (x + 1) % chips
        from_left, from_right = right[xl], left[xr]
        left_first, kept_first = total[xl] - right[xl], left[x]
    else:
        xl, xr = lax.rem(x + chips - 1, chips), lax.rem(x + 1, chips)
        from_left, from_right = pick(right, xl), pick(left, xr)
        left_first, kept_first = pick(total, xl) - from_left, pick(left, x)
    l0, nl = half(from_left, core)
    r0, nr = half(from_right, core)
    first = own - half(from_left, 0)[1] - half(from_right, 0)[1]
    k0 = core * first if isinstance(core, int) else jnp.where(core == 0, 0, first)
    return (xl, left_first + l0, nl), (xr, r0, nr), (x, kept_first + k0, own - nl - nr)


def pack_amplitudes(groups, own, tiles_ref, assign_ref, src_ref, out_ref, held_ref, block_ref):
    held, total, right, left = balance(tiles_ref, assign_ref, held_ref, block_ref, groups)
    blocks = [block_ref[s] for s in range(groups)]
    for g in range(groups):
        place = 0
        for chip, start, count in plan(g // 2, g % 2, total, right, left, own):
            n0 = jnp.clip(held[2 * chip] - start, 0, count)
            second = jnp.maximum(start - held[2 * chip], 0)
            for block, tile, many in ((blocks[2 * chip], start, n0), (blocks[2 * chip + 1], second, count - n0)):

                def move(i, carry, block=block, tile=tile, place=place):
                    into = pl.ds(pl.multiple_of((place + i) * TP, TP), TP)
                    out_ref[g, :, into] = src_ref[block, :, pl.ds(pl.multiple_of((tile + i) * TP, TP), TP)]
                    return carry

                lax.fori_loop(0, many, move, 0)
                place = place + many


def tile_rows(index):
    return pl.ds(pl.multiple_of(index * TP, TP), TP)


def copy_run(border, core, start, count, mine_ref, other_ref, out_ref, place):
    lower = jnp.clip(border - start, 0, count)
    for upper, tile, many, at in ((0, start, lower, place), (1, jnp.maximum(start - border, 0), count - lower, place + lower)):
        for source, here in ((mine_ref, core == upper), (other_ref, core != upper)):

            def move(i, carry, source=source, tile=tile, at=at):
                out_ref[tile_rows(at + i), :] = source[tile_rows(tile + i), :]
                return carry

            lax.fori_loop(0, jnp.where(here, many, 0), move, 0)


def send_tiles(groups, own, tiles_ref, assign_ref, mine_ref, other_ref, right_ref, left_ref, held_ref, block_ref):
    held, total, right, left = balance(tiles_ref, assign_ref, held_ref, block_ref, groups)
    group = lax.axis_index("grp")
    x, core = lax.div(group, 2), lax.rem(group, 2)
    border = pick(held[0::2], x)
    go_right, go_left = pick(right, x), pick(left, x)
    r0, nr = half(go_right, core)
    l0, nl = half(go_left, core)
    copy_run(border, core, pick(total, x) - go_right + r0, nr, mine_ref, other_ref, right_ref, 0)
    copy_run(border, core, l0, nl, mine_ref, other_ref, left_ref, 0)


def join_tiles(groups, own, tiles_ref, assign_ref, mine_ref, other_ref, fl_ref, fr_ref, out_ref, held_ref, block_ref):
    held, total, right, left = balance(tiles_ref, assign_ref, held_ref, block_ref, groups)
    group = lax.axis_index("grp")
    x, core = lax.div(group, 2), lax.rem(group, 2)
    border = pick(held[0::2], x)
    (_, _, nl), (_, _, nr), (_, start, count) = plan(x, core, total, right, left, own)
    for source, many, place in ((fl_ref, nl, 0), (fr_ref, nr, nl)):

        def move(i, carry, source=source, place=place):
            out_ref[tile_rows(place + i), :] = source[tile_rows(i), :]
            return carry

        lax.fori_loop(0, many, move, 0)
    copy_run(border, core, start, count, mine_ref, other_ref, out_ref, nl + nr)


def multiply(ny, nz, rows, *refs):
    refs, (b_ref, keep_ref, send_ref) = refs[:-3], refs[-3:]
    group, y, z = lax.axis_index("grp"), lax.axis_index("row"), lax.axis_index("col")
    x, core = lax.div(group, 2), lax.rem(group, 2)
    near = jnp.where(core == 0, 1, ny - 1)
    far = ny - near
    opposite = nz // 2
    places = [[(0, 0), (2, 0)]]
    for s in range(1, opposite):
        places += [[(0, nz - s), (2, nz - s)], [(0, s), (2, s)]]
    places += [[(0, opposite)], [(2, opposite)], [(near, 0), (far, 0)]]
    for s in range(1, opposite):
        places += [[(near, nz - s), (far, nz - s), (near, s), (far, s)]]
    places += [[(near, opposite), (far, opposite)]]
    for ref, held in zip(refs, places, strict=True):
        out = jnp.dot(ref[...].reshape(len(held) * rows, ref.shape[-1]), b_ref[...], preferred_element_type=jnp.float32)
        for i, (up_y, up_z) in enumerate(held):
            d = lax.rem(y + up_y - x + ny, ny)
            at = lax.rem(z + up_z, nz)
            into = pl.ds(pl.multiple_of(lax.rem(at, nz // 2) * rows, rows), rows)
            side = lax.div(at, nz // 2)
            for to, here in ((keep_ref, side == core), (send_ref, side != core)):

                @pl.when(here)
                def _(to=to, out=out, i=i, d=d, into=into):
                    to[d, into, :] = out[i * rows : (i + 1) * rows]


def steps(n):
    return [(i, (i + 1) % n) for i in range(n)], [(i, (i - 1) % n) for i in range(n)]


def body(amplitudes, integrals, block_tiles, assign):
    groups = assign.shape[0]
    _, rows, cap = amplitudes.shape
    cols = integrals.shape[2]
    ny, nz = lax.axis_size("row"), lax.axis_size("col")
    own = 12
    wide = own * TP
    small = [pltpu.SMEM((groups,), jnp.int32)] * 2
    swap = [(g, g ^ 1) for g in range(groups)]
    up = [(g, (g + 2) % groups) for g in range(groups)]
    down = [(g, (g - 2) % groups) for g in range(groups)]
    limit = pltpu.CompilerParams(vmem_limit_bytes=24 * 2**20)

    mine = integrals[0]
    other = lax.ppermute(mine, "grp", swap)
    moved = lax.all_to_all(amplitudes[0].reshape(groups, rows // groups, cap), "grp", 0, 0, tiled=True)
    packed = pl.pallas_call(
        functools.partial(pack_amplitudes, groups, own),
        out_shape=jax.ShapeDtypeStruct((groups, rows // groups, wide), jnp.bfloat16),
        in_specs=[SMEM, SMEM, VMEM],
        out_specs=VMEM,
        scratch_shapes=small,
    )(block_tiles, assign, moved)
    piece = lax.all_to_all(packed, "grp", 0, 0, tiled=True).reshape(rows, wide)

    sends = jax.ShapeDtypeStruct((wide, cols), jnp.bfloat16)
    to_right, to_left = pl.pallas_call(
        functools.partial(send_tiles, groups, own),
        out_shape=(sends, sends),
        in_specs=[SMEM, SMEM, VMEM, VMEM],
        out_specs=(VMEM, VMEM),
        scratch_shapes=small,
        compiler_params=limit,
    )(block_tiles, assign, mine, other)

    across = [(y, (y + 2) % ny) for y in range(ny)]
    z_up, z_down = steps(nz)
    beside = [(g * ny + y, g * ny + (y - 1 + 2 * (g % 2)) % ny) for g in range(groups) for y in range(ny)]
    pair = jnp.stack([piece, lax.ppermute(piece, "row", across)])
    pair, to_right, to_left = lax.optimization_barrier((pair, to_right, to_left))
    from_left = lax.ppermute(to_right, "grp", up)
    from_right = lax.ppermute(to_left, "grp", down)
    a = b = pair
    parts, swapped = [pair], [lax.ppermute(pair, ("grp", "row"), beside)]
    for s in range(1, nz // 2):
        a, b = lax.ppermute(a, "col", z_up), lax.ppermute(b, "col", z_down)
        parts += [a, b]
        swapped.append(lax.ppermute(jnp.concatenate([a, b]), ("grp", "row"), beside))
    ta, tb = lax.ppermute(a[0], "col", z_up), lax.ppermute(b[1], "col", z_down)
    swapped.append(lax.ppermute(jnp.stack([ta, tb]), ("grp", "row"), beside))
    held = pl.pallas_call(
        functools.partial(join_tiles, groups, own),
        out_shape=sends,
        in_specs=[SMEM, SMEM, VMEM, VMEM, VMEM, VMEM],
        out_specs=VMEM,
        scratch_shapes=small,
        compiler_params=limit,
    )(block_tiles, assign, mine, other, from_left, from_right)
    pieces = parts + [ta, tb] + swapped

    half_rows = rows * nz // 2
    kept = jax.ShapeDtypeStruct((ny, half_rows, cols), jnp.float32)
    keep, send = pl.pallas_call(
        functools.partial(multiply, ny, nz, rows),
        out_shape=(kept, kept),
        in_specs=[VMEM] * (len(pieces) + 1),
        out_specs=(VMEM, VMEM),
        compiler_params=pltpu.CompilerParams(vmem_limit_bytes=32 * 2**20),
    )(*pieces, held)

    p = keep + lax.ppermute(send, "grp", swap)
    h = half_rows // 2
    a = lax.ppermute(jnp.concatenate([p[2, :h], p[1, h:]]), "grp", up)
    b = lax.ppermute(jnp.concatenate([p[2, h:], p[3, :h]]), "grp", down)
    a2 = lax.ppermute(p[1, :h] + a[:h], "grp", up)
    b2 = lax.ppermute(p[3, h:] + b[:h], "grp", down)
    return p[0] + jnp.concatenate([a2, a[h:]]) + jnp.concatenate([b[h:], b2])


def solution(mesh):
    in_specs = (P("grp", ("row", "col"), None), P("grp", None, ("row", "col")), P(), P())
    out_specs = P("grp", ("row", "col"))
    return jax.shard_map(body, mesh=mesh, in_specs=in_specs, out_specs=out_specs, check_vma=False)
```

```python
import functools

import jax
import jax.numpy as jnp
from jax import lax
from jax.experimental import pallas as pl
from jax.experimental.pallas import tpu as pltpu
from jax.sharding import PartitionSpec as P

TP = 128
ANY = pl.BlockSpec(memory_space=pl.ANY)
SMEM = pl.BlockSpec(memory_space=pltpu.SMEM)
VMEM = pl.BlockSpec(memory_space=pltpu.VMEM)


def balance(tiles_ref, assign_ref, held_ref, block_ref, groups):
    for b in range(groups):
        held_ref[assign_ref[b]] = tiles_ref[b]
        block_ref[assign_ref[b]] = b
    chips = groups // 2
    held = [held_ref[s] for s in range(groups)]
    total = [held[2 * x] + held[2 * x + 1] for x in range(chips)]
    share = 0
    for x in range(chips):
        share = share + total[x]
    share = share // chips
    running, prefix = 0, []
    for x in range(chips):
        running = running + total[x] - share
        prefix.append(running)
    high = functools.reduce(jnp.maximum, prefix)
    low = functools.reduce(jnp.minimum, prefix)
    middle = lax.shift_right_arithmetic(high + low, jnp.int32(1))
    flow = [p - middle for p in prefix]
    right = [jnp.maximum(flow[x], 0) for x in range(chips)]
    left = [jnp.maximum(-flow[(x - 1) % chips], 0) for x in range(chips)]
    return held, total, right, left


def half(n, core):
    first = lax.shift_right_arithmetic(n + 1, jnp.int32(1))
    if isinstance(core, int):
        return (0, first) if core == 0 else (first, n - first)
    return jnp.where(core == 0, 0, first), jnp.where(core == 0, first, n - first)


def pick(values, index):
    out = values[0]
    for i in range(1, len(values)):
        out = jnp.where(index == i, values[i], out)
    return out


def plan(x, core, total, right, left, own):
    chips = len(total)
    if isinstance(x, int):
        xl, xr = (x - 1) % chips, (x + 1) % chips
        from_left, from_right = right[xl], left[xr]
        left_first, kept_first = total[xl] - right[xl], left[x]
    else:
        xl, xr = lax.rem(x + chips - 1, chips), lax.rem(x + 1, chips)
        from_left, from_right = pick(right, xl), pick(left, xr)
        left_first, kept_first = pick(total, xl) - from_left, pick(left, x)
    l0, nl = half(from_left, core)
    r0, nr = half(from_right, core)
    first = own - half(from_left, 0)[1] - half(from_right, 0)[1]
    k0 = core * first if isinstance(core, int) else jnp.where(core == 0, 0, first)
    return (xl, left_first + l0, nl), (xr, r0, nr), (x, kept_first + k0, own - nl - nr)


def pack_amplitudes(groups, own, tiles_ref, assign_ref, src_ref, out_ref, held_ref, block_ref):
    held, total, right, left = balance(tiles_ref, assign_ref, held_ref, block_ref, groups)
    blocks = [block_ref[s] for s in range(groups)]
    for g in range(groups):
        x, c = g // 2, g % 2
        place = 0
        for chip, start, count in plan(x, c, total, right, left, own):
            n0 = jnp.clip(held[2 * chip] - start, 0, count)
            second = jnp.maximum(start - held[2 * chip], 0)
            for block, tile, many in ((blocks[2 * chip], start, n0), (blocks[2 * chip + 1], second, count - n0)):

                def move(i, carry, block=block, tile=tile, place=place):
                    data = src_ref[block, :, pl.ds(pl.multiple_of((tile + i) * TP, TP), TP)]
                    for to in range(2):
                        into = pl.ds(pl.multiple_of((place + i + (own if to != c else 0)) * TP, TP), TP)
                        for j in range(2):
                            out_ref[4 * x + 2 * to + j, :, into] = data
                    return carry

                lax.fori_loop(0, many, move, 0)
                place = place + many


def tile_rows(index):
    return pl.ds(pl.multiple_of(index * TP, TP), TP)


def send_tiles(groups, own, tiles_ref, assign_ref, mine_ref, other_ref, right_ref, left_ref, held_ref, block_ref, sems):
    held, total, right, left = balance(tiles_ref, assign_ref, held_ref, block_ref, groups)
    group = lax.axis_index("grp")
    x, core = lax.div(group, 2), lax.rem(group, 2)
    border = pick(held[0::2], x)
    go_right, go_left = pick(right, x), pick(left, x)
    r0, nr = half(go_right, core)
    l0, nl = half(go_left, core)
    jobs = []
    for way, (ref, start, count) in enumerate(((right_ref, pick(total, x) - go_right + r0, nr), (left_ref, l0, nl))):
        for i in range(own):
            tile = start + i
            upper = (tile >= border).astype(jnp.int32)
            row = tile - upper * border
            for source, here in ((mine_ref, upper == core), (other_ref, upper != core)):
                jobs.append((jnp.logical_and(i < count, here), source, row, ref, i, way * own + i))
    run_copies(jobs, sems)


def run_copies(jobs, sems):
    for go, source, row, ref, i, sem in jobs:

        @pl.when(go)
        def _():
            pltpu.make_async_copy(source.at[tile_rows(row)], ref.at[pl.ds(i * TP, TP)], sems.at[sem]).start()

    for go, source, row, ref, i, sem in jobs:

        @pl.when(go)
        def _():
            pltpu.make_async_copy(source.at[tile_rows(row)], ref.at[pl.ds(i * TP, TP)], sems.at[sem]).wait()


def join_tiles(groups, own, tiles_ref, assign_ref, mine_ref, other_ref, fl_ref, fr_ref, out_ref, held_ref, block_ref, sems):
    held, total, right, left = balance(tiles_ref, assign_ref, held_ref, block_ref, groups)
    group = lax.axis_index("grp")
    x, core = lax.div(group, 2), lax.rem(group, 2)
    border = pick(held[0::2], x)
    (_, _, nl), (_, _, nr), (_, start, _) = plan(x, core, total, right, left, own)
    jobs = []
    for i in range(own):
        jobs.append((i < nl, fl_ref, i, out_ref, i, i))
        jobs.append((jnp.logical_and(i >= nl, i < nl + nr), fr_ref, jnp.maximum(i - nl, 0), out_ref, i, i))
        tile = jnp.maximum(start + i - nl - nr, 0)
        upper = (tile >= border).astype(jnp.int32)
        row = tile - upper * border
        kept = i >= nl + nr
        jobs.append((jnp.logical_and(kept, upper == core), mine_ref, row, out_ref, i, i))
        jobs.append((jnp.logical_and(kept, upper != core), other_ref, row, out_ref, i, i))
    run_copies(jobs, sems)


def multiply(ny, nz, first, *refs):
    count = (len(refs) - 4) // 2
    refs, (b0_ref, b1_ref, out_ref, a_ref) = refs[:-4], refs[-4:]
    x, y = lax.div(lax.axis_index("grp"), 2), lax.axis_index("row")
    parity = lax.rem(y, 2)
    at = 0
    for ref in refs:
        n, octet, wide = ref.shape
        a_ref[at : at + n * octet, :] = ref[...].reshape(n * octet, wide)
        at += n * octet
    mid = b0_ref.shape[0]
    out = jnp.dot(a_ref[:, :mid], b0_ref[...], preferred_element_type=jnp.float32)
    out += jnp.dot(a_ref[:, mid:], b1_ref[...], preferred_element_type=jnp.float32)
    at = 0
    for side in range(2):
        row = 0
        for ref in refs[side * count : (side + 1) * count]:
            n, octet, _ = ref.shape
            for j in range(2):
                d = lax.rem(lax.rem(parity + side, 2) + 2 * j - x + ny, ny)
                for g in range(n // 2):
                    start = at + (2 * g + j) * octet
                    out_ref[d, row + g * octet : row + (g + 1) * octet, :] = out[start : start + octet]
            at += n * octet
            row += n // 2 * octet


def finish(nz, rows, mine_ref, other_ref, out_ref):
    core, z = lax.rem(lax.axis_index("grp"), 2), lax.axis_index("col")
    h = rows // 2
    last = nz // 2 * rows - h
    for q in range(nz // 2):
        r = lax.rem(core * (nz // 2) + q - z + nz, nz)
        ends = jnp.logical_or(r == 0, r == nz // 2)
        above = r < nz // 2
        step = jnp.where(above, r, nz - r)
        for part in range(2):
            start = jnp.where(r == 0, 0, jnp.where(r == nz // 2, last, h + rows * (step - 1) + part * h))
            holder = jnp.where(ends, part, jnp.where(above, 1, 0))
            rows_in = pl.ds(pl.multiple_of(start, h), h)
            for ref, here in ((mine_ref, holder == core), (other_ref, holder != core)):

                @pl.when(here)
                def _(ref=ref, q=q, part=part, rows_in=rows_in):
                    out_ref[q * rows + part * h : q * rows + (part + 1) * h, :] = ref[rows_in, :]


def reduce_x(p, up, down):
    h = p.shape[1] // 2
    a = lax.ppermute(jnp.concatenate([p[2, :h], p[1, h:]]), "grp", up)
    b = lax.ppermute(jnp.concatenate([p[2, h:], p[3, :h]]), "grp", down)
    a2 = lax.ppermute(p[1, :h] + a[:h], "grp", up)
    b2 = lax.ppermute(p[3, h:] + b[:h], "grp", down)
    return p[0] + jnp.concatenate([a2, a[h:]]) + jnp.concatenate([b[h:], b2])


def body(amplitudes, integrals, block_tiles, assign):
    groups = assign.shape[0]
    _, rows, cap = amplitudes.shape
    cols = integrals.shape[2]
    ny, nz = lax.axis_size("row"), lax.axis_size("col")
    own = 12
    wide = own * TP
    octet = rows // groups
    small = [pltpu.SMEM((groups,), jnp.int32)] * 2
    swap = [(g, g ^ 1) for g in range(groups)]
    up = [(g, (g + 2) % groups) for g in range(groups)]
    down = [(g, (g - 2) % groups) for g in range(groups)]
    along = [(g * nz + z, g * nz + (z + 1 - 2 * (g % 2)) % nz) for g in range(groups) for z in range(nz)]
    beside = [(g * ny + y, g * ny + (y - 1 + 2 * (g % 2)) % ny) for g in range(groups) for y in range(ny)]
    pairs = [[g * ny + y for g in range(groups) for y in (p, p + 2)] for p in range(2)]
    barrier = lax.optimization_barrier
    limit = pltpu.CompilerParams(vmem_limit_bytes=32 * 2**20)
    core = lax.rem(lax.axis_index("grp"), 2)

    mine = integrals[0]
    other = lax.ppermute(mine, "grp", swap)
    moved = lax.all_to_all(amplitudes[0].reshape(groups, octet, cap), "grp", 0, 0, tiled=True)
    packed = pl.pallas_call(
        functools.partial(pack_amplitudes, groups, own),
        out_shape=jax.ShapeDtypeStruct((2 * groups, octet, 2 * wide), jnp.bfloat16),
        in_specs=[SMEM, SMEM, VMEM],
        out_specs=VMEM,
        scratch_shapes=small,
    )(block_tiles, assign, moved)
    pair = lax.all_to_all(packed, ("grp", "row"), 0, 0, axis_index_groups=pairs, tiled=True)

    sends = jax.ShapeDtypeStruct((wide, cols), jnp.bfloat16)
    to_right, to_left = pl.pallas_call(
        functools.partial(send_tiles, groups, own),
        out_shape=(sends, sends),
        in_specs=[SMEM, SMEM, ANY, ANY],
        out_specs=(VMEM, VMEM),
        scratch_shapes=small + [pltpu.SemaphoreType.DMA((2 * own,))],
        compiler_params=limit,
    )(block_tiles, assign, mine, other)
    pair, to_right, to_left = barrier((pair, to_right, to_left))
    from_left = lax.ppermute(to_right, "grp", up)
    from_right = lax.ppermute(to_left, "grp", down)

    def half_of(block):
        return jnp.where(core == 0, block[:groups], block[groups:])

    def z_step(block):
        return lax.ppermute(block, ("grp", "col"), along)

    def y_step(block):
        return lax.ppermute(block, ("grp", "row"), beside)

    w0 = half_of(pair)
    w1, v0 = barrier((z_step(pair), y_step(w0)))
    w2, v1 = barrier((z_step(w1), y_step(w1)))
    w3, v2 = barrier((z_step(w2), y_step(w2)))
    w4, v3 = z_step(half_of(w3)), y_step(w3)
    v4 = y_step(w4)

    held = pl.pallas_call(
        functools.partial(join_tiles, groups, own),
        out_shape=sends,
        in_specs=[SMEM, SMEM, ANY, ANY, ANY, ANY],
        out_specs=VMEM,
        scratch_shapes=small + [pltpu.SemaphoreType.DMA((own,))],
        compiler_params=limit,
    )(block_tiles, assign, mine, other, from_left, from_right)
    theirs = lax.ppermute(held, "grp", swap)

    def sums(*parts):
        n = sum(part.shape[0] for part in parts) * octet
        return pl.pallas_call(
            functools.partial(multiply, ny, nz, 0),
            out_shape=jax.ShapeDtypeStruct((ny, n // 4, cols), jnp.float32),
            in_specs=[VMEM] * (len(parts) + 2),
            out_specs=VMEM,
            scratch_shapes=[pltpu.VMEM((n, 2 * wide), jnp.bfloat16)],
            compiler_params=limit,
        )(*parts, held, theirs)

    early = reduce_x(sums(w0, w1, w2, v0, v1, v2), up, down)
    late = reduce_x(sums(w3, w4, v3, v4), up, down)
    done = jnp.concatenate([early, late])
    return pl.pallas_call(
        functools.partial(finish, nz, rows),
        out_shape=jax.ShapeDtypeStruct((nz // 2 * rows, cols), jnp.float32),
        in_specs=[VMEM, VMEM],
        out_specs=VMEM,
    )(done, lax.ppermute(done, "grp", swap))


def solution(mesh):
    in_specs = (P("grp", ("row", "col"), None), P("grp", None, ("row", "col")), P(), P())
    out_specs = P("grp", ("row", "col"))
    return jax.shard_map(body, mesh=mesh, in_specs=in_specs, out_specs=out_specs, check_vma=False)
```

```python
import functools

import jax
import jax.numpy as jnp
from jax import lax
from jax.experimental import pallas as pl
from jax.experimental.pallas import tpu as pltpu
from jax.sharding import PartitionSpec as P

TP = 128
ANY = pl.BlockSpec(memory_space=pl.ANY)
SMEM = pl.BlockSpec(memory_space=pltpu.SMEM)
VMEM = pl.BlockSpec(memory_space=pltpu.VMEM)


def balance(tiles_ref, assign_ref, held_ref, block_ref, groups):
    for b in range(groups):
        held_ref[assign_ref[b]] = tiles_ref[b]
        block_ref[assign_ref[b]] = b
    chips = groups // 2
    held = [held_ref[s] for s in range(groups)]
    total = [held[2 * x] + held[2 * x + 1] for x in range(chips)]
    share = 0
    for x in range(chips):
        share = share + total[x]
    share = share // chips
    running, prefix = 0, []
    for x in range(chips):
        running = running + total[x] - share
        prefix.append(running)
    high = functools.reduce(jnp.maximum, prefix)
    low = functools.reduce(jnp.minimum, prefix)
    middle = lax.shift_right_arithmetic(high + low, jnp.int32(1))
    flow = [p - middle for p in prefix]
    right = [jnp.maximum(flow[x], 0) for x in range(chips)]
    left = [jnp.maximum(-flow[(x - 1) % chips], 0) for x in range(chips)]
    return held, total, right, left


def pick(values, index):
    out = values[0]
    for i in range(1, len(values)):
        out = jnp.where(index == i, values[i], out)
    return out


def runs_of(x, total, right, left, chips):
    if isinstance(x, int):
        xl, xr = (x - 1) % chips, (x + 1) % chips
        n, m, t, k = right[xl], left[xr], total[xl], left[x]
    else:
        xl, xr = lax.rem(x + chips - 1, chips), lax.rem(x + 1, chips)
        n, m, t, k = pick(right, xl), pick(left, xr), pick(total, xl), pick(left, x)
    return (xl, t - n, n), (xr, 0, m), (x, k, None)


def pack_amplitudes(groups, share, tiles_ref, assign_ref, src_ref, out_ref, held_ref, block_ref):
    held, total, right, left = balance(tiles_ref, assign_ref, held_ref, block_ref, groups)
    blocks = [block_ref[s] for s in range(groups)]
    for x in range(groups // 2):
        place = 0
        for chip, start, count in runs_of(x, total, right, left, groups // 2):
            if count is None:
                count = share - place
            n0 = jnp.clip(held[2 * chip] - start, 0, count)
            second = jnp.maximum(start - held[2 * chip], 0)
            for block, tile, many in ((blocks[2 * chip], start, n0), (blocks[2 * chip + 1], second, count - n0)):

                def move(i, carry, block=block, tile=tile, place=place):
                    data = src_ref[block, :, pl.ds(pl.multiple_of((tile + i) * TP, TP), TP)]
                    into = pl.ds(pl.multiple_of((place + i) * TP, TP), TP)
                    out_ref[2 * x, :, into] = data
                    out_ref[2 * x + 1, :, into] = data
                    return carry

                lax.fori_loop(0, many, move, 0)
                place = place + many


def tile_rows(index):
    return pl.ds(pl.multiple_of(index * TP, TP), TP)


def run_copies(jobs, out_ref, sems):
    for phase in range(2):
        for source, tile, many, place in jobs:

            def move(i, carry, source=source, tile=tile, place=place):
                copy = pltpu.make_async_copy(source.at[tile_rows(tile + i)], out_ref.at[tile_rows(place + i)], sems.at[place + i])
                copy.start() if phase == 0 else copy.wait()
                return carry

            lax.fori_loop(0, many, move, 0)


def own_tiles(border, core, start, count, mine_ref, other_ref, place):
    lower = jnp.clip(border - start, 0, count)
    jobs = []
    for upper, tile, many, at in ((0, start, lower, place), (1, jnp.maximum(start - border, 0), count - lower, place + lower)):
        jobs.append((mine_ref, tile, jnp.where(core == upper, many, 0), at))
        jobs.append((other_ref, tile, jnp.where(core != upper, many, 0), at))
    return jobs


def send_tiles(groups, share, tiles_ref, assign_ref, mine_ref, other_ref, out_ref, held_ref, block_ref, sems):
    held, total, right, left = balance(tiles_ref, assign_ref, held_ref, block_ref, groups)
    group = lax.axis_index("grp")
    x, core = lax.div(group, 2), lax.rem(group, 2)
    go_right, go_left = pick(right, x), pick(left, x)
    start = jnp.where(core == 0, pick(total, x) - go_right, 0)
    count = jnp.where(core == 0, go_right, go_left)
    run_copies(own_tiles(pick(held[0::2], x), core, start, count, mine_ref, other_ref, 0), out_ref, sems)


def join_tiles(groups, share, tiles_ref, assign_ref, mine_ref, other_ref, got_ref, *refs):
    *their_refs, out_ref, held_ref, block_ref, sems = refs
    held, total, right, left = balance(tiles_ref, assign_ref, held_ref, block_ref, groups)
    group = lax.axis_index("grp")
    x, core = lax.div(group, 2), lax.rem(group, 2)
    (_, _, n), (_, _, m), (_, start, _) = runs_of(x, total, right, left, groups // 2)
    jobs = [
        (got_ref, 0, jnp.where(core == 0, n, 0), 0),
        (got_ref, 0, jnp.where(core == 0, 0, m), n),
    ]
    each = share // len(their_refs)
    for i, ref in enumerate(their_refs):
        jobs.append((ref, 0, jnp.clip(jnp.where(core == 0, m, n) - i * each, 0, each), jnp.where(core == 0, n, 0) + i * each))
    jobs += own_tiles(pick(held[0::2], x), core, start, share - n - m, mine_ref, other_ref, n + m)
    run_copies(jobs, out_ref, sems)


def multiply(ny, *refs):
    refs, (b_ref, out_ref, a_ref) = refs[:-3], refs[-3:]
    group, y = lax.axis_index("grp"), lax.axis_index("row")
    x, core = lax.div(group, 2), lax.rem(group, 2)
    near = jnp.where(core == 0, 1, ny - 1)
    at = 0
    for ref in refs:
        n, octet, wide = ref.shape
        a_ref[at : at + n * octet, :] = ref[...].reshape(n * octet, wide)
        at += n * octet
    out = jnp.dot(a_ref[...], b_ref[...], preferred_element_type=jnp.float32)
    at = row = 0
    for i, ref in enumerate(refs):
        n = ref.shape[0] * ref.shape[1]
        d = lax.rem(y + (0, 2, near, near + 2)[i % 4] - x + 2 * ny, ny)
        out_ref[d, row : row + n, :] = out[at : at + n]
        at += n
        row += n if i % 4 == 3 else 0


def finish(nz, rows, mine_ref, other_ref, out_ref):
    core, z = lax.rem(lax.axis_index("grp"), 2), lax.axis_index("col")
    h = rows // 2
    last = nz // 2 * rows - h
    for q in range(nz // 2):
        r = lax.rem(core * (nz // 2) + q - z + nz, nz)
        ends = jnp.logical_or(r == 0, r == nz // 2)
        above = r < nz // 2
        step = jnp.where(above, r, nz - r)
        for part in range(2):
            start = jnp.where(r == 0, 0, jnp.where(r == nz // 2, last, h + rows * (step - 1) + part * h))
            holder = jnp.where(ends, part, jnp.where(above, 1, 0))
            rows_in = pl.ds(pl.multiple_of(start, h), h)
            for ref, here in ((mine_ref, holder == core), (other_ref, holder != core)):

                @pl.when(here)
                def _(ref=ref, q=q, part=part, rows_in=rows_in):
                    out_ref[q * rows + part * h : q * rows + (part + 1) * h, :] = ref[rows_in, :]


def near_chips(p, up, down):
    h = p.shape[1] // 2
    a = lax.ppermute(jnp.concatenate([p[2, :h], p[1, h:]]), "grp", up)
    return a, lax.ppermute(jnp.concatenate([p[2, h:], p[3, :h]]), "grp", down)


def passed_on(p, a, b, up, down):
    h = p.shape[1] // 2
    return lax.ppermute(p[1, :h] + a[:h], "grp", up), lax.ppermute(p[3, h:] + b[:h], "grp", down)


def total_of(p, a, b, a2, b2):
    h = p.shape[1] // 2
    return p[0] + jnp.concatenate([a2, a[h:]]) + jnp.concatenate([b[h:], b2])


def body(amplitudes, integrals, block_tiles, assign):
    groups = assign.shape[0]
    _, rows, cap = amplitudes.shape
    cols = integrals.shape[2]
    ny, nz = lax.axis_size("row"), lax.axis_size("col")
    share = 24
    wide = share * TP
    octet = rows // groups
    small = [pltpu.SMEM((groups,), jnp.int32)] * 2
    swap = [(g, g ^ 1) for g in range(groups)]
    up = [(g, (g + 2) % groups) for g in range(groups)]
    down = [(g, (g - 2) % groups) for g in range(groups)]
    apart = [(g, (g + 2 - 4 * (g % 2)) % groups) for g in range(groups)]
    along = [(g * nz + z, g * nz + (z + 1 - 2 * (g % 2)) % nz) for g in range(groups) for z in range(nz)]
    beside = [(g * ny + y, g * ny + (y - 1 + 2 * (g % 2)) % ny) for g in range(groups) for y in range(ny)]
    across = [(y, (y + 2) % ny) for y in range(ny)]
    limit = pltpu.CompilerParams(vmem_limit_bytes=32 * 2**20)
    core = lax.rem(lax.axis_index("grp"), 2)
    barrier = lax.optimization_barrier

    mine = integrals[0]
    other = lax.ppermute(mine, "grp", swap)
    moved = lax.all_to_all(amplitudes[0].reshape(groups, octet, cap), "grp", 0, 0, tiled=True)
    moved, other = barrier((moved, other))
    packed = pl.pallas_call(
        functools.partial(pack_amplitudes, groups, share),
        out_shape=jax.ShapeDtypeStruct((groups, octet, wide), jnp.bfloat16),
        in_specs=[SMEM, SMEM, VMEM],
        out_specs=VMEM,
        scratch_shapes=small,
    )(block_tiles, assign, moved)
    piece = lax.all_to_all(packed, "grp", 0, 0, tiled=True)

    tiles = jax.ShapeDtypeStruct((wide, cols), jnp.bfloat16)
    scratch = small + [pltpu.SemaphoreType.DMA((share,))]
    sent = pl.pallas_call(
        functools.partial(send_tiles, groups, share),
        out_shape=tiles,
        in_specs=[SMEM, SMEM, ANY, ANY],
        out_specs=VMEM,
        scratch_shapes=scratch,
        compiler_params=limit,
    )(block_tiles, assign, mine, other)
    got = lax.ppermute(sent, "grp", apart)
    def half_of(block):
        h = block.shape[0] // 2
        return jnp.where(core == 0, block[:h], block[h:])

    def z_step(block):
        return lax.ppermute(block, ("grp", "col"), along)

    def y_step(block):
        return lax.ppermute(block, ("grp", "row"), beside)

    chains = [piece, lax.ppermute(piece, "row", across)]
    order = []
    for s in range(nz // 2 - 1):
        here, beside_here = [], []
        for i, block in enumerate(chains):
            kept = half_of(block) if s == 0 else block
            chains[i], other_y = barrier((z_step(block), y_step(kept)))
            here.append(kept)
            beside_here.append(other_y)
        order.append(here + beside_here)
    ends = [z_step(half_of(block)) for block in chains]
    order.append(chains + [y_step(block) for block in chains])

    theirs = [lax.ppermute(part, "grp", swap) for part in jnp.split(got, 2)]
    held = pl.pallas_call(
        functools.partial(join_tiles, groups, share),
        out_shape=tiles,
        in_specs=[SMEM, SMEM] + [ANY] * (3 + len(theirs)),
        out_specs=VMEM,
        scratch_shapes=scratch,
        compiler_params=limit,
    )(block_tiles, assign, mine, other, got, *theirs)

    def sums(steps):
        parts = [part for step in steps for part in step]
        n = sum(part.shape[0] for part in parts) * octet
        return pl.pallas_call(
            functools.partial(multiply, ny),
            out_shape=jax.ShapeDtypeStruct((ny, n // 4, cols), jnp.float32),
            in_specs=[VMEM] * (len(parts) + 1),
            out_specs=VMEM,
            scratch_shapes=[pltpu.VMEM((n, wide), jnp.bfloat16)],
            compiler_params=limit,
        )(*parts, held)

    p = sums(order[:3])
    a, b = near_chips(p, up, down)
    *ends, a, b = barrier((*ends, a, b))
    *beside_ends, a2, b2 = barrier((*map(y_step, ends), *passed_on(p, a, b, up, down)))
    early = total_of(p, a, b, a2, b2)
    p = sums(order[3:] + [ends + beside_ends])
    a, b = near_chips(p, up, down)
    late = total_of(p, a, b, *passed_on(p, a, b, up, down))
    done = jnp.concatenate([early, late])
    return pl.pallas_call(
        functools.partial(finish, nz, rows),
        out_shape=jax.ShapeDtypeStruct((nz // 2 * rows, cols), jnp.float32),
        in_specs=[VMEM, VMEM],
        out_specs=VMEM,
    )(done, lax.ppermute(done, "grp", swap))


def solution(mesh):
    in_specs = (P("grp", ("row", "col"), None), P("grp", None, ("row", "col")), P(), P())
    out_specs = P("grp", ("row", "col"))
    return jax.shard_map(body, mesh=mesh, in_specs=in_specs, out_specs=out_specs, check_vma=False)
```

```python
import functools

import jax
import jax.numpy as jnp
from jax import lax
from jax.experimental import pallas as pl
from jax.experimental.pallas import tpu as pltpu
from jax.sharding import PartitionSpec as P

TP = 128
ANY = pl.BlockSpec(memory_space=pl.ANY)
SMEM = pl.BlockSpec(memory_space=pltpu.SMEM)
VMEM = pl.BlockSpec(memory_space=pltpu.VMEM)


def balance(tiles_ref, assign_ref, held_ref, block_ref, groups):
    for b in range(groups):
        held_ref[assign_ref[b]] = tiles_ref[b]
        block_ref[assign_ref[b]] = b
    chips = groups // 2
    held = [held_ref[s] for s in range(groups)]
    total = [held[2 * x] + held[2 * x + 1] for x in range(chips)]
    share = 0
    for x in range(chips):
        share = share + total[x]
    share = share // chips
    running, prefix = 0, []
    for x in range(chips):
        running = running + total[x] - share
        prefix.append(running)
    high = functools.reduce(jnp.maximum, prefix)
    low = functools.reduce(jnp.minimum, prefix)
    middle = lax.shift_right_arithmetic(high + low, jnp.int32(1))
    flow = [p - middle for p in prefix]
    right = [jnp.maximum(flow[x], 0) for x in range(chips)]
    left = [jnp.maximum(-flow[(x - 1) % chips], 0) for x in range(chips)]
    return held, total, right, left


def pick(values, index):
    out = values[0]
    for i in range(1, len(values)):
        out = jnp.where(index == i, values[i], out)
    return out


def runs_of(x, total, right, left, chips):
    if isinstance(x, int):
        xl, xr = (x - 1) % chips, (x + 1) % chips
        n, m, t, k = right[xl], left[xr], total[xl], left[x]
    else:
        xl, xr = lax.rem(x + chips - 1, chips), lax.rem(x + 1, chips)
        n, m, t, k = pick(right, xl), pick(left, xr), pick(total, xl), pick(left, x)
    return (xl, t - n, n), (xr, 0, m), (x, k, None)


def pack_amplitudes(groups, share, tiles_ref, assign_ref, src_ref, out_ref, held_ref, block_ref):
    held, total, right, left = balance(tiles_ref, assign_ref, held_ref, block_ref, groups)
    blocks = [block_ref[s] for s in range(groups)]
    for x in range(groups // 2):
        place = 0
        for chip, start, count in runs_of(x, total, right, left, groups // 2):
            if count is None:
                count = share - place
            n0 = jnp.clip(held[2 * chip] - start, 0, count)
            second = jnp.maximum(start - held[2 * chip], 0)
            for block, tile, many in ((blocks[2 * chip], start, n0), (blocks[2 * chip + 1], second, count - n0)):

                def move(i, carry, block=block, tile=tile, place=place):
                    data = src_ref[block, :, pl.ds(pl.multiple_of((tile + i) * TP, TP), TP)]
                    into = pl.ds(pl.multiple_of((place + i) * TP, TP), TP)
                    for copy in range(4):
                        out_ref[4 * x + copy, :, into] = data
                    return carry

                lax.fori_loop(0, many, move, 0)
                place = place + many


def tile_rows(index):
    return pl.ds(pl.multiple_of(index * TP, TP), TP)


def run_copies(jobs, out_ref, sems):
    for phase in range(2):
        for source, tile, many, place in jobs:

            def move(i, carry, source=source, tile=tile, place=place):
                copy = pltpu.make_async_copy(source.at[tile_rows(tile + i)], out_ref.at[tile_rows(place + i)], sems.at[place + i])
                copy.start() if phase == 0 else copy.wait()
                return carry

            lax.fori_loop(0, many, move, 0)


def own_tiles(border, core, start, count, mine_ref, other_ref, place):
    lower = jnp.clip(border - start, 0, count)
    jobs = []
    for upper, tile, many, at in ((0, start, lower, place), (1, jnp.maximum(start - border, 0), count - lower, place + lower)):
        jobs.append((mine_ref, tile, jnp.where(core == upper, many, 0), at))
        jobs.append((other_ref, tile, jnp.where(core != upper, many, 0), at))
    return jobs


def send_tiles(groups, share, tiles_ref, assign_ref, mine_ref, other_ref, out_ref, held_ref, block_ref, sems):
    held, total, right, left = balance(tiles_ref, assign_ref, held_ref, block_ref, groups)
    group = lax.axis_index("grp")
    x, core = lax.div(group, 2), lax.rem(group, 2)
    go_right, go_left = pick(right, x), pick(left, x)
    start = jnp.where(core == 0, pick(total, x) - go_right, 0)
    count = jnp.where(core == 0, go_right, go_left)
    run_copies(own_tiles(pick(held[0::2], x), core, start, count, mine_ref, other_ref, 0), out_ref, sems)


def join_tiles(groups, share, tiles_ref, assign_ref, mine_ref, other_ref, got_ref, *refs):
    *their_refs, out_ref, held_ref, block_ref, sems = refs
    held, total, right, left = balance(tiles_ref, assign_ref, held_ref, block_ref, groups)
    group = lax.axis_index("grp")
    x, core = lax.div(group, 2), lax.rem(group, 2)
    (_, _, n), (_, _, m), (_, start, _) = runs_of(x, total, right, left, groups // 2)
    jobs = [
        (got_ref, 0, jnp.where(core == 0, n, 0), 0),
        (got_ref, 0, jnp.where(core == 0, 0, m), n),
    ]
    each = share // len(their_refs)
    for i, ref in enumerate(their_refs):
        jobs.append((ref, 0, jnp.clip(jnp.where(core == 0, m, n) - i * each, 0, each), jnp.where(core == 0, n, 0) + i * each))
    jobs += own_tiles(pick(held[0::2], x), core, start, share - n - m, mine_ref, other_ref, n + m)
    run_copies(jobs, out_ref, sems)


def multiply(ny, *refs):
    refs, (b_ref, out_ref, a_ref) = refs[:-3], refs[-3:]
    x, y = lax.div(lax.axis_index("grp"), 2), lax.axis_index("row")
    at = 0
    for ref in refs:
        n, octet, wide = ref.shape
        a_ref[at : at + n * octet, :] = ref[...].reshape(n * octet, wide)
        at += n * octet
    out = jnp.dot(a_ref[...], b_ref[...], preferred_element_type=jnp.float32)
    at = row = 0
    for i, ref in enumerate(refs):
        n, octet, _ = ref.shape
        for j in range(2):
            d = lax.rem(lax.rem(y + i % 2, 2) + 2 * j - x + ny, ny)
            for g in range(n // 2):
                start = at + (2 * g + j) * octet
                out_ref[d, row + g * octet : row + (g + 1) * octet, :] = out[start : start + octet]
        at += n * octet
        row += n // 2 * octet if i % 2 else 0


def finish(nz, rows, mine_ref, other_ref, out_ref):
    core, z = lax.rem(lax.axis_index("grp"), 2), lax.axis_index("col")
    h = rows // 2
    last = nz // 2 * rows - h
    for q in range(nz // 2):
        r = lax.rem(core * (nz // 2) + q - z + nz, nz)
        ends = jnp.logical_or(r == 0, r == nz // 2)
        above = r < nz // 2
        step = jnp.where(above, r, nz - r)
        for part in range(2):
            start = jnp.where(r == 0, 0, jnp.where(r == nz // 2, last, h + rows * (step - 1) + part * h))
            holder = jnp.where(ends, part, jnp.where(above, 1, 0))
            rows_in = pl.ds(pl.multiple_of(start, h), h)
            for ref, here in ((mine_ref, holder == core), (other_ref, holder != core)):

                @pl.when(here)
                def _(ref=ref, q=q, part=part, rows_in=rows_in):
                    out_ref[q * rows + part * h : q * rows + (part + 1) * h, :] = ref[rows_in, :]


def near_chips(p, up, down):
    h = p.shape[1] // 2
    a = lax.ppermute(jnp.concatenate([p[2, :h], p[1, h:]]), "grp", up)
    return a, lax.ppermute(jnp.concatenate([p[2, h:], p[3, :h]]), "grp", down)


def passed_on(p, a, b, up, down):
    h = p.shape[1] // 2
    return lax.ppermute(p[1, :h] + a[:h], "grp", up), lax.ppermute(p[3, h:] + b[:h], "grp", down)


def total_of(p, a, b, a2, b2):
    h = p.shape[1] // 2
    return p[0] + jnp.concatenate([a2, a[h:]]) + jnp.concatenate([b[h:], b2])


def body(amplitudes, integrals, block_tiles, assign):
    groups = assign.shape[0]
    _, rows, cap = amplitudes.shape
    cols = integrals.shape[2]
    ny, nz = lax.axis_size("row"), lax.axis_size("col")
    share = 24
    wide = share * TP
    octet = rows // groups
    small = [pltpu.SMEM((groups,), jnp.int32)] * 2
    swap = [(g, g ^ 1) for g in range(groups)]
    up = [(g, (g + 2) % groups) for g in range(groups)]
    down = [(g, (g - 2) % groups) for g in range(groups)]
    apart = [(g, (g + 2 - 4 * (g % 2)) % groups) for g in range(groups)]
    along = [(g * nz + z, g * nz + (z + 1 - 2 * (g % 2)) % nz) for g in range(groups) for z in range(nz)]
    beside = [(g * ny + y, g * ny + (y - 1 + 2 * (g % 2)) % ny) for g in range(groups) for y in range(ny)]
    pairs = [[g * ny + y for g in range(groups) for y in (p, p + 2)] for p in range(2)]
    limit = pltpu.CompilerParams(vmem_limit_bytes=32 * 2**20)
    core = lax.rem(lax.axis_index("grp"), 2)
    barrier = lax.optimization_barrier

    mine = integrals[0]
    other = lax.ppermute(mine, "grp", swap)
    moved = lax.all_to_all(amplitudes[0].reshape(groups, octet, cap), "grp", 0, 0, tiled=True)
    packed = pl.pallas_call(
        functools.partial(pack_amplitudes, groups, share),
        out_shape=jax.ShapeDtypeStruct((2 * groups, octet, wide), jnp.bfloat16),
        in_specs=[SMEM, SMEM, VMEM],
        out_specs=VMEM,
        scratch_shapes=small,
    )(block_tiles, assign, moved)
    pair = lax.all_to_all(packed, ("grp", "row"), 0, 0, axis_index_groups=pairs, tiled=True)

    tiles = jax.ShapeDtypeStruct((wide, cols), jnp.bfloat16)
    scratch = small + [pltpu.SemaphoreType.DMA((share,))]
    sent = pl.pallas_call(
        functools.partial(send_tiles, groups, share),
        out_shape=tiles,
        in_specs=[SMEM, SMEM, ANY, ANY],
        out_specs=VMEM,
        scratch_shapes=scratch,
        compiler_params=limit,
    )(block_tiles, assign, mine, other)
    pair, sent = barrier((pair, sent))
    got = lax.ppermute(sent, "grp", apart)
    def half_of(block):
        h = block.shape[0] // 2
        return jnp.where(core == 0, block[:h], block[h:])

    def z_step(block):
        return lax.ppermute(block, ("grp", "col"), along)

    def y_step(block):
        return lax.ppermute(block, ("grp", "row"), beside)

    block, order = pair, []
    for s in range(nz // 2 - 1):
        kept = half_of(block) if s == 0 else block
        block, near = barrier((z_step(block), y_step(kept)))
        if s == nz // 2 - 3:
            block, near, got = barrier((block, near, got))
        order += [kept, near]
    theirs = [lax.ppermute(part, "grp", swap) for part in jnp.split(got, 2)]
    end = z_step(half_of(block))
    order += [block, y_step(block), end, y_step(end)]

    held = pl.pallas_call(
        functools.partial(join_tiles, groups, share),
        out_shape=tiles,
        in_specs=[SMEM, SMEM] + [ANY] * (3 + len(theirs)),
        out_specs=VMEM,
        scratch_shapes=scratch,
        compiler_params=limit,
    )(block_tiles, assign, mine, other, got, *theirs)

    def sums(parts):
        n = sum(part.shape[0] for part in parts) * octet
        return pl.pallas_call(
            functools.partial(multiply, ny),
            out_shape=jax.ShapeDtypeStruct((ny, n // 4, cols), jnp.float32),
            in_specs=[VMEM] * (len(parts) + 1),
            out_specs=VMEM,
            scratch_shapes=[pltpu.VMEM((n, wide), jnp.bfloat16)],
            compiler_params=limit,
        )(*parts, held)

    early, late = sums(order[:6]), order[6:]
    a, b = near_chips(early, up, down)
    *late, a, b = barrier((*late, a, b))
    late = sums(late)
    c, d = near_chips(late, up, down)
    early = total_of(early, a, b, *passed_on(early, a, b, up, down))
    late = total_of(late, c, d, *passed_on(late, c, d, up, down))
    done = jnp.concatenate([early, late])
    return pl.pallas_call(
        functools.partial(finish, nz, rows),
        out_shape=jax.ShapeDtypeStruct((nz // 2 * rows, cols), jnp.float32),
        in_specs=[VMEM, VMEM],
        out_specs=VMEM,
    )(done, lax.ppermute(done, "grp", swap))


def solution(mesh):
    in_specs = (P("grp", ("row", "col"), None), P("grp", None, ("row", "col")), P(), P())
    out_specs = P("grp", ("row", "col"))
    return jax.shard_map(body, mesh=mesh, in_specs=in_specs, out_specs=out_specs, check_vma=False)
```

```python
import functools

import jax
import jax.numpy as jnp
from jax import lax
from jax.experimental import pallas as pl
from jax.experimental.pallas import tpu as pltpu
from jax.sharding import PartitionSpec as P

TP = 128
ANY = pl.BlockSpec(memory_space=pl.ANY)
SMEM = pl.BlockSpec(memory_space=pltpu.SMEM)
VMEM = pl.BlockSpec(memory_space=pltpu.VMEM)


def balance(tiles_ref, assign_ref, held_ref, block_ref, groups):
    for b in range(groups):
        held_ref[assign_ref[b]] = tiles_ref[b]
        block_ref[assign_ref[b]] = b
    chips = groups // 2
    held = [held_ref[s] for s in range(groups)]
    total = [held[2 * x] + held[2 * x + 1] for x in range(chips)]
    share = 0
    for x in range(chips):
        share = share + total[x]
    share = share // chips
    running, prefix = 0, []
    for x in range(chips):
        running = running + total[x] - share
        prefix.append(running)
    high = functools.reduce(jnp.maximum, prefix)
    low = functools.reduce(jnp.minimum, prefix)
    middle = lax.shift_right_arithmetic(high + low, jnp.int32(1))
    flow = [p - middle for p in prefix]
    right = [jnp.maximum(flow[x], 0) for x in range(chips)]
    left = [jnp.maximum(-flow[(x - 1) % chips], 0) for x in range(chips)]
    return held, total, right, left


def pick(values, index):
    out = values[0]
    for i in range(1, len(values)):
        out = jnp.where(index == i, values[i], out)
    return out


def runs_of(x, total, right, left, chips):
    if isinstance(x, int):
        xl, xr = (x - 1) % chips, (x + 1) % chips
        n, m, t, k = right[xl], left[xr], total[xl], left[x]
    else:
        xl, xr = lax.rem(x + chips - 1, chips), lax.rem(x + 1, chips)
        n, m, t, k = pick(right, xl), pick(left, xr), pick(total, xl), pick(left, x)
    return (xl, t - n, n), (xr, 0, m), (x, k, None)


def pack_amplitudes(groups, share, tiles_ref, assign_ref, src_ref, out_ref, held_ref, block_ref):
    held, total, right, left = balance(tiles_ref, assign_ref, held_ref, block_ref, groups)
    blocks = [block_ref[s] for s in range(groups)]
    for x in range(groups // 2):
        place = 0
        for chip, start, count in runs_of(x, total, right, left, groups // 2):
            if count is None:
                count = share - place
            n0 = jnp.clip(held[2 * chip] - start, 0, count)
            second = jnp.maximum(start - held[2 * chip], 0)
            for block, tile, many in ((blocks[2 * chip], start, n0), (blocks[2 * chip + 1], second, count - n0)):

                def move(i, carry, block=block, tile=tile, place=place):
                    data = src_ref[block, :, pl.ds(pl.multiple_of((tile + i) * TP, TP), TP)]
                    into = pl.ds(pl.multiple_of((place + i) * TP, TP), TP)
                    for copy in range(4):
                        out_ref[4 * x + copy, :, into] = data
                    return carry

                lax.fori_loop(0, many, move, 0)
                place = place + many


def tile_rows(index):
    return pl.ds(pl.multiple_of(index * TP, TP), TP)


def run_copies(jobs, sems):
    for phase in range(2):
        for source, tile, many, out_ref, place, sem in jobs:

            def move(i, carry, source=source, tile=tile, out_ref=out_ref, place=place, sem=sem):
                copy = pltpu.make_async_copy(source.at[tile_rows(tile + i)], out_ref.at[tile_rows(place + i)], sems.at[sem + i])
                copy.start() if phase == 0 else copy.wait()
                return carry

            lax.fori_loop(0, many, move, 0)


def own_tiles(border, core, start, count, mine_ref, other_ref, out_ref, place, sem):
    lower = jnp.clip(border - start, 0, count)
    jobs = []
    for upper, tile, many, at in ((0, start, lower, 0), (1, jnp.maximum(start - border, 0), count - lower, lower)):
        jobs.append((mine_ref, tile, jnp.where(core == upper, many, 0), out_ref, place + at, sem + at))
        jobs.append((other_ref, tile, jnp.where(core != upper, many, 0), out_ref, place + at, sem + at))
    return jobs


def send_tiles(groups, share, tiles_ref, assign_ref, mine_ref, other_ref, *refs):
    *out_refs, held_ref, block_ref, sems = refs
    held, total, right, left = balance(tiles_ref, assign_ref, held_ref, block_ref, groups)
    group = lax.axis_index("grp")
    x, core = lax.div(group, 2), lax.rem(group, 2)
    go_right, go_left = pick(right, x), pick(left, x)
    start = jnp.where(core == 0, pick(total, x) - go_right, 0)
    count = jnp.where(core == 0, go_right, go_left)
    each = share // len(out_refs)
    jobs = []
    for i, ref in enumerate(out_refs):
        many = jnp.clip(count - i * each, 0, each)
        jobs += own_tiles(pick(held[0::2], x), core, start + i * each, many, mine_ref, other_ref, ref, 0, i * each)
    run_copies(jobs, sems)


def join_tiles(groups, share, tiles_ref, assign_ref, mine_ref, other_ref, *refs):
    *moved_refs, out_ref, held_ref, block_ref, sems = refs
    held, total, right, left = balance(tiles_ref, assign_ref, held_ref, block_ref, groups)
    group = lax.axis_index("grp")
    x, core = lax.div(group, 2), lax.rem(group, 2)
    (_, _, n), (_, _, m), (_, start, _) = runs_of(x, total, right, left, groups // 2)
    halves = len(moved_refs) // 2
    each = share // halves
    jobs = []
    for i, ref in enumerate(moved_refs):
        h, below = i % halves, (core == 0) == (i < halves)
        many = jnp.clip(jnp.where(below, n, m) - h * each, 0, each)
        place = jnp.where(below, 0, n) + h * each
        jobs.append((ref, 0, many, out_ref, place, place))
    kept = own_tiles(pick(held[0::2], x), core, start, share - n - m, mine_ref, other_ref, out_ref, n + m, n + m)
    run_copies(jobs + kept, sems)


def multiply(ny, *refs):
    refs, (b_ref, out_ref, a_ref) = refs[:-3], refs[-3:]
    x, y = lax.div(lax.axis_index("grp"), 2), lax.axis_index("row")
    at = 0
    for ref in refs:
        n, octet, wide = ref.shape
        a_ref[at : at + n * octet, :] = ref[...].reshape(n * octet, wide)
        at += n * octet
    out = jnp.dot(a_ref[...], b_ref[...], preferred_element_type=jnp.float32)
    at = row = 0
    for i, ref in enumerate(refs):
        n, octet, _ = ref.shape
        for j in range(2):
            d = lax.rem(lax.rem(y + i % 2, 2) + 2 * j - x + ny, ny)
            for g in range(n // 2):
                start = at + (2 * g + j) * octet
                out_ref[d, row + g * octet : row + (g + 1) * octet, :] = out[start : start + octet]
        at += n * octet
        row += n // 2 * octet if i % 2 else 0


def finish(nz, rows, mine_ref, other_ref, out_ref, sems):
    core, z = lax.rem(lax.axis_index("grp"), 2), lax.axis_index("col")
    h = rows // 2
    last = nz // 2 * rows - h
    for phase in range(2):
        for q in range(nz // 2):
            r = lax.rem(core * (nz // 2) + q - z + nz, nz)
            ends = jnp.logical_or(r == 0, r == nz // 2)
            above = r < nz // 2
            step = jnp.where(above, r, nz - r)
            for part in range(2):
                start = jnp.where(r == 0, 0, jnp.where(r == nz // 2, last, h + rows * (step - 1) + part * h))
                holder = jnp.where(ends, part, jnp.where(above, 1, 0))
                rows_in = pl.ds(pl.multiple_of(start, h), h)
                i = 2 * q + part
                for ref, here in ((mine_ref, holder == core), (other_ref, holder != core)):

                    @pl.when(here)
                    def _(ref=ref, i=i, rows_in=rows_in):
                        copy = pltpu.make_async_copy(ref.at[rows_in], out_ref.at[pl.ds(i * h, h)], sems.at[i])
                        copy.start() if phase == 0 else copy.wait()


def nothing(in_ref, out_ref):
    pass


def collect(block):
    return pl.pallas_call(
        nothing,
        out_shape=jax.ShapeDtypeStruct(block.shape, block.dtype),
        in_specs=[ANY],
        out_specs=ANY,
        input_output_aliases={0: 0},
        cost_estimate=pl.CostEstimate(flops=20_000_000_000, bytes_accessed=0, transcendentals=0),
    )(block)


def near_chips(p, up, down):
    h = p.shape[1] // 2
    a = lax.ppermute(jnp.concatenate([p[2, :h], p[1, h:]]), "grp", up)
    return a, lax.ppermute(jnp.concatenate([p[2, h:], p[3, :h]]), "grp", down)


def passed_on(p, a, b, up, down):
    h = p.shape[1] // 2
    return lax.ppermute(p[1, :h] + a[:h], "grp", up), lax.ppermute(p[3, h:] + b[:h], "grp", down)


def total_of(p, a, b, a2, b2):
    h = p.shape[1] // 2
    return p[0] + jnp.concatenate([a2, a[h:]]) + jnp.concatenate([b[h:], b2])


def body(amplitudes, integrals, block_tiles, assign):
    groups = assign.shape[0]
    _, rows, cap = amplitudes.shape
    cols = integrals.shape[2]
    ny, nz = lax.axis_size("row"), lax.axis_size("col")
    share = 24
    wide = share * TP
    octet = rows // groups
    small = [pltpu.SMEM((groups,), jnp.int32)] * 2
    swap = [(g, g ^ 1) for g in range(groups)]
    up = [(g, (g + 2) % groups) for g in range(groups)]
    down = [(g, (g - 2) % groups) for g in range(groups)]
    apart = [(g, (g + 2 - 4 * (g % 2)) % groups) for g in range(groups)]
    along = [(g * nz + z, g * nz + (z + 1 - 2 * (g % 2)) % nz) for g in range(groups) for z in range(nz)]
    beside = [(g * ny + y, g * ny + (y - 1 + 2 * (g % 2)) % ny) for g in range(groups) for y in range(ny)]
    pairs = [[g * ny + y for g in range(groups) for y in (p, p + 2)] for p in range(2)]
    limit = pltpu.CompilerParams(vmem_limit_bytes=32 * 2**20)
    core = lax.rem(lax.axis_index("grp"), 2)
    barrier = lax.optimization_barrier

    mine = integrals[0]
    other = lax.ppermute(mine, "grp", swap)
    moved = lax.all_to_all(amplitudes[0].reshape(groups, octet, cap), "grp", 0, 0, tiled=True)
    packed = pl.pallas_call(
        functools.partial(pack_amplitudes, groups, share),
        out_shape=jax.ShapeDtypeStruct((2 * groups, octet, wide), jnp.bfloat16),
        in_specs=[SMEM, SMEM, VMEM],
        out_specs=VMEM,
        scratch_shapes=small,
    )(block_tiles, assign, moved)
    pair = lax.all_to_all(packed, ("grp", "row"), 0, 0, axis_index_groups=pairs, tiled=True)

    tiles = jax.ShapeDtypeStruct((wide, cols), jnp.bfloat16)
    half_tiles = jax.ShapeDtypeStruct((wide // 2, cols), jnp.bfloat16)
    scratch = small + [pltpu.SemaphoreType.DMA((share,))]
    sent = pl.pallas_call(
        functools.partial(send_tiles, groups, share),
        out_shape=(half_tiles, half_tiles),
        in_specs=[SMEM, SMEM, ANY, ANY],
        out_specs=(VMEM, VMEM),
        scratch_shapes=scratch,
        compiler_params=limit,
    )(block_tiles, assign, mine, other)
    pair, *sent = barrier((pair, *sent))
    got = [lax.ppermute(part, "grp", apart) for part in sent]
    def half_of(block):
        h = block.shape[0] // 2
        return jnp.where(core == 0, block[:h], block[h:])

    def z_step(block):
        return lax.ppermute(block, ("grp", "col"), along)

    def y_step(block):
        return lax.ppermute(block, ("grp", "row"), beside)

    blocks, near = [half_of(pair), z_step(pair)], [y_step(half_of(pair))]
    for s in range(1, nz // 2):
        near.append(y_step(blocks[s]))
        beyond = z_step(half_of(blocks[s]) if s == nz // 2 - 1 else blocks[s])
        beyond, near[s - 1] = barrier((beyond, collect(near[s - 1])))
        if s < nz // 2 - 1:
            beyond, got[s - 1] = barrier((beyond, got[s - 1]))
        blocks.append(beyond)
    near.append(y_step(blocks[-1]))
    order = [part for both in zip(blocks, near) for part in both]
    theirs = [lax.ppermute(part, "grp", swap) for part in got]
    held = pl.pallas_call(
        functools.partial(join_tiles, groups, share),
        out_shape=tiles,
        in_specs=[SMEM, SMEM] + [ANY] * (2 + len(got) + len(theirs)),
        out_specs=VMEM,
        scratch_shapes=scratch,
        compiler_params=limit,
    )(block_tiles, assign, mine, other, *got, *theirs)

    def sums(parts):
        n = sum(part.shape[0] for part in parts) * octet
        return pl.pallas_call(
            functools.partial(multiply, ny),
            out_shape=jax.ShapeDtypeStruct((ny, n // 4, cols), jnp.float32),
            in_specs=[VMEM] * (len(parts) + 1),
            out_specs=VMEM,
            scratch_shapes=[pltpu.VMEM((n, wide), jnp.bfloat16)],
            compiler_params=limit,
        )(*parts, held)

    early, late = sums(order[:6]), order[6:]
    a, b = near_chips(early, up, down)
    *late, a, b = barrier((*late, a, b))
    late = sums(late)
    c, d = near_chips(late, up, down)
    early = total_of(early, a, b, *passed_on(early, a, b, up, down))
    late = total_of(late, c, d, *passed_on(late, c, d, up, down))
    done = jnp.concatenate([early, late])
    return pl.pallas_call(
        functools.partial(finish, nz, rows),
        out_shape=jax.ShapeDtypeStruct((nz // 2 * rows, cols), jnp.float32),
        in_specs=[ANY, ANY],
        out_specs=ANY,
        scratch_shapes=[pltpu.SemaphoreType.DMA((nz,))],
    )(done, lax.ppermute(done, "grp", swap))


def solution(mesh):
    in_specs = (P("grp", ("row", "col"), None), P("grp", None, ("row", "col")), P(), P())
    out_specs = P("grp", ("row", "col"))
    return jax.shard_map(body, mesh=mesh, in_specs=in_specs, out_specs=out_specs, check_vma=False)
```

```python
import functools

import jax
import jax.numpy as jnp
from jax import lax
from jax.experimental import pallas as pl
from jax.experimental.pallas import tpu as pltpu
from jax.sharding import PartitionSpec as P

TP = 128
ANY = pl.BlockSpec(memory_space=pl.ANY)
SMEM = pl.BlockSpec(memory_space=pltpu.SMEM)
VMEM = pl.BlockSpec(memory_space=pltpu.VMEM)


def balance(tiles_ref, assign_ref, held_ref, block_ref, groups):
    for b in range(groups):
        held_ref[assign_ref[b]] = tiles_ref[b]
        block_ref[assign_ref[b]] = b
    chips = groups // 2
    held = [held_ref[s] for s in range(groups)]
    total = [held[2 * x] + held[2 * x + 1] for x in range(chips)]
    share = 0
    for x in range(chips):
        share = share + total[x]
    share = share // chips
    running, prefix = 0, []
    for x in range(chips):
        running = running + total[x] - share
        prefix.append(running)
    high = functools.reduce(jnp.maximum, prefix)
    low = functools.reduce(jnp.minimum, prefix)
    middle = lax.shift_right_arithmetic(high + low, jnp.int32(1))
    flow = [p - middle for p in prefix]
    right = [jnp.maximum(flow[x], 0) for x in range(chips)]
    left = [jnp.maximum(-flow[(x - 1) % chips], 0) for x in range(chips)]
    return held, total, right, left


def pick(values, index):
    out = values[0]
    for i in range(1, len(values)):
        out = jnp.where(index == i, values[i], out)
    return out


def runs_of(x, total, right, left, chips):
    if isinstance(x, int):
        xl, xr = (x - 1) % chips, (x + 1) % chips
        n, m, t, k = right[xl], left[xr], total[xl], left[x]
    else:
        xl, xr = lax.rem(x + chips - 1, chips), lax.rem(x + 1, chips)
        n, m, t, k = pick(right, xl), pick(left, xr), pick(total, xl), pick(left, x)
    return (xl, t - n, n), (xr, 0, m), (x, k, None)


def pack_amplitudes(groups, share, tiles_ref, assign_ref, src_ref, out_ref, held_ref, block_ref):
    held, total, right, left = balance(tiles_ref, assign_ref, held_ref, block_ref, groups)
    blocks = [block_ref[s] for s in range(groups)]
    each = share // 2
    for x in range(groups // 2):
        place = 0
        for chip, start, count in runs_of(x, total, right, left, groups // 2):
            if count is None:
                count = share - place
            n0 = jnp.clip(held[2 * chip] - start, 0, count)
            second = jnp.maximum(start - held[2 * chip], 0)
            for block, tile, many in ((blocks[2 * chip], start, n0), (blocks[2 * chip + 1], second, count - n0)):

                def move(i, carry, block=block, tile=tile, place=place):
                    data = src_ref[block, :, pl.ds(pl.multiple_of((tile + i) * TP, TP), TP)]
                    upper = (place + i >= each).astype(jnp.int32)
                    into = pl.ds(pl.multiple_of((place + i - upper * each) * TP, TP), TP)
                    for j in range(2):
                        out_ref[4 * x + 2 * upper + j, :, into] = data
                    return carry

                lax.fori_loop(0, many, move, 0)
                place = place + many


def tile_rows(index):
    return pl.ds(pl.multiple_of(index * TP, TP), TP)


def run_copies(jobs, out_ref, sems):
    for phase in range(2):
        for source, tile, many, place in jobs:

            def move(i, carry, source=source, tile=tile, place=place):
                copy = pltpu.make_async_copy(source.at[tile_rows(tile + i)], out_ref.at[tile_rows(place + i)], sems.at[place + i])
                copy.start() if phase == 0 else copy.wait()
                return carry

            lax.fori_loop(0, many, move, 0)


def own_tiles(border, core, start, count, mine_ref, other_ref, place):
    lower = jnp.clip(border - start, 0, count)
    jobs = []
    for upper, tile, many, at in ((0, start, lower, place), (1, jnp.maximum(start - border, 0), count - lower, place + lower)):
        jobs.append((mine_ref, tile, jnp.where(core == upper, many, 0), at))
        jobs.append((other_ref, tile, jnp.where(core != upper, many, 0), at))
    return jobs


def send_tiles(groups, share, tiles_ref, assign_ref, mine_ref, other_ref, out_ref, held_ref, block_ref, sems):
    held, total, right, left = balance(tiles_ref, assign_ref, held_ref, block_ref, groups)
    group = lax.axis_index("grp")
    x, core = lax.div(group, 2), lax.rem(group, 2)
    go_right, go_left = pick(right, x), pick(left, x)
    start = jnp.where(core == 0, pick(total, x) - go_right, 0)
    count = jnp.where(core == 0, go_right, go_left)
    run_copies(own_tiles(pick(held[0::2], x), core, start, count, mine_ref, other_ref, 0), out_ref, sems)


def join_tiles(groups, share, tiles_ref, assign_ref, mine_ref, other_ref, got_ref, *refs):
    *their_refs, out_ref, held_ref, block_ref, sems = refs
    held, total, right, left = balance(tiles_ref, assign_ref, held_ref, block_ref, groups)
    group = lax.axis_index("grp")
    x, core = lax.div(group, 2), lax.rem(group, 2)
    (_, _, n), (_, _, m), (_, start, _) = runs_of(x, total, right, left, groups // 2)
    jobs = [
        (got_ref, 0, jnp.where(core == 0, n, 0), 0),
        (got_ref, 0, jnp.where(core == 0, 0, m), n),
    ]
    each = share // len(their_refs)
    for i, ref in enumerate(their_refs):
        jobs.append((ref, 0, jnp.clip(jnp.where(core == 0, m, n) - i * each, 0, each), jnp.where(core == 0, n, 0) + i * each))
    jobs += own_tiles(pick(held[0::2], x), core, start, share - n - m, mine_ref, other_ref, n + m)
    run_copies(jobs, out_ref, sems)


def multiply(ny, *refs):
    refs, (b_ref, out_ref, a_ref) = refs[:-3], refs[-3:]
    group, y = lax.axis_index("grp"), lax.axis_index("row")
    x, core = lax.div(group, 2), lax.rem(group, 2)
    at = 0
    for ref in refs:
        _, n, octet, each = ref.shape
        for k in range(2):
            a_ref[at : at + n * octet, k * each : (k + 1) * each] = ref[k].reshape(n * octet, each)
        at += n * octet
    first = pl.ds(pl.multiple_of(core * each, each), each)
    last = pl.ds(pl.multiple_of((1 - core) * each, each), each)
    out = jnp.dot(a_ref[:, :each], b_ref[first, :], preferred_element_type=jnp.float32)
    out += jnp.dot(a_ref[:, each:], b_ref[last, :], preferred_element_type=jnp.float32)
    at = row = 0
    for i, ref in enumerate(refs):
        _, n, octet, _ = ref.shape
        for j in range(2):
            d = lax.rem(lax.rem(y + i % 2, 2) + 2 * j - x + ny, ny)
            for g in range(n // 2):
                start = at + (2 * g + j) * octet
                out_ref[d, row + g * octet : row + (g + 1) * octet, :] = out[start : start + octet]
        at += n * octet
        row += n // 2 * octet if i % 2 else 0


def finish(nz, rows, mine_ref, other_ref, out_ref, sems):
    core, z = lax.rem(lax.axis_index("grp"), 2), lax.axis_index("col")
    h = rows // 2
    last = nz // 2 * rows - h
    for phase in range(2):
        for q in range(nz // 2):
            r = lax.rem(core * (nz // 2) + q - z + nz, nz)
            ends = jnp.logical_or(r == 0, r == nz // 2)
            above = r < nz // 2
            step = jnp.where(above, r, nz - r)
            for part in range(2):
                start = jnp.where(r == 0, 0, jnp.where(r == nz // 2, last, h + rows * (step - 1) + part * h))
                holder = jnp.where(ends, part, jnp.where(above, 1, 0))
                rows_in = pl.ds(pl.multiple_of(start, h), h)
                i = 2 * q + part
                for ref, here in ((mine_ref, holder == core), (other_ref, holder != core)):

                    @pl.when(here)
                    def _(ref=ref, i=i, rows_in=rows_in):
                        copy = pltpu.make_async_copy(ref.at[rows_in], out_ref.at[pl.ds(i * h, h)], sems.at[i])
                        copy.start() if phase == 0 else copy.wait()


def near_chips(p, up, down):
    h = p.shape[1] // 2
    a = lax.ppermute(jnp.concatenate([p[2, :h], p[1, h:]]), "grp", up)
    return a, lax.ppermute(jnp.concatenate([p[2, h:], p[3, :h]]), "grp", down)


def passed_on(p, a, b, up, down):
    h = p.shape[1] // 2
    return lax.ppermute(p[1, :h] + a[:h], "grp", up), lax.ppermute(p[3, h:] + b[:h], "grp", down)


def total_of(p, a, b, a2, b2):
    h = p.shape[1] // 2
    return p[0] + jnp.concatenate([a2, a[h:]]) + jnp.concatenate([b[h:], b2])


def body(amplitudes, integrals, block_tiles, assign):
    groups = assign.shape[0]
    _, rows, cap = amplitudes.shape
    cols = integrals.shape[2]
    ny, nz = lax.axis_size("row"), lax.axis_size("col")
    share = 24
    wide = share * TP
    octet = rows // groups
    small = [pltpu.SMEM((groups,), jnp.int32)] * 2
    swap = [(g, g ^ 1) for g in range(groups)]
    up = [(g, (g + 2) % groups) for g in range(groups)]
    down = [(g, (g - 2) % groups) for g in range(groups)]
    opposite = [(g, (g + 4) % groups) for g in range(groups)]
    apart = [(g, (g + 2 - 4 * (g % 2)) % groups) for g in range(groups)]
    along = [(g * nz + z, g * nz + (z + 1 - 2 * (g % 2)) % nz) for g in range(groups) for z in range(nz)]
    beside = [(g * ny + y, g * ny + (y - 1 + 2 * (g % 2)) % ny) for g in range(groups) for y in range(ny)]
    pairs = [[g * ny + y for g in range(groups) for y in (p, p + 2)] for p in range(2)]
    limit = pltpu.CompilerParams(vmem_limit_bytes=32 * 2**20)
    core = lax.rem(lax.axis_index("grp"), 2)
    barrier = lax.optimization_barrier

    mine = integrals[0]
    other = lax.ppermute(mine, "grp", swap)
    moved = lax.all_to_all(amplitudes[0].reshape(groups, octet, cap), "grp", 0, 0, tiled=True)
    packed = pl.pallas_call(
        functools.partial(pack_amplitudes, groups, share),
        out_shape=jax.ShapeDtypeStruct((2 * groups, octet, wide // 2), jnp.bfloat16),
        in_specs=[SMEM, SMEM, VMEM],
        out_specs=VMEM,
        scratch_shapes=small,
    )(block_tiles, assign, moved)
    pair = lax.all_to_all(packed, ("grp", "row"), 0, 0, axis_index_groups=pairs, tiled=True)

    tiles = jax.ShapeDtypeStruct((wide, cols), jnp.bfloat16)
    scratch = small + [pltpu.SemaphoreType.DMA((share,))]
    sent = pl.pallas_call(
        functools.partial(send_tiles, groups, share),
        out_shape=tiles,
        in_specs=[SMEM, SMEM, ANY, ANY],
        out_specs=VMEM,
        scratch_shapes=scratch,
        compiler_params=limit,
    )(block_tiles, assign, mine, other)
    pair, sent = barrier((pair, sent))
    got = lax.ppermute(sent, "grp", apart)
    def half_of(block):
        h = block.shape[1] // 2
        return jnp.where(core == 0, block[:, :h], block[:, h:])

    def z_step(block):
        return lax.ppermute(block, ("grp", "col"), along)

    def y_step(block):
        return lax.ppermute(block, ("grp", "row"), beside)

    pair_too = lax.ppermute(pair, "grp", swap)
    block = half_of(jnp.stack([pair, pair_too]))
    order = [block]
    block, near = barrier((jnp.stack([z_step(pair), z_step(pair_too)]), y_step(block)))
    order += [near]
    for s in range(1, nz // 2 - 1):
        order += [block]
        block, near = barrier((z_step(block), y_step(block)))
        if s == nz // 2 - 3:
            block, near, got = barrier((block, near, got))
        order += [near]
    theirs = [lax.ppermute(part, "grp", swap) for part in jnp.split(got, 2)]
    end = z_step(half_of(block))
    order += [block, y_step(block), end, y_step(end)]

    held = pl.pallas_call(
        functools.partial(join_tiles, groups, share),
        out_shape=tiles,
        in_specs=[SMEM, SMEM] + [ANY] * (3 + len(theirs)),
        out_specs=VMEM,
        scratch_shapes=scratch,
        compiler_params=limit,
    )(block_tiles, assign, mine, other, got, *theirs)

    def sums(parts):
        n = sum(part.shape[1] for part in parts) * octet
        return pl.pallas_call(
            functools.partial(multiply, ny),
            out_shape=jax.ShapeDtypeStruct((ny, n // 4, cols), jnp.float32),
            in_specs=[VMEM] * (len(parts) + 1),
            out_specs=VMEM,
            scratch_shapes=[pltpu.VMEM((n, wide), jnp.bfloat16)],
            compiler_params=limit,
        )(*parts, held)

    early, late = sums(order[:6]), order[6:]
    a, b = near_chips(early, up, down)
    *late, a, b = barrier((*late, a, b))
    late = sums(late)
    ways = zip((1, 3, 2), (up, down, opposite))
    late = sum([lax.ppermute(late[d], "grp", way) for d, way in ways], late[0])
    early = total_of(early, a, b, *passed_on(early, a, b, up, down))
    done = jnp.concatenate([early, late])
    return pl.pallas_call(
        functools.partial(finish, nz, rows),
        out_shape=jax.ShapeDtypeStruct((nz // 2 * rows, cols), jnp.float32),
        in_specs=[ANY, ANY],
        out_specs=VMEM,
        scratch_shapes=[pltpu.SemaphoreType.DMA((nz,))],
    )(done, lax.ppermute(done, "grp", swap))


def solution(mesh):
    in_specs = (P("grp", ("row", "col"), None), P("grp", None, ("row", "col")), P(), P())
    out_specs = P("grp", ("row", "col"))
    return jax.shard_map(body, mesh=mesh, in_specs=in_specs, out_specs=out_specs, check_vma=False)
```

```python
import functools

import jax
import jax.numpy as jnp
from jax import lax
from jax.experimental import pallas as pl
from jax.experimental.pallas import tpu as pltpu
from jax.sharding import PartitionSpec as P

TP = 128
ANY = pl.BlockSpec(memory_space=pl.ANY)
SMEM = pl.BlockSpec(memory_space=pltpu.SMEM)
VMEM = pl.BlockSpec(memory_space=pltpu.VMEM)


def balance(tiles_ref, assign_ref, held_ref, block_ref, groups):
    for b in range(groups):
        held_ref[assign_ref[b]] = tiles_ref[b]
        block_ref[assign_ref[b]] = b
    chips = groups // 2
    held = [held_ref[s] for s in range(groups)]
    total = [held[2 * x] + held[2 * x + 1] for x in range(chips)]
    share = 0
    for x in range(chips):
        share = share + total[x]
    share = share // chips
    running, prefix = 0, []
    for x in range(chips):
        running = running + total[x] - share
        prefix.append(running)
    high = functools.reduce(jnp.maximum, prefix)
    low = functools.reduce(jnp.minimum, prefix)
    middle = lax.shift_right_arithmetic(high + low, jnp.int32(1))
    flow = [p - middle for p in prefix]
    right = [jnp.maximum(flow[x], 0) for x in range(chips)]
    left = [jnp.maximum(-flow[(x - 1) % chips], 0) for x in range(chips)]
    return held, total, right, left


def pick(values, index):
    out = values[0]
    for i in range(1, len(values)):
        out = jnp.where(index == i, values[i], out)
    return out


def runs_of(x, total, right, left, chips):
    if isinstance(x, int):
        xl, xr = (x - 1) % chips, (x + 1) % chips
        n, m, t, k = right[xl], left[xr], total[xl], left[x]
    else:
        xl, xr = lax.rem(x + chips - 1, chips), lax.rem(x + 1, chips)
        n, m, t, k = pick(right, xl), pick(left, xr), pick(total, xl), pick(left, x)
    return (xl, t - n, n), (xr, 0, m), (x, k, None)


def pack_amplitudes(groups, share, tiles_ref, assign_ref, src_ref, out_ref, held_ref, block_ref):
    held, total, right, left = balance(tiles_ref, assign_ref, held_ref, block_ref, groups)
    blocks = [block_ref[s] for s in range(groups)]
    each = share // 2
    for x in range(groups // 2):
        place = 0
        for chip, start, count in runs_of(x, total, right, left, groups // 2):
            if count is None:
                count = share - place
            n0 = jnp.clip(held[2 * chip] - start, 0, count)
            second = jnp.maximum(start - held[2 * chip], 0)
            for block, tile, many in ((blocks[2 * chip], start, n0), (blocks[2 * chip + 1], second, count - n0)):

                def move(i, carry, block=block, tile=tile, place=place):
                    data = src_ref[block, :, pl.ds(pl.multiple_of((tile + i) * TP, TP), TP)]
                    upper = (place + i >= each).astype(jnp.int32)
                    into = pl.ds(pl.multiple_of((place + i - upper * each) * TP, TP), TP)
                    for j in range(2):
                        out_ref[4 * x + 2 * upper + j, :, into] = data
                    return carry

                lax.fori_loop(0, many, move, 0)
                place = place + many


def tile_rows(index):
    return pl.ds(pl.multiple_of(index * TP, TP), TP)


def run_copies(jobs, out_ref, sems):
    for phase in range(2):
        for source, tile, many, place in jobs:

            def move(i, carry, source=source, tile=tile, place=place):
                copy = pltpu.make_async_copy(source.at[tile_rows(tile + i)], out_ref.at[tile_rows(place + i)], sems.at[place + i])
                copy.start() if phase == 0 else copy.wait()
                return carry

            lax.fori_loop(0, many, move, 0)


def own_tiles(border, core, start, count, mine_ref, other_ref, place):
    lower = jnp.clip(border - start, 0, count)
    jobs = []
    for upper, tile, many, at in ((0, start, lower, place), (1, jnp.maximum(start - border, 0), count - lower, place + lower)):
        jobs.append((mine_ref, tile, jnp.where(core == upper, many, 0), at))
        jobs.append((other_ref, tile, jnp.where(core != upper, many, 0), at))
    return jobs


def send_tiles(groups, share, tiles_ref, assign_ref, mine_ref, other_ref, out_ref, held_ref, block_ref, sems):
    held, total, right, left = balance(tiles_ref, assign_ref, held_ref, block_ref, groups)
    group = lax.axis_index("grp")
    x, core = lax.div(group, 2), lax.rem(group, 2)
    go_right, go_left = pick(right, x), pick(left, x)
    start = jnp.where(core == 0, pick(total, x) - go_right, 0)
    count = jnp.where(core == 0, go_right, go_left)
    run_copies(own_tiles(pick(held[0::2], x), core, start, count, mine_ref, other_ref, 0), out_ref, sems)


def join_tiles(groups, share, tiles_ref, assign_ref, mine_ref, other_ref, got_ref, *refs):
    *their_refs, out_ref, held_ref, block_ref, sems = refs
    held, total, right, left = balance(tiles_ref, assign_ref, held_ref, block_ref, groups)
    group = lax.axis_index("grp")
    x, core = lax.div(group, 2), lax.rem(group, 2)
    (_, _, n), (_, _, m), (_, start, _) = runs_of(x, total, right, left, groups // 2)
    jobs = [
        (got_ref, 0, jnp.where(core == 0, n, 0), 0),
        (got_ref, 0, jnp.where(core == 0, 0, m), n),
    ]
    each = share // len(their_refs)
    for i, ref in enumerate(their_refs):
        jobs.append((ref, 0, jnp.clip(jnp.where(core == 0, m, n) - i * each, 0, each), jnp.where(core == 0, n, 0) + i * each))
    jobs += own_tiles(pick(held[0::2], x), core, start, share - n - m, mine_ref, other_ref, n + m)
    run_copies(jobs, out_ref, sems)


def multiply(ny, *refs):
    refs, (b_ref, out_ref, a_ref) = refs[:-3], refs[-3:]
    group, y = lax.axis_index("grp"), lax.axis_index("row")
    x, core = lax.div(group, 2), lax.rem(group, 2)
    at = 0
    for ref in refs:
        _, n, octet, each = ref.shape
        for k in range(2):
            a_ref[at : at + n * octet, k * each : (k + 1) * each] = ref[k].reshape(n * octet, each)
        at += n * octet
    first = pl.ds(pl.multiple_of(core * each, each), each)
    last = pl.ds(pl.multiple_of((1 - core) * each, each), each)
    out = jnp.dot(a_ref[:, :each], b_ref[first, :], preferred_element_type=jnp.float32)
    out += jnp.dot(a_ref[:, each:], b_ref[last, :], preferred_element_type=jnp.float32)
    at = row = 0
    for i, ref in enumerate(refs):
        _, n, octet, _ = ref.shape
        for j in range(2):
            d = lax.rem(lax.rem(y + i % 2, 2) + 2 * j - x + ny, ny)
            for g in range(n // 2):
                start = at + (2 * g + j) * octet
                out_ref[d, row + g * octet : row + (g + 1) * octet, :] = out[start : start + octet]
        at += n * octet
        row += n // 2 * octet if i % 2 else 0


def finish(nz, rows, mine_ref, other_ref, out_ref):
    core, z = lax.rem(lax.axis_index("grp"), 2), lax.axis_index("col")
    h = rows // 2
    last = nz // 2 * rows - h
    for q in range(nz // 2):
        r = lax.rem(core * (nz // 2) + q - z + nz, nz)
        ends = jnp.logical_or(r == 0, r == nz // 2)
        above = r < nz // 2
        step = jnp.where(above, r, nz - r)
        for part in range(2):
            start = jnp.where(r == 0, 0, jnp.where(r == nz // 2, last, h + rows * (step - 1) + part * h))
            holder = jnp.where(ends, part, jnp.where(above, 1, 0))
            rows_in = pl.ds(pl.multiple_of(start, h), h)
            for ref, here in ((mine_ref, holder == core), (other_ref, holder != core)):

                @pl.when(here)
                def _(ref=ref, q=q, part=part, rows_in=rows_in):
                    out_ref[q * rows + part * h : q * rows + (part + 1) * h, :] = ref[rows_in, :]


def near_chips(p, up, down):
    h = p.shape[1] // 2
    a = lax.ppermute(jnp.concatenate([p[2, :h], p[1, h:]]), "grp", up)
    return a, lax.ppermute(jnp.concatenate([p[2, h:], p[3, :h]]), "grp", down)


def body(amplitudes, integrals, block_tiles, assign):
    groups = assign.shape[0]
    _, rows, cap = amplitudes.shape
    cols = integrals.shape[2]
    ny, nz = lax.axis_size("row"), lax.axis_size("col")
    share = 24
    wide = share * TP
    octet = rows // groups
    small = [pltpu.SMEM((groups,), jnp.int32)] * 2
    swap = [(g, g ^ 1) for g in range(groups)]
    up = [(g, (g + 2) % groups) for g in range(groups)]
    down = [(g, (g - 2) % groups) for g in range(groups)]
    opposite = [(g, (g + 4) % groups) for g in range(groups)]
    apart = [(g, (g + 2 - 4 * (g % 2)) % groups) for g in range(groups)]
    along = [(g * nz + z, g * nz + (z + 1 - 2 * (g % 2)) % nz) for g in range(groups) for z in range(nz)]
    beside = [(g * ny + y, g * ny + (y - 1 + 2 * (g % 2)) % ny) for g in range(groups) for y in range(ny)]
    pairs = [[g * ny + y for g in range(groups) for y in (p, p + 2)] for p in range(2)]
    limit = pltpu.CompilerParams(vmem_limit_bytes=32 * 2**20)
    core = lax.rem(lax.axis_index("grp"), 2)
    barrier = lax.optimization_barrier

    mine = integrals[0]
    other = lax.ppermute(mine, "grp", swap)
    moved = lax.all_to_all(amplitudes[0].reshape(groups, octet, cap), "grp", 0, 0, tiled=True)
    packed = pl.pallas_call(
        functools.partial(pack_amplitudes, groups, share),
        out_shape=jax.ShapeDtypeStruct((2 * groups, octet, wide // 2), jnp.bfloat16),
        in_specs=[SMEM, SMEM, VMEM],
        out_specs=VMEM,
        scratch_shapes=small,
        compiler_params=pltpu.CompilerParams(vmem_limit_bytes=8 * 2**20),
    )(block_tiles, assign, moved)
    pair = lax.all_to_all(packed, ("grp", "row"), 0, 0, axis_index_groups=pairs, tiled=True)

    tiles = jax.ShapeDtypeStruct((wide, cols), jnp.bfloat16)
    scratch = small + [pltpu.SemaphoreType.DMA((share,))]
    sent = pl.pallas_call(
        functools.partial(send_tiles, groups, share),
        out_shape=tiles,
        in_specs=[SMEM, SMEM, ANY, ANY],
        out_specs=VMEM,
        scratch_shapes=scratch,
        compiler_params=limit,
    )(block_tiles, assign, mine, other)
    pair, sent = barrier((pair, sent))
    got = lax.ppermute(sent, "grp", apart)
    def half_of(block):
        h = block.shape[1] // 2
        return jnp.where(core == 0, block[:, :h], block[:, h:])

    def z_step(block):
        return lax.ppermute(block, ("grp", "col"), along)

    def y_step(block):
        return lax.ppermute(block, ("grp", "row"), beside)

    pair_too = lax.ppermute(pair, "grp", swap)
    block = half_of(jnp.stack([pair, pair_too]))
    order = [block]
    block, near = barrier((jnp.stack([z_step(pair), z_step(pair_too)]), y_step(block)))
    order += [near]
    for s in range(1, nz // 2 - 1):
        order += [block]
        block, near = barrier((z_step(block), y_step(block)))
        if s == nz // 2 - 3:
            block, near, got = barrier((block, near, got))
        order += [near]
    theirs = [lax.ppermute(part, "grp", swap) for part in jnp.split(got, 2)]
    end = z_step(half_of(block))
    order += [block, y_step(block), end, y_step(end)]

    held = pl.pallas_call(
        functools.partial(join_tiles, groups, share),
        out_shape=tiles,
        in_specs=[SMEM, SMEM] + [ANY] * (3 + len(theirs)),
        out_specs=VMEM,
        scratch_shapes=scratch,
        compiler_params=limit,
    )(block_tiles, assign, mine, other, got, *theirs)

    def sums(parts):
        n = sum(part.shape[1] for part in parts) * octet
        return pl.pallas_call(
            functools.partial(multiply, ny),
            out_shape=jax.ShapeDtypeStruct((ny, n // 4, cols), jnp.float32),
            in_specs=[VMEM] * (len(parts) + 1),
            out_specs=VMEM,
            scratch_shapes=[pltpu.VMEM((n, wide), jnp.bfloat16)],
            compiler_params=limit,
        )(*parts, held)

    early, late = sums(order[:6]), order[6:]
    a, b = near_chips(early, up, down)
    *late, a, b = barrier((*late, a, b))
    late = sums(late)
    h, n = early.shape[1] // 2, late.shape[1]
    c = lax.ppermute(late[2], "grp", opposite)
    a2 = lax.ppermute(jnp.concatenate([late[1], early[1, :h] + a[:h]]), "grp", up)
    b2 = lax.ppermute(jnp.concatenate([late[3], early[3, h:] + b[:h]]), "grp", down)
    early = early[0] + jnp.concatenate([a2[n:], a[h:]]) + jnp.concatenate([b[h:], b2[n:]])
    done = jnp.concatenate([early, late[0] + a2[:n] + b2[:n] + c])
    return pl.pallas_call(
        functools.partial(finish, nz, rows),
        out_shape=jax.ShapeDtypeStruct((nz // 2 * rows, cols), jnp.float32),
        in_specs=[VMEM, VMEM],
        out_specs=VMEM,
        compiler_params=pltpu.CompilerParams(vmem_limit_bytes=8 * 2**20),
    )(done, lax.ppermute(done, "grp", swap))


def solution(mesh):
    in_specs = (P("grp", ("row", "col"), None), P("grp", None, ("row", "col")), P(), P())
    out_specs = P("grp", ("row", "col"))
    return jax.shard_map(body, mesh=mesh, in_specs=in_specs, out_specs=out_specs, check_vma=False)
```

```python
import functools

import jax
import jax.numpy as jnp
from jax import lax
from jax.experimental import pallas as pl
from jax.experimental.pallas import tpu as pltpu
from jax.sharding import PartitionSpec as P

TP = 128
ANY = pl.BlockSpec(memory_space=pl.ANY)
SMEM = pl.BlockSpec(memory_space=pltpu.SMEM)
VMEM = pl.BlockSpec(memory_space=pltpu.VMEM)


def balance(both_ref, held_ref, block_ref, groups):
    for b in range(groups):
        held_ref[both_ref[1, b]] = both_ref[0, b]
        block_ref[both_ref[1, b]] = b
    chips = groups // 2
    held = [held_ref[s] for s in range(groups)]
    total = [held[2 * x] + held[2 * x + 1] for x in range(chips)]
    share = 0
    for x in range(chips):
        share = share + total[x]
    share = share // chips
    running, prefix = 0, []
    for x in range(chips):
        running = running + total[x] - share
        prefix.append(running)
    high = functools.reduce(jnp.maximum, prefix)
    low = functools.reduce(jnp.minimum, prefix)
    middle = lax.shift_right_arithmetic(high + low, jnp.int32(1))
    flow = [p - middle for p in prefix]
    right = [jnp.maximum(flow[x], 0) for x in range(chips)]
    left = [jnp.maximum(-flow[(x - 1) % chips], 0) for x in range(chips)]
    return held, total, right, left


def pick(values, index):
    out = values[0]
    for i in range(1, len(values)):
        out = jnp.where(index == i, values[i], out)
    return out


def runs_of(x, total, right, left, chips):
    if isinstance(x, int):
        xl, xr = (x - 1) % chips, (x + 1) % chips
        n, m, t, k = right[xl], left[xr], total[xl], left[x]
    else:
        xl, xr = lax.rem(x + chips - 1, chips), lax.rem(x + 1, chips)
        n, m, t, k = pick(right, xl), pick(left, xr), pick(total, xl), pick(left, x)
    return (xl, t - n, n), (xr, 0, m), (x, k, None)


def pack_amplitudes(groups, share, both_ref, src_ref, out_ref, held_ref, block_ref):
    held, total, right, left = balance(both_ref, held_ref, block_ref, groups)
    blocks = [block_ref[s] for s in range(groups)]
    each = share // 2
    for x in range(groups // 2):
        place = 0
        for chip, start, count in runs_of(x, total, right, left, groups // 2):
            if count is None:
                count = share - place
            n0 = jnp.clip(held[2 * chip] - start, 0, count)
            second = jnp.maximum(start - held[2 * chip], 0)
            for block, tile, many in ((blocks[2 * chip], start, n0), (blocks[2 * chip + 1], second, count - n0)):

                def move(i, carry, block=block, tile=tile, place=place):
                    data = src_ref[block, :, pl.ds(pl.multiple_of((tile + i) * TP, TP), TP)]
                    upper = (place + i >= each).astype(jnp.int32)
                    into = pl.ds(pl.multiple_of((place + i - upper * each) * TP, TP), TP)
                    for j in range(2):
                        out_ref[4 * x + 2 * upper + j, :, into] = data
                    return carry

                lax.fori_loop(0, many, move, 0)
                place = place + many


def tile_rows(index):
    return pl.ds(pl.multiple_of(index * TP, TP), TP)


def run_copies(jobs, out_ref, sems):
    for phase in range(2):
        for source, tile, many, place in jobs:

            def move(i, carry, source=source, tile=tile, place=place):
                copy = pltpu.make_async_copy(source.at[tile_rows(tile + i)], out_ref.at[tile_rows(place + i)], sems.at[place + i])
                copy.start() if phase == 0 else copy.wait()
                return carry

            lax.fori_loop(0, many, move, 0)


def own_tiles(border, core, start, count, mine_ref, other_ref, place):
    lower = jnp.clip(border - start, 0, count)
    jobs = []
    for upper, tile, many, at in ((0, start, lower, place), (1, jnp.maximum(start - border, 0), count - lower, place + lower)):
        jobs.append((mine_ref, tile, jnp.where(core == upper, many, 0), at))
        jobs.append((other_ref, tile, jnp.where(core != upper, many, 0), at))
    return jobs


def send_tiles(groups, share, both_ref, mine_ref, other_ref, out_ref, held_ref, block_ref, sems):
    held, total, right, left = balance(both_ref, held_ref, block_ref, groups)
    group = lax.axis_index("grp")
    x, core = lax.div(group, 2), lax.rem(group, 2)
    go_right, go_left = pick(right, x), pick(left, x)
    start = jnp.where(core == 0, pick(total, x) - go_right, 0)
    count = jnp.where(core == 0, go_right, go_left)
    run_copies(own_tiles(pick(held[0::2], x), core, start, count, mine_ref, other_ref, 0), out_ref, sems)


def join_tiles(groups, share, both_ref, mine_ref, other_ref, got_ref, *refs):
    *their_refs, out_ref, held_ref, block_ref, sems = refs
    held, total, right, left = balance(both_ref, held_ref, block_ref, groups)
    group = lax.axis_index("grp")
    x, core = lax.div(group, 2), lax.rem(group, 2)
    (_, _, n), (_, _, m), (_, start, _) = runs_of(x, total, right, left, groups // 2)
    jobs = [
        (got_ref, 0, jnp.where(core == 0, n, 0), 0),
        (got_ref, 0, jnp.where(core == 0, 0, m), n),
    ]
    each = share // len(their_refs)
    for i, ref in enumerate(their_refs):
        jobs.append((ref, 0, jnp.clip(jnp.where(core == 0, m, n) - i * each, 0, each), jnp.where(core == 0, n, 0) + i * each))
    jobs += own_tiles(pick(held[0::2], x), core, start, share - n - m, mine_ref, other_ref, n + m)
    run_copies(jobs, out_ref, sems)


def multiply(ny, *refs):
    refs, (b_ref, out_ref, a_ref) = refs[:-3], refs[-3:]
    group, y = lax.axis_index("grp"), lax.axis_index("row")
    x, core = lax.div(group, 2), lax.rem(group, 2)
    at = 0
    for ref in refs:
        _, n, octet, each = ref.shape
        for k in range(2):
            a_ref[at : at + n * octet, k * each : (k + 1) * each] = ref[k].reshape(n * octet, each)
        at += n * octet
    first = pl.ds(pl.multiple_of(core * each, each), each)
    last = pl.ds(pl.multiple_of((1 - core) * each, each), each)
    out = jnp.dot(a_ref[:, :each], b_ref[first, :], preferred_element_type=jnp.float32)
    out += jnp.dot(a_ref[:, each:], b_ref[last, :], preferred_element_type=jnp.float32)
    at = row = 0
    for i, ref in enumerate(refs):
        _, n, octet, _ = ref.shape
        for j in range(2):
            d = lax.rem(lax.rem(y + i % 2, 2) + 2 * j - x + ny, ny)
            for g in range(n // 2):
                start = at + (2 * g + j) * octet
                out_ref[d, row + g * octet : row + (g + 1) * octet, :] = out[start : start + octet]
        at += n * octet
        row += n // 2 * octet if i % 2 else 0


def finish(nz, rows, mine_ref, other_ref, out_ref):
    core, z = lax.rem(lax.axis_index("grp"), 2), lax.axis_index("col")
    h = rows // 2
    last = nz // 2 * rows - h
    for q in range(nz // 2):
        r = lax.rem(core * (nz // 2) + q - z + nz, nz)
        ends = jnp.logical_or(r == 0, r == nz // 2)
        above = r < nz // 2
        step = jnp.where(above, r, nz - r)
        for part in range(2):
            start = jnp.where(r == 0, 0, jnp.where(r == nz // 2, last, h + rows * (step - 1) + part * h))
            holder = jnp.where(ends, part, jnp.where(above, 1, 0))
            rows_in = pl.ds(pl.multiple_of(start, h), h)
            for ref, here in ((mine_ref, holder == core), (other_ref, holder != core)):

                @pl.when(here)
                def _(ref=ref, q=q, part=part, rows_in=rows_in):
                    out_ref[q * rows + part * h : q * rows + (part + 1) * h, :] = ref[rows_in, :]


def near_chips(p, up, down):
    h = p.shape[1] // 2
    a = lax.ppermute(jnp.concatenate([p[2, :h], p[1, h:]]), "grp", up)
    return a, lax.ppermute(jnp.concatenate([p[2, h:], p[3, :h]]), "grp", down)


def body(amplitudes, integrals, block_tiles, assign):
    groups = assign.shape[0]
    _, rows, cap = amplitudes.shape
    cols = integrals.shape[2]
    ny, nz = lax.axis_size("row"), lax.axis_size("col")
    share = 24
    wide = share * TP
    octet = rows // groups
    small = [pltpu.SMEM((groups,), jnp.int32)] * 2
    swap = [(g, g ^ 1) for g in range(groups)]
    up = [(g, (g + 2) % groups) for g in range(groups)]
    down = [(g, (g - 2) % groups) for g in range(groups)]
    opposite = [(g, (g + 4) % groups) for g in range(groups)]
    apart = [(g, (g + 2 - 4 * (g % 2)) % groups) for g in range(groups)]
    along = [(g * nz + z, g * nz + (z + 1 - 2 * (g % 2)) % nz) for g in range(groups) for z in range(nz)]
    beside = [(g * ny + y, g * ny + (y - 1 + 2 * (g % 2)) % ny) for g in range(groups) for y in range(ny)]
    pairs = [[g * ny + y for g in range(groups) for y in (p, p + 2)] for p in range(2)]
    limit = pltpu.CompilerParams(vmem_limit_bytes=32 * 2**20)
    core = lax.rem(lax.axis_index("grp"), 2)
    barrier = lax.optimization_barrier

    both = jnp.stack([block_tiles, assign])
    mine = integrals[0]
    other = lax.ppermute(mine, "grp", swap)
    moved = lax.all_to_all(amplitudes[0].reshape(groups, octet, cap), "grp", 0, 0, tiled=True)
    packed = pl.pallas_call(
        functools.partial(pack_amplitudes, groups, share),
        out_shape=jax.ShapeDtypeStruct((2 * groups, octet, wide // 2), jnp.bfloat16),
        in_specs=[SMEM, VMEM],
        out_specs=VMEM,
        scratch_shapes=small,
        compiler_params=pltpu.CompilerParams(vmem_limit_bytes=8 * 2**20),
    )(both, moved)
    pair = lax.all_to_all(packed, ("grp", "row"), 0, 0, axis_index_groups=pairs, tiled=True)

    tiles = jax.ShapeDtypeStruct((wide, cols), jnp.bfloat16)
    scratch = small + [pltpu.SemaphoreType.DMA((share,))]
    sent = pl.pallas_call(
        functools.partial(send_tiles, groups, share),
        out_shape=tiles,
        in_specs=[SMEM, ANY, ANY],
        out_specs=VMEM,
        scratch_shapes=scratch,
        compiler_params=limit,
    )(both, mine, other)
    pair, sent = barrier((pair, sent))
    got = lax.ppermute(sent, "grp", apart)
    def half_of(block):
        h = block.shape[1] // 2
        return jnp.where(core == 0, block[:, :h], block[:, h:])

    def z_step(block):
        return lax.ppermute(block, ("grp", "col"), along)

    def y_step(block):
        return lax.ppermute(block, ("grp", "row"), beside)

    pair_too = lax.ppermute(pair, "grp", swap)
    block = half_of(jnp.stack([pair, pair_too]))
    order = [block]
    block, near = barrier((jnp.stack([z_step(pair), z_step(pair_too)]), y_step(block)))
    order += [near]
    for s in range(1, nz // 2 - 1):
        order += [block]
        block, near = barrier((z_step(block), y_step(block)))
        if s == nz // 2 - 3:
            block, near, got = barrier((block, near, got))
        order += [near]
    theirs = [lax.ppermute(part, "grp", swap) for part in jnp.split(got, 2)]
    end = z_step(half_of(block))
    order += [block, y_step(block), end, y_step(end)]

    held = pl.pallas_call(
        functools.partial(join_tiles, groups, share),
        out_shape=tiles,
        in_specs=[SMEM] + [ANY] * (3 + len(theirs)),
        out_specs=VMEM,
        scratch_shapes=scratch,
        compiler_params=limit,
    )(both, mine, other, got, *theirs)

    def sums(parts):
        n = sum(part.shape[1] for part in parts) * octet
        return pl.pallas_call(
            functools.partial(multiply, ny),
            out_shape=jax.ShapeDtypeStruct((ny, n // 4, cols), jnp.float32),
            in_specs=[VMEM] * (len(parts) + 1),
            out_specs=VMEM,
            scratch_shapes=[pltpu.VMEM((n, wide), jnp.bfloat16)],
            compiler_params=limit,
        )(*parts, held)

    early, late = sums(order[:6]), order[6:]
    a, b = near_chips(early, up, down)
    *late, a, b = barrier((*late, a, b))
    late = sums(late)
    h, n = early.shape[1] // 2, late.shape[1]
    c = lax.ppermute(late[2], "grp", opposite)
    a2 = lax.ppermute(jnp.concatenate([late[1], early[1, :h] + a[:h]]), "grp", up)
    b2 = lax.ppermute(jnp.concatenate([late[3], early[3, h:] + b[:h]]), "grp", down)
    early = early[0] + jnp.concatenate([a2[n:], a[h:]]) + jnp.concatenate([b[h:], b2[n:]])
    done = jnp.concatenate([early, late[0] + a2[:n] + b2[:n] + c])
    return pl.pallas_call(
        functools.partial(finish, nz, rows),
        out_shape=jax.ShapeDtypeStruct((nz // 2 * rows, cols), jnp.float32),
        in_specs=[VMEM, VMEM],
        out_specs=VMEM,
        compiler_params=pltpu.CompilerParams(vmem_limit_bytes=8 * 2**20),
    )(done, lax.ppermute(done, "grp", swap))


def solution(mesh):
    in_specs = (P("grp", ("row", "col"), None), P("grp", None, ("row", "col")), P(), P())
    out_specs = P("grp", ("row", "col"))
    return jax.shard_map(body, mesh=mesh, in_specs=in_specs, out_specs=out_specs, check_vma=False)
```

```python
import functools

import jax
import jax.numpy as jnp
from jax import lax
from jax.experimental import pallas as pl
from jax.experimental.pallas import tpu as pltpu
from jax.sharding import PartitionSpec as P

TP = 128
ANY = pl.BlockSpec(memory_space=pl.ANY)
SMEM = pl.BlockSpec(memory_space=pltpu.SMEM)
VMEM = pl.BlockSpec(memory_space=pltpu.VMEM)


def balance(both_ref, held_ref, block_ref, groups):
    for b in range(groups):
        held_ref[both_ref[1, b]] = both_ref[0, b]
        block_ref[both_ref[1, b]] = b
    chips = groups // 2
    held = [held_ref[s] for s in range(groups)]
    total = [held[2 * x] + held[2 * x + 1] for x in range(chips)]
    share = 0
    for x in range(chips):
        share = share + total[x]
    share = share // chips
    running, prefix = 0, []
    for x in range(chips):
        running = running + total[x] - share
        prefix.append(running)
    high = functools.reduce(jnp.maximum, prefix)
    low = functools.reduce(jnp.minimum, prefix)
    middle = lax.shift_right_arithmetic(high + low, jnp.int32(1))
    flow = [p - middle for p in prefix]
    right = [jnp.maximum(flow[x], 0) for x in range(chips)]
    left = [jnp.maximum(-flow[(x - 1) % chips], 0) for x in range(chips)]
    return held, total, right, left


def pick(values, index):
    out = values[0]
    for i in range(1, len(values)):
        out = jnp.where(index == i, values[i], out)
    return out


def runs_of(x, total, right, left, chips):
    if isinstance(x, int):
        xl, xr = (x - 1) % chips, (x + 1) % chips
        n, m, t, k = right[xl], left[xr], total[xl], left[x]
    else:
        xl, xr = lax.rem(x + chips - 1, chips), lax.rem(x + 1, chips)
        n, m, t, k = pick(right, xl), pick(left, xr), pick(total, xl), pick(left, x)
    return (xl, t - n, n), (xr, 0, m), (x, k, None)


def pack_amplitudes(groups, share, both_ref, src_ref, out_ref, held_ref, block_ref):
    held, total, right, left = balance(both_ref, held_ref, block_ref, groups)
    blocks = [block_ref[s] for s in range(groups)]
    each = share // 2
    for x in range(groups // 2):
        place = 0
        for chip, start, count in runs_of(x, total, right, left, groups // 2):
            if count is None:
                count = share - place
            n0 = jnp.clip(held[2 * chip] - start, 0, count)
            second = jnp.maximum(start - held[2 * chip], 0)
            for block, tile, many in ((blocks[2 * chip], start, n0), (blocks[2 * chip + 1], second, count - n0)):

                def move(i, carry, block=block, tile=tile, place=place):
                    data = src_ref[block, :, pl.ds(pl.multiple_of((tile + i) * TP, TP), TP)]
                    upper = (place + i >= each).astype(jnp.int32)
                    into = pl.ds(pl.multiple_of((place + i - upper * each) * TP, TP), TP)
                    for j in range(2):
                        out_ref[4 * x + 2 * upper + j, :, into] = data
                    return carry

                lax.fori_loop(0, many, move, 0)
                place = place + many


def tile_rows(index):
    return pl.ds(pl.multiple_of(index * TP, TP), TP)


def run_copies(jobs, out_ref, sems):
    for phase in range(2):
        for source, tile, many, place in jobs:

            def move(i, carry, source=source, tile=tile, place=place):
                copy = pltpu.make_async_copy(source.at[tile_rows(tile + i)], out_ref.at[tile_rows(place + i)], sems.at[place + i])
                copy.start() if phase == 0 else copy.wait()
                return carry

            lax.fori_loop(0, many, move, 0)


def own_tiles(border, core, start, count, mine_ref, other_ref, place):
    lower = jnp.clip(border - start, 0, count)
    jobs = []
    for upper, tile, many, at in ((0, start, lower, place), (1, jnp.maximum(start - border, 0), count - lower, place + lower)):
        jobs.append((mine_ref, tile, jnp.where(core == upper, many, 0), at))
        jobs.append((other_ref, tile, jnp.where(core != upper, many, 0), at))
    return jobs


def send_tiles(groups, share, both_ref, mine_ref, other_ref, out_ref, held_ref, block_ref, sems):
    held, total, right, left = balance(both_ref, held_ref, block_ref, groups)
    group = lax.axis_index("grp")
    x, core = lax.div(group, 2), lax.rem(group, 2)
    go_right, go_left = pick(right, x), pick(left, x)
    start = jnp.where(core == 0, pick(total, x) - go_right, 0)
    count = jnp.where(core == 0, go_right, go_left)
    run_copies(own_tiles(pick(held[0::2], x), core, start, count, mine_ref, other_ref, 0), out_ref, sems)


def join_tiles(groups, share, both_ref, mine_ref, other_ref, got_ref, *refs):
    *their_refs, out_ref, held_ref, block_ref, sems = refs
    held, total, right, left = balance(both_ref, held_ref, block_ref, groups)
    group = lax.axis_index("grp")
    x, core = lax.div(group, 2), lax.rem(group, 2)
    (_, _, n), (_, _, m), (_, start, _) = runs_of(x, total, right, left, groups // 2)
    jobs = [
        (got_ref, 0, jnp.where(core == 0, n, 0), 0),
        (got_ref, 0, jnp.where(core == 0, 0, m), n),
    ]
    each = share // len(their_refs)
    for i, ref in enumerate(their_refs):
        jobs.append((ref, 0, jnp.clip(jnp.where(core == 0, m, n) - i * each, 0, each), jnp.where(core == 0, n, 0) + i * each))
    jobs += own_tiles(pick(held[0::2], x), core, start, share - n - m, mine_ref, other_ref, n + m)
    run_copies(jobs, out_ref, sems)


def multiply(ny, *refs):
    refs, (b_ref, out_ref, a_ref) = refs[:-3], refs[-3:]
    group, y = lax.axis_index("grp"), lax.axis_index("row")
    x, core = lax.div(group, 2), lax.rem(group, 2)
    at = 0
    for ref in refs:
        _, n, octet, each = ref.shape
        for k in range(2):
            a_ref[at : at + n * octet, k * each : (k + 1) * each] = ref[k].reshape(n * octet, each)
        at += n * octet
    first = pl.ds(pl.multiple_of(core * each, each), each)
    last = pl.ds(pl.multiple_of((1 - core) * each, each), each)
    out = jnp.dot(a_ref[:, :each], b_ref[first, :], preferred_element_type=jnp.float32)
    out += jnp.dot(a_ref[:, each:], b_ref[last, :], preferred_element_type=jnp.float32)
    at = row = 0
    for i, ref in enumerate(refs):
        _, n, octet, _ = ref.shape
        for j in range(2):
            d = lax.rem(lax.rem(y + i % 2, 2) + 2 * j - x + ny, ny)
            for g in range(n // 2):
                start = at + (2 * g + j) * octet
                out_ref[d, row + g * octet : row + (g + 1) * octet, :] = out[start : start + octet]
        at += n * octet
        row += n // 2 * octet if i % 2 else 0


def finish(nz, rows, mine_ref, other_ref, out_ref):
    core, z = lax.rem(lax.axis_index("grp"), 2), lax.axis_index("col")
    h = rows // 2
    last = nz // 2 * rows - h
    for q in range(nz // 2):
        r = lax.rem(core * (nz // 2) + q - z + nz, nz)
        ends = jnp.logical_or(r == 0, r == nz // 2)
        above = r < nz // 2
        step = jnp.where(above, r, nz - r)
        for part in range(2):
            start = jnp.where(r == 0, 0, jnp.where(r == nz // 2, last, h + rows * (step - 1) + part * h))
            holder = jnp.where(ends, part, jnp.where(above, 1, 0))
            rows_in = pl.ds(pl.multiple_of(start, h), h)
            for ref, here in ((mine_ref, holder == core), (other_ref, holder != core)):

                @pl.when(here)
                def _(ref=ref, q=q, part=part, rows_in=rows_in):
                    out_ref[q * rows + part * h : q * rows + (part + 1) * h, :] = ref[rows_in, :]


def body(amplitudes, integrals, block_tiles, assign):
    groups = assign.shape[0]
    _, rows, cap = amplitudes.shape
    cols = integrals.shape[2]
    ny, nz = lax.axis_size("row"), lax.axis_size("col")
    share = 24
    wide = share * TP
    octet = rows // groups
    small = [pltpu.SMEM((groups,), jnp.int32)] * 2
    swap = [(g, g ^ 1) for g in range(groups)]
    up = [(g, (g + 2) % groups) for g in range(groups)]
    down = [(g, (g - 2) % groups) for g in range(groups)]
    opposite = [(g, (g + 4) % groups) for g in range(groups)]
    apart = [(g, (g + 2 - 4 * (g % 2)) % groups) for g in range(groups)]
    along = [(g * nz + z, g * nz + (z + 1 - 2 * (g % 2)) % nz) for g in range(groups) for z in range(nz)]
    beside = [(g * ny + y, g * ny + (y - 1 + 2 * (g % 2)) % ny) for g in range(groups) for y in range(ny)]
    pairs = [[g * ny + y for g in range(groups) for y in (p, p + 2)] for p in range(2)]
    limit = pltpu.CompilerParams(vmem_limit_bytes=32 * 2**20)
    core = lax.rem(lax.axis_index("grp"), 2)
    barrier = lax.optimization_barrier

    both = jnp.stack([block_tiles, assign])
    mine = integrals[0]
    other = lax.ppermute(mine, "grp", swap)
    moved = lax.all_to_all(amplitudes[0].reshape(groups, octet, cap), "grp", 0, 0, tiled=True)
    packed = pl.pallas_call(
        functools.partial(pack_amplitudes, groups, share),
        out_shape=jax.ShapeDtypeStruct((2 * groups, octet, wide // 2), jnp.bfloat16),
        in_specs=[SMEM, VMEM],
        out_specs=VMEM,
        scratch_shapes=small,
        compiler_params=pltpu.CompilerParams(vmem_limit_bytes=8 * 2**20),
    )(both, moved)
    pair = lax.all_to_all(packed, ("grp", "row"), 0, 0, axis_index_groups=pairs, tiled=True)

    tiles = jax.ShapeDtypeStruct((wide, cols), jnp.bfloat16)
    scratch = small + [pltpu.SemaphoreType.DMA((share,))]
    sent = pl.pallas_call(
        functools.partial(send_tiles, groups, share),
        out_shape=tiles,
        in_specs=[SMEM, ANY, ANY],
        out_specs=VMEM,
        scratch_shapes=scratch,
        compiler_params=limit,
    )(both, mine, other)
    pair, sent = barrier((pair, sent))
    got = lax.ppermute(sent, "grp", apart)
    def half_of(block):
        h = block.shape[1] // 2
        return jnp.where(core == 0, block[:, :h], block[:, h:])

    def z_step(block):
        return lax.ppermute(block, ("grp", "col"), along)

    def y_step(block):
        return lax.ppermute(block, ("grp", "row"), beside)

    pair_too = lax.ppermute(pair, "grp", swap)
    block = half_of(jnp.stack([pair, pair_too]))
    order = [block]
    block, near = barrier((jnp.stack([z_step(pair), z_step(pair_too)]), y_step(block)))
    order += [near]
    for s in range(1, nz // 2 - 1):
        order += [block]
        block, near = z_step(block), y_step(block)
        if s < nz // 2 - 2:
            block, near = barrier((block, near))
        if s == nz // 2 - 3:
            block, near, got = barrier((block, near, got))
        order += [near]
    theirs = [lax.ppermute(part, "grp", swap) for part in jnp.split(got, 2)]
    end = z_step(half_of(block))
    order += [block, y_step(block), end, y_step(end)]

    held = pl.pallas_call(
        functools.partial(join_tiles, groups, share),
        out_shape=tiles,
        in_specs=[SMEM] + [ANY] * (3 + len(theirs)),
        out_specs=VMEM,
        scratch_shapes=scratch,
        compiler_params=limit,
    )(both, mine, other, got, *theirs)

    def sums(parts):
        n = sum(part.shape[1] for part in parts) * octet
        return pl.pallas_call(
            functools.partial(multiply, ny),
            out_shape=jax.ShapeDtypeStruct((ny, n // 4, cols), jnp.float32),
            in_specs=[VMEM] * (len(parts) + 1),
            out_specs=VMEM,
            scratch_shapes=[pltpu.VMEM((n, wide), jnp.bfloat16)],
            compiler_params=limit,
        )(*parts, held)

    def to_chips(p):
        return [lax.ppermute(p[d], "grp", way) for d, way in ((2, opposite), (1, up), (3, down))]

    early, late = sums(order[:6]), order[6:]
    arrived = to_chips(early)
    *late, arrived[1], arrived[2] = barrier((*late, *arrived[1:]))
    late = sums(late)
    done = jnp.concatenate([sum(arrived, early[0]), sum(to_chips(late), late[0])])
    return pl.pallas_call(
        functools.partial(finish, nz, rows),
        out_shape=jax.ShapeDtypeStruct((nz // 2 * rows, cols), jnp.float32),
        in_specs=[VMEM, VMEM],
        out_specs=VMEM,
        compiler_params=pltpu.CompilerParams(vmem_limit_bytes=8 * 2**20),
    )(done, lax.ppermute(done, "grp", swap))


def solution(mesh):
    in_specs = (P("grp", ("row", "col"), None), P("grp", None, ("row", "col")), P(), P())
    out_specs = P("grp", ("row", "col"))
    return jax.shard_map(body, mesh=mesh, in_specs=in_specs, out_specs=out_specs, check_vma=False)
```

```python
import functools

import jax
import jax.numpy as jnp
from jax import lax
from jax.experimental import pallas as pl
from jax.experimental.pallas import tpu as pltpu
from jax.sharding import PartitionSpec as P

TP = 128
ANY = pl.BlockSpec(memory_space=pl.ANY)
SMEM = pl.BlockSpec(memory_space=pltpu.SMEM)
VMEM = pl.BlockSpec(memory_space=pltpu.VMEM)


def balance(both_ref, held_ref, block_ref, groups):
    for b in range(groups):
        held_ref[both_ref[1, b]] = both_ref[0, b]
        block_ref[both_ref[1, b]] = b
    chips = groups // 2
    held = [held_ref[s] for s in range(groups)]
    total = [held[2 * x] + held[2 * x + 1] for x in range(chips)]
    share = 0
    for x in range(chips):
        share = share + total[x]
    share = share // chips
    running, prefix = 0, []
    for x in range(chips):
        running = running + total[x] - share
        prefix.append(running)
    high = functools.reduce(jnp.maximum, prefix)
    low = functools.reduce(jnp.minimum, prefix)
    middle = lax.shift_right_arithmetic(high + low, jnp.int32(1))
    flow = [p - middle for p in prefix]
    right = [jnp.maximum(flow[x], 0) for x in range(chips)]
    left = [jnp.maximum(-flow[(x - 1) % chips], 0) for x in range(chips)]
    return held, total, right, left


def pick(values, index):
    out = values[0]
    for i in range(1, len(values)):
        out = jnp.where(index == i, values[i], out)
    return out


def runs_of(x, total, right, left, chips):
    if isinstance(x, int):
        xl, xr = (x - 1) % chips, (x + 1) % chips
        n, m, t, k = right[xl], left[xr], total[xl], left[x]
    else:
        xl, xr = lax.rem(x + chips - 1, chips), lax.rem(x + 1, chips)
        n, m, t, k = pick(right, xl), pick(left, xr), pick(total, xl), pick(left, x)
    return (xl, t - n, n), (xr, 0, m), (x, k, None)


def pack_amplitudes(groups, share, both_ref, src_ref, out_ref, held_ref, block_ref):
    held, total, right, left = balance(both_ref, held_ref, block_ref, groups)
    blocks = [block_ref[s] for s in range(groups)]
    each = share // 2
    for x in range(groups // 2):
        place = 0
        for chip, start, count in runs_of(x, total, right, left, groups // 2):
            if count is None:
                count = share - place
            n0 = jnp.clip(held[2 * chip] - start, 0, count)
            second = jnp.maximum(start - held[2 * chip], 0)
            for block, tile, many in ((blocks[2 * chip], start, n0), (blocks[2 * chip + 1], second, count - n0)):

                def move(i, carry, block=block, tile=tile, place=place):
                    data = src_ref[block, :, pl.ds(pl.multiple_of((tile + i) * TP, TP), TP)]
                    upper = (place + i >= each).astype(jnp.int32)
                    into = pl.ds(pl.multiple_of((place + i - upper * each) * TP, TP), TP)
                    for j in range(2):
                        out_ref[4 * x + 2 * upper + j, :, into] = data
                    return carry

                lax.fori_loop(0, many, move, 0)
                place = place + many


def tile_rows(index):
    return pl.ds(pl.multiple_of(index * TP, TP), TP)


def run_copies(jobs, out_ref, sems):
    for phase in range(2):
        for source, tile, many, place in jobs:

            def move(i, carry, source=source, tile=tile, place=place):
                copy = pltpu.make_async_copy(source.at[tile_rows(tile + i)], out_ref.at[tile_rows(place + i)], sems.at[place + i])
                copy.start() if phase == 0 else copy.wait()
                return carry

            lax.fori_loop(0, many, move, 0)


def own_tiles(border, core, start, count, mine_ref, other_ref, place):
    lower = jnp.clip(border - start, 0, count)
    jobs = []
    for upper, tile, many, at in ((0, start, lower, place), (1, jnp.maximum(start - border, 0), count - lower, place + lower)):
        jobs.append((mine_ref, tile, jnp.where(core == upper, many, 0), at))
        jobs.append((other_ref, tile, jnp.where(core != upper, many, 0), at))
    return jobs


def send_tiles(groups, share, both_ref, mine_ref, other_ref, out_ref, held_ref, block_ref, sems):
    held, total, right, left = balance(both_ref, held_ref, block_ref, groups)
    group = lax.axis_index("grp")
    x, core = lax.div(group, 2), lax.rem(group, 2)
    go_right, go_left = pick(right, x), pick(left, x)
    start = jnp.where(core == 0, pick(total, x) - go_right, 0)
    count = jnp.where(core == 0, go_right, go_left)
    run_copies(own_tiles(pick(held[0::2], x), core, start, count, mine_ref, other_ref, 0), out_ref, sems)


def join_tiles(groups, share, both_ref, mine_ref, other_ref, got_ref, *refs):
    *their_refs, out_ref, held_ref, block_ref, sems = refs
    held, total, right, left = balance(both_ref, held_ref, block_ref, groups)
    group = lax.axis_index("grp")
    x, core = lax.div(group, 2), lax.rem(group, 2)
    (_, _, n), (_, _, m), (_, start, _) = runs_of(x, total, right, left, groups // 2)
    jobs = [
        (got_ref, 0, jnp.where(core == 0, n, 0), 0),
        (got_ref, 0, jnp.where(core == 0, 0, m), n),
    ]
    each = share // len(their_refs)
    for i, ref in enumerate(their_refs):
        jobs.append((ref, 0, jnp.clip(jnp.where(core == 0, m, n) - i * each, 0, each), jnp.where(core == 0, n, 0) + i * each))
    jobs += own_tiles(pick(held[0::2], x), core, start, share - n - m, mine_ref, other_ref, n + m)
    run_copies(jobs, out_ref, sems)


def multiply(ny, *refs):
    refs, (b_ref, out_ref, a_ref) = refs[:-3], refs[-3:]
    group, y = lax.axis_index("grp"), lax.axis_index("row")
    x, core = lax.div(group, 2), lax.rem(group, 2)
    at = 0
    for ref in refs:
        _, n, octet, each = ref.shape
        for k in range(2):
            a_ref[at : at + n * octet, k * each : (k + 1) * each] = ref[k].reshape(n * octet, each)
        at += n * octet
    first = pl.ds(pl.multiple_of(core * each, each), each)
    last = pl.ds(pl.multiple_of((1 - core) * each, each), each)
    out = jnp.dot(a_ref[:, :each], b_ref[first, :], preferred_element_type=jnp.float32)
    out += jnp.dot(a_ref[:, each:], b_ref[last, :], preferred_element_type=jnp.float32)
    at = row = 0
    for i, ref in enumerate(refs):
        _, n, octet, _ = ref.shape
        for j in range(2):
            d = lax.rem(lax.rem(y + i % 2, 2) + 2 * j - x + ny, ny)
            for g in range(n // 2):
                start = at + (2 * g + j) * octet
                out_ref[d, row + g * octet : row + (g + 1) * octet, :] = out[start : start + octet]
        at += n * octet
        row += n // 2 * octet if i % 2 else 0


def finish(nz, rows, mine_ref, other_ref, out_ref):
    core, z = lax.rem(lax.axis_index("grp"), 2), lax.axis_index("col")
    h = rows // 2
    last = nz // 2 * rows - h
    for q in range(nz // 2):
        r = lax.rem(core * (nz // 2) + q - z + nz, nz)
        ends = jnp.logical_or(r == 0, r == nz // 2)
        above = r < nz // 2
        step = jnp.where(above, r, nz - r)
        for part in range(2):
            start = jnp.where(r == 0, 0, jnp.where(r == nz // 2, last, h + rows * (step - 1) + part * h))
            holder = jnp.where(ends, part, jnp.where(above, 1, 0))
            rows_in = pl.ds(pl.multiple_of(start, h), h)
            for ref, here in ((mine_ref, holder == core), (other_ref, holder != core)):

                @pl.when(here)
                def _(ref=ref, q=q, part=part, rows_in=rows_in):
                    out_ref[q * rows + part * h : q * rows + (part + 1) * h, :] = ref[rows_in, :]


def near_chips(p, up, down):
    h = p.shape[1] // 2
    a = lax.ppermute(jnp.concatenate([p[2, :h], p[1, h:]]), "grp", up)
    return a, lax.ppermute(jnp.concatenate([p[2, h:], p[3, :h]]), "grp", down)


def body(amplitudes, integrals, block_tiles, assign):
    groups = assign.shape[0]
    _, rows, cap = amplitudes.shape
    cols = integrals.shape[2]
    ny, nz = lax.axis_size("row"), lax.axis_size("col")
    share = 24
    wide = share * TP
    octet = rows // groups
    small = [pltpu.SMEM((groups,), jnp.int32)] * 2
    swap = [(g, g ^ 1) for g in range(groups)]
    up = [(g, (g + 2) % groups) for g in range(groups)]
    down = [(g, (g - 2) % groups) for g in range(groups)]
    opposite = [(g, (g + 4) % groups) for g in range(groups)]
    apart = [(g, (g + 2 - 4 * (g % 2)) % groups) for g in range(groups)]
    along = [(g * nz + z, g * nz + (z + 1 - 2 * (g % 2)) % nz) for g in range(groups) for z in range(nz)]
    beside = [(g * ny + y, g * ny + (y - 1 + 2 * (g % 2)) % ny) for g in range(groups) for y in range(ny)]
    pairs = [[g * ny + y for g in range(groups) for y in (p, p + 2)] for p in range(2)]
    limit = pltpu.CompilerParams(vmem_limit_bytes=32 * 2**20)
    core = lax.rem(lax.axis_index("grp"), 2)
    barrier = lax.optimization_barrier

    both = jnp.stack([block_tiles, assign])
    mine = integrals[0]
    other = lax.ppermute(mine, "grp", swap)
    moved = lax.all_to_all(amplitudes[0].reshape(groups, octet, cap), "grp", 0, 0, tiled=True)
    packed = pl.pallas_call(
        functools.partial(pack_amplitudes, groups, share),
        out_shape=jax.ShapeDtypeStruct((2 * groups, octet, wide // 2), jnp.bfloat16),
        in_specs=[SMEM, VMEM],
        out_specs=VMEM,
        scratch_shapes=small,
        compiler_params=pltpu.CompilerParams(vmem_limit_bytes=8 * 2**20),
    )(both, moved)
    pair = lax.all_to_all(packed, ("grp", "row"), 0, 0, axis_index_groups=pairs, tiled=True)

    tiles = jax.ShapeDtypeStruct((wide, cols), jnp.bfloat16)
    scratch = small + [pltpu.SemaphoreType.DMA((share,))]
    sent = pl.pallas_call(
        functools.partial(send_tiles, groups, share),
        out_shape=tiles,
        in_specs=[SMEM, ANY, ANY],
        out_specs=VMEM,
        scratch_shapes=scratch,
        compiler_params=limit,
    )(both, mine, other)
    pair, sent = barrier((pair, sent))
    got = lax.ppermute(sent, "grp", apart)
    def half_of(block):
        h = block.shape[1] // 2
        return jnp.where(core == 0, block[:, :h], block[:, h:])

    def z_step(block):
        return lax.ppermute(block, ("grp", "col"), along)

    def y_step(block):
        return lax.ppermute(block, ("grp", "row"), beside)

    pair_too = lax.ppermute(pair, "grp", swap)
    block = half_of(jnp.stack([pair, pair_too]))
    order = [block]
    block, near = barrier((jnp.stack([z_step(pair), z_step(pair_too)]), y_step(block)))
    order += [near]
    for s in range(1, nz // 2 - 1):
        order += [block]
        block, near = z_step(block), y_step(block)
        if s < nz // 2 - 2:
            block, near = barrier((block, near))
        if s == nz // 2 - 3:
            block, near, got = barrier((block, near, got))
        order += [near]
    theirs = [lax.ppermute(part, "grp", swap) for part in jnp.split(got, 2)]
    end = z_step(half_of(block))
    order += [block, y_step(block), end, y_step(end)]

    held = pl.pallas_call(
        functools.partial(join_tiles, groups, share),
        out_shape=tiles,
        in_specs=[SMEM] + [ANY] * (3 + len(theirs)),
        out_specs=VMEM,
        scratch_shapes=scratch,
        compiler_params=limit,
    )(both, mine, other, got, *theirs)

    def sums(parts):
        n = sum(part.shape[1] for part in parts) * octet
        return pl.pallas_call(
            functools.partial(multiply, ny),
            out_shape=jax.ShapeDtypeStruct((ny, n // 4, cols), jnp.float32),
            in_specs=[VMEM] * (len(parts) + 1),
            out_specs=VMEM,
            scratch_shapes=[pltpu.VMEM((n, wide), jnp.bfloat16)],
            compiler_params=limit,
        )(*parts, held)

    early, late = sums(order[:6]), order[6:]
    a, b = near_chips(early, up, down)
    *late, a, b = barrier((*late, a, b))
    late = sums(late)
    h, n = early.shape[1] // 2, late.shape[1]
    c = lax.ppermute(late[2], "grp", opposite)
    a2 = lax.ppermute(jnp.concatenate([late[1], early[1, :h] + a[:h]]), "grp", up)
    b2 = lax.ppermute(jnp.concatenate([late[3], early[3, h:] + b[:h]]), "grp", down)
    early = early[0] + jnp.concatenate([a2[n:], a[h:]]) + jnp.concatenate([b[h:], b2[n:]])
    done = jnp.concatenate([early, late[0] + a2[:n] + b2[:n] + c])
    return pl.pallas_call(
        functools.partial(finish, nz, rows),
        out_shape=jax.ShapeDtypeStruct((nz // 2 * rows, cols), jnp.float32),
        in_specs=[VMEM, VMEM],
        out_specs=VMEM,
        compiler_params=pltpu.CompilerParams(vmem_limit_bytes=8 * 2**20),
    )(done, lax.ppermute(done, "grp", swap))


def solution(mesh):
    in_specs = (P("grp", ("row", "col"), None), P("grp", None, ("row", "col")), P(), P())
    out_specs = P("grp", ("row", "col"))
    return jax.shard_map(body, mesh=mesh, in_specs=in_specs, out_specs=out_specs, check_vma=False)
```

```python
import functools

import jax
import jax.numpy as jnp
from jax import lax
from jax.experimental import pallas as pl
from jax.experimental.pallas import tpu as pltpu
from jax.sharding import PartitionSpec as P

TP = 128
ANY = pl.BlockSpec(memory_space=pl.ANY)
SMEM = pl.BlockSpec(memory_space=pltpu.SMEM)
VMEM = pl.BlockSpec(memory_space=pltpu.VMEM)


def balance(both_ref, held_ref, block_ref, groups):
    for b in range(groups):
        held_ref[both_ref[1, b]] = both_ref[0, b]
        block_ref[both_ref[1, b]] = b
    chips = groups // 2
    held = [held_ref[s] for s in range(groups)]
    total = [held[2 * x] + held[2 * x + 1] for x in range(chips)]
    share = 0
    for x in range(chips):
        share = share + total[x]
    share = share // chips
    running, prefix = 0, []
    for x in range(chips):
        running = running + total[x] - share
        prefix.append(running)
    high = functools.reduce(jnp.maximum, prefix)
    low = functools.reduce(jnp.minimum, prefix)
    middle = lax.shift_right_arithmetic(high + low, jnp.int32(1))
    flow = [p - middle for p in prefix]
    right = [jnp.maximum(flow[x], 0) for x in range(chips)]
    left = [jnp.maximum(-flow[(x - 1) % chips], 0) for x in range(chips)]
    return held, total, right, left


def pick(values, index):
    out = values[0]
    for i in range(1, len(values)):
        out = jnp.where(index == i, values[i], out)
    return out


def runs_of(x, total, right, left, chips):
    if isinstance(x, int):
        xl, xr = (x - 1) % chips, (x + 1) % chips
        n, m, t, k = right[xl], left[xr], total[xl], left[x]
    else:
        xl, xr = lax.rem(x + chips - 1, chips), lax.rem(x + 1, chips)
        n, m, t, k = pick(right, xl), pick(left, xr), pick(total, xl), pick(left, x)
    return (xl, t - n, n), (xr, 0, m), (x, k, None)


def list_tiles(groups, share, shift, both_ref, out_ref, held_ref, block_ref):
    held, total, right, left = balance(both_ref, held_ref, block_ref, groups)
    blocks = [block_ref[s] << shift for s in range(groups)]
    for x in range(groups // 2):
        place = x * share
        for chip, start, count in runs_of(x, total, right, left, groups // 2):
            if count is None:
                count = (x + 1) * share - place
            n0 = jnp.clip(held[2 * chip] - start, 0, count)
            second = jnp.maximum(start - held[2 * chip], 0)
            for first, many in ((blocks[2 * chip] + start, n0), (blocks[2 * chip + 1] + second, count - n0)):

                def note(i, carry, first=first, place=place):
                    out_ref[place + i] = first + i
                    return carry

                lax.fori_loop(0, many, note, 0)
                place = place + many


def pack_amplitudes(groups, share, shift, list_ref, src_ref, out_ref, packed_ref, sems):
    each = share // 2
    copies = []
    for x in range(groups // 2):
        for p in range(share):
            entry = list_ref[x * share + p]
            tile = pl.multiple_of((entry & ((1 << shift) - 1)) * TP, TP)
            data = src_ref[lax.shift_right_logical(entry, jnp.int32(shift)), :, pl.ds(tile, TP)]
            at = p % each * TP
            for j in range(2):
                packed_ref[4 * x + p // each * 2 + j, :, at : at + TP] = data
        part = pl.ds(4 * x, 4)
        copies.append(pltpu.make_async_copy(packed_ref.at[part], out_ref.at[part], sems.at[x]))
        copies[-1].start()
    for copy in copies:
        copy.wait()


def tile_rows(index):
    return pl.ds(pl.multiple_of(index * TP, TP), TP)


def run_copies(jobs, sems):
    for phase in range(2):
        for source, tile, many, out_ref, place, sem in jobs:

            def move(i, carry, source=source, tile=tile, out_ref=out_ref, place=place, sem=sem):
                copy = pltpu.make_async_copy(source.at[tile_rows(tile + i)], out_ref.at[tile_rows(place + i)], sems.at[sem + i])
                copy.start() if phase == 0 else copy.wait()
                return carry

            lax.fori_loop(0, many, move, 0)


def own_tiles(border, core, start, count, mine_ref, other_ref, out_ref, place, sem):
    lower = jnp.clip(border - start, 0, count)
    jobs = []
    for upper, tile, many, at in ((0, start, lower, 0), (1, jnp.maximum(start - border, 0), count - lower, lower)):
        jobs.append((mine_ref, tile, jnp.where(core == upper, many, 0), out_ref, place + at, sem + at))
        jobs.append((other_ref, tile, jnp.where(core != upper, many, 0), out_ref, place + at, sem + at))
    return jobs


def send_tiles(groups, share, both_ref, mine_ref, other_ref, *refs):
    *out_refs, held_ref, block_ref, sems = refs
    held, total, right, left = balance(both_ref, held_ref, block_ref, groups)
    group = lax.axis_index("grp")
    x, core = lax.div(group, 2), lax.rem(group, 2)
    go_right, go_left = pick(right, x), pick(left, x)
    start = jnp.where(core == 0, pick(total, x) - go_right, 0)
    count = jnp.where(core == 0, go_right, go_left)
    each = share // len(out_refs)
    jobs = []
    for i, ref in enumerate(out_refs):
        many = jnp.clip(count - i * each, 0, each)
        jobs += own_tiles(pick(held[0::2], x), core, start + i * each, many, mine_ref, other_ref, ref, 0, i * each)
    run_copies(jobs, sems)


def join_tiles(groups, share, both_ref, mine_ref, other_ref, *refs):
    *moved_refs, out_ref, held_ref, block_ref, sems = refs
    held, total, right, left = balance(both_ref, held_ref, block_ref, groups)
    group = lax.axis_index("grp")
    x, core = lax.div(group, 2), lax.rem(group, 2)
    (_, _, n), (_, _, m), (_, start, _) = runs_of(x, total, right, left, groups // 2)
    halves = len(moved_refs) // 2
    each = share // halves
    jobs = []
    for i, ref in enumerate(moved_refs):
        h, below = i % halves, (core == 0) == (i < halves)
        many = jnp.clip(jnp.where(below, n, m) - h * each, 0, each)
        place = jnp.where(below, 0, n) + h * each
        jobs.append((ref, 0, many, out_ref, place, place))
    kept = own_tiles(pick(held[0::2], x), core, start, share - n - m, mine_ref, other_ref, out_ref, n + m, n + m)
    run_copies(jobs + kept, sems)


def multiply(ny, *refs):
    refs, (b_ref, out_ref, a_ref) = refs[:-3], refs[-3:]
    group, y = lax.axis_index("grp"), lax.axis_index("row")
    x, core = lax.div(group, 2), lax.rem(group, 2)
    at = 0
    for ref in refs:
        _, n, octet, each = ref.shape
        for k in range(2):
            a_ref[at : at + n * octet, k * each : (k + 1) * each] = ref[k].reshape(n * octet, each)
        at += n * octet
    first = pl.ds(pl.multiple_of(core * each, each), each)
    last = pl.ds(pl.multiple_of((1 - core) * each, each), each)
    out = jnp.dot(a_ref[:, :each], b_ref[first, :], preferred_element_type=jnp.float32)
    out += jnp.dot(a_ref[:, each:], b_ref[last, :], preferred_element_type=jnp.float32)
    at = row = 0
    for i, ref in enumerate(refs):
        _, n, octet, _ = ref.shape
        for j in range(2):
            d = lax.rem(lax.rem(y + i % 2, 2) + 2 * j - x + ny, ny)
            for g in range(n // 2):
                start = at + (2 * g + j) * octet
                out_ref[d, row + g * octet : row + (g + 1) * octet, :] = out[start : start + octet]
        at += n * octet
        row += n // 2 * octet if i % 2 else 0


def finish(nz, rows, mine_ref, other_ref, out_ref):
    core, z = lax.rem(lax.axis_index("grp"), 2), lax.axis_index("col")
    h = rows // 2
    last = nz // 2 * rows - h
    for q in range(nz // 2):
        r = lax.rem(core * (nz // 2) + q - z + nz, nz)
        ends = jnp.logical_or(r == 0, r == nz // 2)
        above = r < nz // 2
        step = jnp.where(above, r, nz - r)
        for part in range(2):
            start = jnp.where(r == 0, 0, jnp.where(r == nz // 2, last, h + rows * (step - 1) + part * h))
            holder = jnp.where(ends, part, jnp.where(above, 1, 0))
            rows_in = pl.ds(pl.multiple_of(start, h), h)
            for ref, here in ((mine_ref, holder == core), (other_ref, holder != core)):

                @pl.when(here)
                def _(ref=ref, q=q, part=part, rows_in=rows_in):
                    out_ref[q * rows + part * h : q * rows + (part + 1) * h, :] = ref[rows_in, :]


def near_chips(p, up, down):
    h = p.shape[1] // 2
    a = lax.ppermute(jnp.concatenate([p[2, :h], p[1, h:]]), "grp", up)
    return a, lax.ppermute(jnp.concatenate([p[2, h:], p[3, :h]]), "grp", down)


def body(amplitudes, integrals, block_tiles, assign):
    groups = assign.shape[0]
    _, rows, cap = amplitudes.shape
    cols = integrals.shape[2]
    ny, nz = lax.axis_size("row"), lax.axis_size("col")
    share = 24
    wide = share * TP
    octet = rows // groups
    small = [pltpu.SMEM((groups,), jnp.int32)] * 2
    swap = [(g, g ^ 1) for g in range(groups)]
    up = [(g, (g + 2) % groups) for g in range(groups)]
    down = [(g, (g - 2) % groups) for g in range(groups)]
    opposite = [(g, (g + 4) % groups) for g in range(groups)]
    apart = [(g, (g + 2 - 4 * (g % 2)) % groups) for g in range(groups)]
    along = [(g * nz + z, g * nz + (z + 1 - 2 * (g % 2)) % nz) for g in range(groups) for z in range(nz)]
    beside = [(g * ny + y, g * ny + (y - 1 + 2 * (g % 2)) % ny) for g in range(groups) for y in range(ny)]
    pairs = [[g * ny + y for g in range(groups) for y in (p, p + 2)] for p in range(2)]
    limit = pltpu.CompilerParams(vmem_limit_bytes=32 * 2**20)
    core = lax.rem(lax.axis_index("grp"), 2)
    barrier = lax.optimization_barrier

    both = jnp.stack([block_tiles, assign])
    mine = integrals[0]
    other = lax.ppermute(mine, "grp", swap)
    moved = lax.all_to_all(amplitudes[0].reshape(groups, octet, cap), "grp", 0, 0, tiled=True)
    shift = (cap // TP).bit_length()
    little = pltpu.CompilerParams(vmem_limit_bytes=8 * 2**20)
    listed = pl.pallas_call(
        functools.partial(list_tiles, groups, share, shift),
        out_shape=jax.ShapeDtypeStruct((groups // 2 * share,), jnp.int32),
        in_specs=[SMEM],
        out_specs=SMEM,
        scratch_shapes=small,
        compiler_params=little,
    )(both)
    packed = jax.ShapeDtypeStruct((2 * groups, octet, wide // 2), jnp.bfloat16)
    packed = pl.pallas_call(
        functools.partial(pack_amplitudes, groups, share, shift),
        out_shape=packed,
        in_specs=[SMEM, VMEM],
        out_specs=pl.BlockSpec(memory_space=pltpu.HBM),
        scratch_shapes=[pltpu.VMEM(packed.shape, packed.dtype), pltpu.SemaphoreType.DMA((groups // 2,))],
        compiler_params=little,
    )(listed, moved)
    pair = lax.all_to_all(packed, ("grp", "row"), 0, 0, axis_index_groups=pairs, tiled=True)

    tiles = jax.ShapeDtypeStruct((wide, cols), jnp.bfloat16)
    half_tiles = jax.ShapeDtypeStruct((wide // 2, cols), jnp.bfloat16)
    scratch = small + [pltpu.SemaphoreType.DMA((share,))]
    sent = pl.pallas_call(
        functools.partial(send_tiles, groups, share),
        out_shape=(half_tiles, half_tiles),
        in_specs=[SMEM, ANY, ANY],
        out_specs=(VMEM, VMEM),
        scratch_shapes=scratch,
        compiler_params=limit,
    )(both, mine, other)
    pair, *sent = barrier((pair, *sent))
    got = [lax.ppermute(part, "grp", apart) for part in sent]
    def half_of(block):
        h = block.shape[1] // 2
        return jnp.where(core == 0, block[:, :h], block[:, h:])

    def z_step(block):
        return lax.ppermute(block, ("grp", "col"), along)

    def y_step(block):
        return lax.ppermute(block, ("grp", "row"), beside)

    pair_too = lax.ppermute(pair, "grp", swap)
    block = half_of(jnp.stack([pair, pair_too]))
    order = [block]
    block, near = barrier((jnp.stack([z_step(pair), z_step(pair_too)]), y_step(block)))
    block, got[0] = barrier((block, got[0]))
    order += [near]
    for s in range(1, nz // 2 - 1):
        order += [block]
        block, near = z_step(block), y_step(block)
        if s < nz // 2 - 2:
            block, near = barrier((block, near))
        if s == nz // 2 - 3:
            block, near, got[1] = barrier((block, near, got[1]))
        order += [near]
    theirs = [lax.ppermute(part, "grp", swap) for part in got]
    end = z_step(half_of(block))
    order += [block, y_step(block)]

    held = pl.pallas_call(
        functools.partial(join_tiles, groups, share),
        out_shape=tiles,
        in_specs=[SMEM] + [ANY] * (2 + len(got) + len(theirs)),
        out_specs=VMEM,
        scratch_shapes=scratch,
        compiler_params=limit,
    )(both, mine, other, *got, *theirs)

    def sums(parts):
        n = sum(part.shape[1] for part in parts) * octet
        return pl.pallas_call(
            functools.partial(multiply, ny),
            out_shape=jax.ShapeDtypeStruct((ny, n // 4, cols), jnp.float32),
            in_specs=[VMEM] * (len(parts) + 1),
            out_specs=VMEM,
            scratch_shapes=[pltpu.VMEM((n, wide), jnp.bfloat16)],
            compiler_params=limit,
        )(*parts, held)

    early = sums(order[:6])
    end, early = barrier((end, early))
    late = order[6:] + [end, y_step(end)]
    a, b = near_chips(early, up, down)
    *late, a, b = barrier((*late, a, b))
    late = sums(late)
    h, n = early.shape[1] // 2, late.shape[1]
    c = lax.ppermute(late[2], "grp", opposite)
    a2 = lax.ppermute(jnp.concatenate([late[1], early[1, :h] + a[:h]]), "grp", up)
    b2 = lax.ppermute(jnp.concatenate([late[3], early[3, h:] + b[:h]]), "grp", down)
    early = early[0] + jnp.concatenate([a2[n:], a[h:]]) + jnp.concatenate([b[h:], b2[n:]])
    done = jnp.concatenate([early, late[0] + a2[:n] + b2[:n] + c])
    return pl.pallas_call(
        functools.partial(finish, nz, rows),
        out_shape=jax.ShapeDtypeStruct((nz // 2 * rows, cols), jnp.float32),
        in_specs=[VMEM, VMEM],
        out_specs=VMEM,
        compiler_params=pltpu.CompilerParams(vmem_limit_bytes=8 * 2**20),
    )(done, lax.ppermute(done, "grp", swap))


def solution(mesh):
    in_specs = (P("grp", ("row", "col"), None), P("grp", None, ("row", "col")), P(), P())
    out_specs = P("grp", ("row", "col"))
    return jax.shard_map(body, mesh=mesh, in_specs=in_specs, out_specs=out_specs, check_vma=False)
```

```python
import functools

import jax
import jax.numpy as jnp
from jax import lax
from jax.experimental import pallas as pl
from jax.experimental.pallas import tpu as pltpu
from jax.sharding import PartitionSpec as P

TP = 128
ANY = pl.BlockSpec(memory_space=pl.ANY)
SMEM = pl.BlockSpec(memory_space=pltpu.SMEM)
VMEM = pl.BlockSpec(memory_space=pltpu.VMEM)


def balance(both_ref, held_ref, block_ref, groups):
    for b in range(groups):
        held_ref[both_ref[1, b]] = both_ref[0, b]
        block_ref[both_ref[1, b]] = b
    chips = groups // 2
    held = [held_ref[s] for s in range(groups)]
    total = [held[2 * x] + held[2 * x + 1] for x in range(chips)]
    share = 0
    for x in range(chips):
        share = share + total[x]
    share = share // chips
    running, prefix = 0, []
    for x in range(chips):
        running = running + total[x] - share
        prefix.append(running)
    high = functools.reduce(jnp.maximum, prefix)
    low = functools.reduce(jnp.minimum, prefix)
    middle = lax.shift_right_arithmetic(high + low, jnp.int32(1))
    flow = [p - middle for p in prefix]
    right = [jnp.maximum(flow[x], 0) for x in range(chips)]
    left = [jnp.maximum(-flow[(x - 1) % chips], 0) for x in range(chips)]
    return held, total, right, left


def pick(values, index):
    out = values[0]
    for i in range(1, len(values)):
        out = jnp.where(index == i, values[i], out)
    return out


def runs_of(x, total, right, left, chips):
    if isinstance(x, int):
        xl, xr = (x - 1) % chips, (x + 1) % chips
        n, m, t, k = right[xl], left[xr], total[xl], left[x]
    else:
        xl, xr = lax.rem(x + chips - 1, chips), lax.rem(x + 1, chips)
        n, m, t, k = pick(right, xl), pick(left, xr), pick(total, xl), pick(left, x)
    return (xl, t - n, n), (xr, 0, m), (x, k, None)


def list_tiles(groups, share, shift, both_ref, out_ref, held_ref, block_ref):
    held, total, right, left = balance(both_ref, held_ref, block_ref, groups)
    blocks = [block_ref[s] << shift for s in range(groups)]
    for x in range(groups // 2):
        place = x * share
        for chip, start, count in runs_of(x, total, right, left, groups // 2):
            if count is None:
                count = (x + 1) * share - place
            n0 = jnp.clip(held[2 * chip] - start, 0, count)
            second = jnp.maximum(start - held[2 * chip], 0)
            for first, many in ((blocks[2 * chip] + start, n0), (blocks[2 * chip + 1] + second, count - n0)):

                def note(i, carry, first=first, place=place):
                    out_ref[place + i] = first + i
                    return carry

                lax.fori_loop(0, many, note, 0)
                place = place + many


def pack_amplitudes(groups, share, shift, list_ref, src_ref, out_ref, packed_ref, sems):
    each = share // 2
    copies = []
    for x in range(groups // 2):
        for p in range(share):
            entry = list_ref[x * share + p]
            tile = pl.multiple_of((entry & ((1 << shift) - 1)) * TP, TP)
            data = src_ref[lax.shift_right_logical(entry, jnp.int32(shift)), :, pl.ds(tile, TP)]
            at = p % each * TP
            for j in range(2):
                packed_ref[4 * x + p // each * 2 + j, :, at : at + TP] = data
        part = pl.ds(4 * x, 4)
        copies.append(pltpu.make_async_copy(packed_ref.at[part], out_ref.at[part], sems.at[x]))
        copies[-1].start()
    for copy in copies:
        copy.wait()


def tile_rows(index):
    return pl.ds(pl.multiple_of(index * TP, TP), TP)


def run_copies(jobs, out_ref, sems):
    for phase in range(2):
        for source, tile, many, place in jobs:

            def move(i, carry, source=source, tile=tile, place=place):
                copy = pltpu.make_async_copy(source.at[tile_rows(tile + i)], out_ref.at[tile_rows(place + i)], sems.at[place + i])
                copy.start() if phase == 0 else copy.wait()
                return carry

            lax.fori_loop(0, many, move, 0)


def own_tiles(border, core, start, count, mine_ref, other_ref, place):
    lower = jnp.clip(border - start, 0, count)
    jobs = []
    for upper, tile, many, at in ((0, start, lower, place), (1, jnp.maximum(start - border, 0), count - lower, place + lower)):
        jobs.append((mine_ref, tile, jnp.where(core == upper, many, 0), at))
        jobs.append((other_ref, tile, jnp.where(core != upper, many, 0), at))
    return jobs


def send_tiles(groups, share, both_ref, mine_ref, other_ref, out_ref, held_ref, block_ref, sems):
    held, total, right, left = balance(both_ref, held_ref, block_ref, groups)
    group = lax.axis_index("grp")
    x, core = lax.div(group, 2), lax.rem(group, 2)
    go_right, go_left = pick(right, x), pick(left, x)
    start = jnp.where(core == 0, pick(total, x) - go_right, 0)
    count = jnp.where(core == 0, go_right, go_left)
    run_copies(own_tiles(pick(held[0::2], x), core, start, count, mine_ref, other_ref, 0), out_ref, sems)


def join_tiles(groups, share, both_ref, mine_ref, other_ref, got_ref, *refs):
    *their_refs, out_ref, held_ref, block_ref = refs
    held, total, right, left = balance(both_ref, held_ref, block_ref, groups)
    group = lax.axis_index("grp")
    x, core = lax.div(group, 2), lax.rem(group, 2)
    (_, _, n), (_, _, m), (_, start, _) = runs_of(x, total, right, left, groups // 2)
    jobs = [
        (got_ref, 0, jnp.where(core == 0, n, 0), 0),
        (got_ref, 0, jnp.where(core == 0, 0, m), n),
    ]
    each = share // len(their_refs)
    for i, ref in enumerate(their_refs):
        jobs.append((ref, 0, jnp.clip(jnp.where(core == 0, m, n) - i * each, 0, each), jnp.where(core == 0, n, 0) + i * each))
    jobs += own_tiles(pick(held[0::2], x), core, start, share - n - m, mine_ref, other_ref, n + m)
    for source, tile, many, place in jobs:

        def move(i, carry, source=source, tile=tile, place=place):
            out_ref[tile_rows(place + i), :] = source[tile_rows(tile + i), :]
            return carry

        lax.fori_loop(0, many, move, 0)


def multiply(ny, *refs):
    refs, (b_ref, out_ref, a_ref) = refs[:-3], refs[-3:]
    group, y = lax.axis_index("grp"), lax.axis_index("row")
    x, core = lax.div(group, 2), lax.rem(group, 2)
    at = 0
    for ref in refs:
        _, n, octet, each = ref.shape
        for k in range(2):
            a_ref[at : at + n * octet, k * each : (k + 1) * each] = ref[k].reshape(n * octet, each)
        at += n * octet
    first = pl.ds(pl.multiple_of(core * each, each), each)
    last = pl.ds(pl.multiple_of((1 - core) * each, each), each)
    out = jnp.dot(a_ref[:, :each], b_ref[first, :], preferred_element_type=jnp.float32)
    out += jnp.dot(a_ref[:, each:], b_ref[last, :], preferred_element_type=jnp.float32)
    at = row = 0
    for i, ref in enumerate(refs):
        _, n, octet, _ = ref.shape
        for j in range(2):
            d = lax.rem(lax.rem(y + i % 2, 2) + 2 * j - x + ny, ny)
            for g in range(n // 2):
                start = at + (2 * g + j) * octet
                out_ref[d, row + g * octet : row + (g + 1) * octet, :] = out[start : start + octet]
        at += n * octet
        row += n // 2 * octet if i % 2 else 0


def finish(nz, rows, mine_ref, other_ref, out_ref):
    core, z = lax.rem(lax.axis_index("grp"), 2), lax.axis_index("col")
    h = rows // 2
    last = nz // 2 * rows - h
    for q in range(nz // 2):
        r = lax.rem(core * (nz // 2) + q - z + nz, nz)
        ends = jnp.logical_or(r == 0, r == nz // 2)
        above = r < nz // 2
        step = jnp.where(above, r, nz - r)
        for part in range(2):
            start = jnp.where(r == 0, 0, jnp.where(r == nz // 2, last, h + rows * (step - 1) + part * h))
            holder = jnp.where(ends, part, jnp.where(above, 1, 0))
            rows_in = pl.ds(pl.multiple_of(start, h), h)
            for ref, here in ((mine_ref, holder == core), (other_ref, holder != core)):

                @pl.when(here)
                def _(ref=ref, q=q, part=part, rows_in=rows_in):
                    out_ref[q * rows + part * h : q * rows + (part + 1) * h, :] = ref[rows_in, :]


def near_chips(p, up, down):
    h = p.shape[1] // 2
    a = lax.ppermute(jnp.concatenate([p[2, :h], p[1, h:]]), "grp", up)
    return a, lax.ppermute(jnp.concatenate([p[2, h:], p[3, :h]]), "grp", down)


def body(amplitudes, integrals, block_tiles, assign):
    groups = assign.shape[0]
    _, rows, cap = amplitudes.shape
    cols = integrals.shape[2]
    ny, nz = lax.axis_size("row"), lax.axis_size("col")
    share = 24
    wide = share * TP
    octet = rows // groups
    small = [pltpu.SMEM((groups,), jnp.int32)] * 2
    swap = [(g, g ^ 1) for g in range(groups)]
    up = [(g, (g + 2) % groups) for g in range(groups)]
    down = [(g, (g - 2) % groups) for g in range(groups)]
    opposite = [(g, (g + 4) % groups) for g in range(groups)]
    apart = [(g, (g + 2 - 4 * (g % 2)) % groups) for g in range(groups)]
    along = [(g * nz + z, g * nz + (z + 1 - 2 * (g % 2)) % nz) for g in range(groups) for z in range(nz)]
    beside = [(g * ny + y, g * ny + (y - 1 + 2 * (g % 2)) % ny) for g in range(groups) for y in range(ny)]
    pairs = [[g * ny + y for g in range(groups) for y in (p, p + 2)] for p in range(2)]
    limit = pltpu.CompilerParams(vmem_limit_bytes=32 * 2**20)
    core = lax.rem(lax.axis_index("grp"), 2)
    barrier = lax.optimization_barrier

    both = jnp.stack([block_tiles, assign])
    mine = integrals[0]
    other = lax.ppermute(mine, "grp", swap)
    moved = lax.all_to_all(amplitudes[0].reshape(groups, octet, cap), "grp", 0, 0, tiled=True)
    shift = (cap // TP).bit_length()
    little = pltpu.CompilerParams(vmem_limit_bytes=8 * 2**20)
    listed = pl.pallas_call(
        functools.partial(list_tiles, groups, share, shift),
        out_shape=jax.ShapeDtypeStruct((groups // 2 * share,), jnp.int32),
        in_specs=[SMEM],
        out_specs=SMEM,
        scratch_shapes=small,
        compiler_params=little,
    )(both)
    packed = jax.ShapeDtypeStruct((2 * groups, octet, wide // 2), jnp.bfloat16)
    packed = pl.pallas_call(
        functools.partial(pack_amplitudes, groups, share, shift),
        out_shape=packed,
        in_specs=[SMEM, VMEM],
        out_specs=pl.BlockSpec(memory_space=pltpu.HBM),
        scratch_shapes=[pltpu.VMEM(packed.shape, packed.dtype), pltpu.SemaphoreType.DMA((groups // 2,))],
        compiler_params=little,
    )(listed, moved)
    pair = lax.all_to_all(packed, ("grp", "row"), 0, 0, axis_index_groups=pairs, tiled=True)

    tiles = jax.ShapeDtypeStruct((wide, cols), jnp.bfloat16)
    scratch = small + [pltpu.SemaphoreType.DMA((share,))]
    sent = pl.pallas_call(
        functools.partial(send_tiles, groups, share),
        out_shape=tiles,
        in_specs=[SMEM, ANY, ANY],
        out_specs=VMEM,
        scratch_shapes=scratch,
        compiler_params=limit,
    )(both, mine, other)
    pair, sent = barrier((pair, sent))
    got = lax.ppermute(sent, "grp", apart)
    def half_of(block):
        h = block.shape[1] // 2
        return jnp.where(core == 0, block[:, :h], block[:, h:])

    def z_step(block):
        return lax.ppermute(block, ("grp", "col"), along)

    def y_step(block):
        return lax.ppermute(block, ("grp", "row"), beside)

    pair_too = lax.ppermute(pair, "grp", swap)
    block = half_of(jnp.stack([pair, pair_too]))
    order = [block]
    block, near = barrier((jnp.stack([z_step(pair), z_step(pair_too)]), y_step(block)))
    order += [near]
    for s in range(1, nz // 2 - 1):
        order += [block]
        block, near = z_step(block), y_step(block)
        if s < nz // 2 - 2:
            block, near = barrier((block, near))
        if s == nz // 2 - 3:
            block, near, got = barrier((block, near, got))
        order += [near]
    theirs = [lax.ppermute(part, "grp", swap) for part in jnp.split(got, 2)]
    end = z_step(half_of(block))
    order += [block, y_step(block), end, y_step(end)]

    held = pl.pallas_call(
        functools.partial(join_tiles, groups, share),
        out_shape=tiles,
        in_specs=[SMEM] + [VMEM] * (3 + len(theirs)),
        out_specs=VMEM,
        scratch_shapes=small,
        compiler_params=limit,
    )(both, mine, other, got, *theirs)

    def sums(parts):
        n = sum(part.shape[1] for part in parts) * octet
        return pl.pallas_call(
            functools.partial(multiply, ny),
            out_shape=jax.ShapeDtypeStruct((ny, n // 4, cols), jnp.float32),
            in_specs=[VMEM] * (len(parts) + 1),
            out_specs=VMEM,
            scratch_shapes=[pltpu.VMEM((n, wide), jnp.bfloat16)],
            compiler_params=limit,
        )(*parts, held)

    early, late = sums(order[:6]), order[6:]
    a, b = near_chips(early, up, down)
    *late, a, b = barrier((*late, a, b))
    late = sums(late)
    h, n = early.shape[1] // 2, late.shape[1]
    c = lax.ppermute(late[2], "grp", opposite)
    a2 = lax.ppermute(jnp.concatenate([late[1], early[1, :h] + a[:h]]), "grp", up)
    b2 = lax.ppermute(jnp.concatenate([late[3], early[3, h:] + b[:h]]), "grp", down)
    early = early[0] + jnp.concatenate([a2[n:], a[h:]]) + jnp.concatenate([b[h:], b2[n:]])
    done = jnp.concatenate([early, late[0] + a2[:n] + b2[:n] + c])
    return pl.pallas_call(
        functools.partial(finish, nz, rows),
        out_shape=jax.ShapeDtypeStruct((nz // 2 * rows, cols), jnp.float32),
        in_specs=[VMEM, VMEM],
        out_specs=VMEM,
        compiler_params=pltpu.CompilerParams(vmem_limit_bytes=8 * 2**20),
    )(done, lax.ppermute(done, "grp", swap))


def solution(mesh):
    in_specs = (P("grp", ("row", "col"), None), P("grp", None, ("row", "col")), P(), P())
    out_specs = P("grp", ("row", "col"))
    return jax.shard_map(body, mesh=mesh, in_specs=in_specs, out_specs=out_specs, check_vma=False)
```

```python
import functools

import jax
import jax.numpy as jnp
from jax import lax
from jax.experimental import pallas as pl
from jax.experimental.pallas import tpu as pltpu
from jax.sharding import PartitionSpec as P

TP = 128
ANY = pl.BlockSpec(memory_space=pl.ANY)
SMEM = pl.BlockSpec(memory_space=pltpu.SMEM)
VMEM = pl.BlockSpec(memory_space=pltpu.VMEM)


def balance(both_ref, held_ref, block_ref, groups):
    for b in range(groups):
        held_ref[both_ref[1, b]] = both_ref[0, b]
        block_ref[both_ref[1, b]] = b
    chips = groups // 2
    held = [held_ref[s] for s in range(groups)]
    total = [held[2 * x] + held[2 * x + 1] for x in range(chips)]
    share = 0
    for x in range(chips):
        share = share + total[x]
    share = share // chips
    running, prefix = 0, []
    for x in range(chips):
        running = running + total[x] - share
        prefix.append(running)
    high = functools.reduce(jnp.maximum, prefix)
    low = functools.reduce(jnp.minimum, prefix)
    middle = lax.shift_right_arithmetic(high + low, jnp.int32(1))
    flow = [p - middle for p in prefix]
    right = [jnp.maximum(flow[x], 0) for x in range(chips)]
    left = [jnp.maximum(-flow[(x - 1) % chips], 0) for x in range(chips)]
    return held, total, right, left


def pick(values, index):
    out = values[0]
    for i in range(1, len(values)):
        out = jnp.where(index == i, values[i], out)
    return out


def runs_of(x, total, right, left, chips):
    if isinstance(x, int):
        xl, xr = (x - 1) % chips, (x + 1) % chips
        n, m, t, k = right[xl], left[xr], total[xl], left[x]
    else:
        xl, xr = lax.rem(x + chips - 1, chips), lax.rem(x + 1, chips)
        n, m, t, k = pick(right, xl), pick(left, xr), pick(total, xl), pick(left, x)
    return (xl, t - n, n), (xr, 0, m), (x, k, None)


def list_tiles(groups, share, shift, both_ref, out_ref, held_ref, block_ref):
    held, total, right, left = balance(both_ref, held_ref, block_ref, groups)
    blocks = [block_ref[s] << shift for s in range(groups)]
    for x in range(groups // 2):
        place = x * share
        for chip, start, count in runs_of(x, total, right, left, groups // 2):
            if count is None:
                count = (x + 1) * share - place
            n0 = jnp.clip(held[2 * chip] - start, 0, count)
            second = jnp.maximum(start - held[2 * chip], 0)
            for first, many in ((blocks[2 * chip] + start, n0), (blocks[2 * chip + 1] + second, count - n0)):

                def note(i, carry, first=first, place=place):
                    out_ref[place + i] = first + i
                    return carry

                lax.fori_loop(0, many, note, 0)
                place = place + many


def pack_amplitudes(groups, share, shift, list_ref, src_ref, out_ref, packed_ref, sems):
    each = share // 2
    copies = []
    for x in range(groups // 2):
        for p in range(share):
            entry = list_ref[x * share + p]
            tile = pl.multiple_of((entry & ((1 << shift) - 1)) * TP, TP)
            data = src_ref[lax.shift_right_logical(entry, jnp.int32(shift)), :, pl.ds(tile, TP)]
            at = p % each * TP
            for j in range(2):
                packed_ref[4 * x + p // each * 2 + j, :, at : at + TP] = data
        part = pl.ds(4 * x, 4)
        copies.append(pltpu.make_async_copy(packed_ref.at[part], out_ref.at[part], sems.at[x]))
        copies[-1].start()
    for copy in copies:
        copy.wait()


def tile_rows(index):
    return pl.ds(pl.multiple_of(index * TP, TP), TP)


def run_copies(jobs, out_ref, sems):
    for phase in range(2):
        for source, tile, many, place in jobs:

            def move(i, carry, source=source, tile=tile, place=place):
                copy = pltpu.make_async_copy(source.at[tile_rows(tile + i)], out_ref.at[tile_rows(place + i)], sems.at[place + i])
                copy.start() if phase == 0 else copy.wait()
                return carry

            lax.fori_loop(0, many, move, 0)


def own_tiles(border, core, start, count, mine_ref, other_ref, place):
    lower = jnp.clip(border - start, 0, count)
    jobs = []
    for upper, tile, many, at in ((0, start, lower, place), (1, jnp.maximum(start - border, 0), count - lower, place + lower)):
        jobs.append((mine_ref, tile, jnp.where(core == upper, many, 0), at))
        jobs.append((other_ref, tile, jnp.where(core != upper, many, 0), at))
    return jobs


def send_tiles(groups, share, both_ref, mine_ref, other_ref, out_ref, held_ref, block_ref, sems):
    held, total, right, left = balance(both_ref, held_ref, block_ref, groups)
    group = lax.axis_index("grp")
    x, core = lax.div(group, 2), lax.rem(group, 2)
    go_right, go_left = pick(right, x), pick(left, x)
    start = jnp.where(core == 0, pick(total, x) - go_right, 0)
    count = jnp.where(core == 0, go_right, go_left)
    run_copies(own_tiles(pick(held[0::2], x), core, start, count, mine_ref, other_ref, 0), out_ref, sems)


def join_tiles(groups, share, both_ref, mine_ref, other_ref, got_ref, *refs):
    *their_refs, out_ref, held_ref, block_ref = refs
    held, total, right, left = balance(both_ref, held_ref, block_ref, groups)
    group = lax.axis_index("grp")
    x, core = lax.div(group, 2), lax.rem(group, 2)
    (_, _, n), (_, _, m), (_, start, _) = runs_of(x, total, right, left, groups // 2)
    jobs = [
        (got_ref, 0, jnp.where(core == 0, n, 0), 0),
        (got_ref, 0, jnp.where(core == 0, 0, m), n),
    ]
    each = share // len(their_refs)
    for i, ref in enumerate(their_refs):
        jobs.append((ref, 0, jnp.clip(jnp.where(core == 0, m, n) - i * each, 0, each), jnp.where(core == 0, n, 0) + i * each))
    jobs += own_tiles(pick(held[0::2], x), core, start, share - n - m, mine_ref, other_ref, n + m)
    for source, tile, many, place in jobs:

        def move(i, carry, source=source, tile=tile, place=place):
            out_ref[tile_rows(place + i), :] = source[tile_rows(tile + i), :]
            return carry

        lax.fori_loop(0, many, move, 0)


def multiply(ny, *refs):
    refs, (b_ref, out_ref, a_ref) = refs[:-3], refs[-3:]
    group, y = lax.axis_index("grp"), lax.axis_index("row")
    x, core = lax.div(group, 2), lax.rem(group, 2)
    at = 0
    for ref in refs:
        _, n, octet, each = ref.shape
        for k in range(2):
            a_ref[at : at + n * octet, k * each : (k + 1) * each] = ref[k].reshape(n * octet, each)
        at += n * octet
    first = pl.ds(pl.multiple_of(core * each, each), each)
    last = pl.ds(pl.multiple_of((1 - core) * each, each), each)
    out = jnp.dot(a_ref[:, :each], b_ref[first, :], preferred_element_type=jnp.float32)
    out += jnp.dot(a_ref[:, each:], b_ref[last, :], preferred_element_type=jnp.float32)
    at = row = 0
    for i, ref in enumerate(refs):
        _, n, octet, _ = ref.shape
        for j in range(2):
            d = lax.rem(lax.rem(y + i % 2, 2) + 2 * j - x + ny, ny)
            for g in range(n // 2):
                start = at + (2 * g + j) * octet
                out_ref[d, row + g * octet : row + (g + 1) * octet, :] = out[start : start + octet]
        at += n * octet
        row += n // 2 * octet if i % 2 else 0


def finish(nz, rows, mine_ref, other_ref, out_ref):
    core, z = lax.rem(lax.axis_index("grp"), 2), lax.axis_index("col")
    h = rows // 2
    last = nz // 2 * rows - h
    for q in range(nz // 2):
        r = lax.rem(core * (nz // 2) + q - z + nz, nz)
        ends = jnp.logical_or(r == 0, r == nz // 2)
        above = r < nz // 2
        step = jnp.where(above, r, nz - r)
        for part in range(2):
            start = jnp.where(r == 0, 0, jnp.where(r == nz // 2, last, h + rows * (step - 1) + part * h))
            holder = jnp.where(ends, part, jnp.where(above, 1, 0))
            rows_in = pl.ds(pl.multiple_of(start, h), h)
            for ref, here in ((mine_ref, holder == core), (other_ref, holder != core)):

                @pl.when(here)
                def _(ref=ref, q=q, part=part, rows_in=rows_in):
                    out_ref[q * rows + part * h : q * rows + (part + 1) * h, :] = ref[rows_in, :]


def near_chips(p, up, down):
    h = p.shape[1] // 2
    a = lax.ppermute(jnp.concatenate([p[2, :h], p[1, h:]]), "grp", up)
    return a, lax.ppermute(jnp.concatenate([p[2, h:], p[3, :h]]), "grp", down)


def body(amplitudes, integrals, block_tiles, assign):
    groups = assign.shape[0]
    _, rows, cap = amplitudes.shape
    cols = integrals.shape[2]
    ny, nz = lax.axis_size("row"), lax.axis_size("col")
    share = 24
    wide = share * TP
    octet = rows // groups
    small = [pltpu.SMEM((groups,), jnp.int32)] * 2
    swap = [(g, g ^ 1) for g in range(groups)]
    up = [(g, (g + 2) % groups) for g in range(groups)]
    down = [(g, (g - 2) % groups) for g in range(groups)]
    opposite = [(g, (g + 4) % groups) for g in range(groups)]
    apart = [(g, (g + 2 - 4 * (g % 2)) % groups) for g in range(groups)]
    along = [(g * nz + z, g * nz + (z + 1 - 2 * (g % 2)) % nz) for g in range(groups) for z in range(nz)]
    beside = [(g * ny + y, g * ny + (y - 1 + 2 * (g % 2)) % ny) for g in range(groups) for y in range(ny)]
    pairs = [[g * ny + y for g in range(groups) for y in (p, p + 2)] for p in range(2)]
    limit = pltpu.CompilerParams(vmem_limit_bytes=32 * 2**20)
    core = lax.rem(lax.axis_index("grp"), 2)
    barrier = lax.optimization_barrier

    both = jnp.stack([block_tiles, assign])
    mine = integrals[0]
    other = lax.ppermute(mine, "grp", swap)
    moved = lax.all_to_all(amplitudes[0].reshape(groups, octet, cap), "grp", 0, 0, tiled=True)
    shift = (cap // TP).bit_length()
    little = pltpu.CompilerParams(vmem_limit_bytes=8 * 2**20)
    listed = pl.pallas_call(
        functools.partial(list_tiles, groups, share, shift),
        out_shape=jax.ShapeDtypeStruct((groups // 2 * share,), jnp.int32),
        in_specs=[SMEM],
        out_specs=SMEM,
        scratch_shapes=small,
        compiler_params=little,
    )(both)
    packed = jax.ShapeDtypeStruct((2 * groups, octet, wide // 2), jnp.bfloat16)
    packed = pl.pallas_call(
        functools.partial(pack_amplitudes, groups, share, shift),
        out_shape=packed,
        in_specs=[SMEM, VMEM],
        out_specs=pl.BlockSpec(memory_space=pltpu.HBM),
        scratch_shapes=[pltpu.VMEM(packed.shape, packed.dtype), pltpu.SemaphoreType.DMA((groups // 2,))],
        compiler_params=little,
    )(listed, moved)
    pair = lax.all_to_all(packed, ("grp", "row"), 0, 0, axis_index_groups=pairs, tiled=True)

    tiles = jax.ShapeDtypeStruct((wide, cols), jnp.bfloat16)
    scratch = small + [pltpu.SemaphoreType.DMA((share,))]
    sent = pl.pallas_call(
        functools.partial(send_tiles, groups, share),
        out_shape=tiles,
        in_specs=[SMEM, ANY, ANY],
        out_specs=VMEM,
        scratch_shapes=scratch,
        compiler_params=limit,
    )(both, mine, other)
    pair, sent = barrier((pair, sent))
    got = lax.ppermute(sent, "grp", apart)
    def half_of(block):
        h = block.shape[1] // 2
        return jnp.where(core == 0, block[:, :h], block[:, h:])

    def z_step(block):
        return lax.ppermute(block, ("grp", "col"), along)

    def y_step(block):
        return lax.ppermute(block, ("grp", "row"), beside)

    pair_too = lax.ppermute(pair, "grp", swap)
    block = half_of(jnp.stack([pair, pair_too]))
    order = [block]
    block, near = barrier((jnp.stack([z_step(pair), z_step(pair_too)]), y_step(block)))
    order += [near]
    for s in range(1, nz // 2 - 1):
        order += [block]
        block, near = z_step(block), y_step(block)
        if s < nz // 2 - 2:
            block, near = barrier((block, near))
        if s == nz // 2 - 3:
            block, near, got = barrier((block, near, got))
        order += [near]
    theirs = [lax.ppermute(got, "grp", swap)]
    end = z_step(half_of(block))
    order += [block, y_step(block)]

    held = pl.pallas_call(
        functools.partial(join_tiles, groups, share),
        out_shape=tiles,
        in_specs=[SMEM] + [VMEM] * (3 + len(theirs)),
        out_specs=VMEM,
        scratch_shapes=small,
        compiler_params=limit,
    )(both, mine, other, got, *theirs)

    def sums(parts):
        n = sum(part.shape[1] for part in parts) * octet
        return pl.pallas_call(
            functools.partial(multiply, ny),
            out_shape=jax.ShapeDtypeStruct((ny, n // 4, cols), jnp.float32),
            in_specs=[VMEM] * (len(parts) + 1),
            out_specs=VMEM,
            scratch_shapes=[pltpu.VMEM((n, wide), jnp.bfloat16)],
            compiler_params=limit,
        )(*parts, held)

    early = sums(order[:6])
    end, early = barrier((end, early))
    late = order[6:] + [end, y_step(end)]
    a, b = near_chips(early, up, down)
    *late, a, b = barrier((*late, a, b))
    late = sums(late)
    h, n = early.shape[1] // 2, late.shape[1]
    c = lax.ppermute(late[2], "grp", opposite)
    a2 = lax.ppermute(jnp.concatenate([late[1], early[1, :h] + a[:h]]), "grp", up)
    b2 = lax.ppermute(jnp.concatenate([late[3], early[3, h:] + b[:h]]), "grp", down)
    early = early[0] + jnp.concatenate([a2[n:], a[h:]]) + jnp.concatenate([b[h:], b2[n:]])
    done = jnp.concatenate([early, late[0] + a2[:n] + b2[:n] + c])
    return pl.pallas_call(
        functools.partial(finish, nz, rows),
        out_shape=jax.ShapeDtypeStruct((nz // 2 * rows, cols), jnp.float32),
        in_specs=[VMEM, VMEM],
        out_specs=VMEM,
        compiler_params=pltpu.CompilerParams(vmem_limit_bytes=8 * 2**20),
    )(done, lax.ppermute(done, "grp", swap))


def solution(mesh):
    in_specs = (P("grp", ("row", "col"), None), P("grp", None, ("row", "col")), P(), P())
    out_specs = P("grp", ("row", "col"))
    return jax.shard_map(body, mesh=mesh, in_specs=in_specs, out_specs=out_specs, check_vma=False)
```

```python
import functools

import jax
import jax.numpy as jnp
from jax import lax
from jax.experimental import pallas as pl
from jax.experimental.pallas import tpu as pltpu
from jax.sharding import PartitionSpec as P

TP = 128
ANY = pl.BlockSpec(memory_space=pl.ANY)
SMEM = pl.BlockSpec(memory_space=pltpu.SMEM)
VMEM = pl.BlockSpec(memory_space=pltpu.VMEM)


def balance(both_ref, held_ref, block_ref, groups):
    for b in range(groups):
        held_ref[both_ref[1, b]] = both_ref[0, b]
        block_ref[both_ref[1, b]] = b
    chips = groups // 2
    held = [held_ref[s] for s in range(groups)]
    total = [held[2 * x] + held[2 * x + 1] for x in range(chips)]
    share = 0
    for x in range(chips):
        share = share + total[x]
    share = share // chips
    running, prefix = 0, []
    for x in range(chips):
        running = running + total[x] - share
        prefix.append(running)
    high = functools.reduce(jnp.maximum, prefix)
    low = functools.reduce(jnp.minimum, prefix)
    middle = lax.shift_right_arithmetic(high + low, jnp.int32(1))
    flow = [p - middle for p in prefix]
    right = [jnp.maximum(flow[x], 0) for x in range(chips)]
    left = [jnp.maximum(-flow[(x - 1) % chips], 0) for x in range(chips)]
    return held, total, right, left


def pick(values, index):
    out = values[0]
    for i in range(1, len(values)):
        out = jnp.where(index == i, values[i], out)
    return out


def runs_of(x, total, right, left, chips):
    if isinstance(x, int):
        xl, xr = (x - 1) % chips, (x + 1) % chips
        n, m, t, k = right[xl], left[xr], total[xl], left[x]
    else:
        xl, xr = lax.rem(x + chips - 1, chips), lax.rem(x + 1, chips)
        n, m, t, k = pick(right, xl), pick(left, xr), pick(total, xl), pick(left, x)
    return (xl, t - n, n), (xr, 0, m), (x, k, None)


def list_tiles(groups, share, shift, both_ref, out_ref, held_ref, block_ref):
    held, total, right, left = balance(both_ref, held_ref, block_ref, groups)
    blocks = [block_ref[s] << shift for s in range(groups)]
    for x in range(groups // 2):
        place = x * share
        for chip, start, count in runs_of(x, total, right, left, groups // 2):
            if count is None:
                count = (x + 1) * share - place
            n0 = jnp.clip(held[2 * chip] - start, 0, count)
            second = jnp.maximum(start - held[2 * chip], 0)
            for first, many in ((blocks[2 * chip] + start, n0), (blocks[2 * chip + 1] + second, count - n0)):

                def note(i, carry, first=first, place=place):
                    out_ref[place + i] = first + i
                    return carry

                lax.fori_loop(0, many, note, 0)
                place = place + many


def pack_amplitudes(groups, share, shift, list_ref, src_ref, out_ref, packed_ref, sems):
    each = share // 2
    copies = []
    for x in range(groups // 2):
        for p in range(share):
            entry = list_ref[x * share + p]
            tile = pl.multiple_of((entry & ((1 << shift) - 1)) * TP, TP)
            data = src_ref[lax.shift_right_logical(entry, jnp.int32(shift)), :, pl.ds(tile, TP)]
            at = p % each * TP
            for j in range(2):
                packed_ref[4 * x + p // each * 2 + j, :, at : at + TP] = data
        part = pl.ds(4 * x, 4)
        copies.append(pltpu.make_async_copy(packed_ref.at[part], out_ref.at[part], sems.at[x]))
        copies[-1].start()
    for copy in copies:
        copy.wait()


def tile_rows(index):
    return pl.ds(pl.multiple_of(index * TP, TP), TP)


def run_copies(jobs, out_ref, sems):
    for phase in range(2):
        for source, tile, many, place in jobs:

            def move(i, carry, source=source, tile=tile, place=place):
                copy = pltpu.make_async_copy(source.at[tile_rows(tile + i)], out_ref.at[tile_rows(place + i)], sems.at[place + i])
                copy.start() if phase == 0 else copy.wait()
                return carry

            lax.fori_loop(0, many, move, 0)


def own_tiles(border, core, start, count, mine_ref, other_ref, place):
    lower = jnp.clip(border - start, 0, count)
    jobs = []
    for upper, tile, many, at in ((0, start, lower, place), (1, jnp.maximum(start - border, 0), count - lower, place + lower)):
        jobs.append((mine_ref, tile, jnp.where(core == upper, many, 0), at))
        jobs.append((other_ref, tile, jnp.where(core != upper, many, 0), at))
    return jobs


def send_tiles(groups, share, both_ref, mine_ref, other_ref, out_ref, held_ref, block_ref, sems):
    held, total, right, left = balance(both_ref, held_ref, block_ref, groups)
    group = lax.axis_index("grp")
    x, core = lax.div(group, 2), lax.rem(group, 2)
    go_right, go_left = pick(right, x), pick(left, x)
    start = jnp.where(core == 0, pick(total, x) - go_right, 0)
    count = jnp.where(core == 0, go_right, go_left)
    run_copies(own_tiles(pick(held[0::2], x), core, start, count, mine_ref, other_ref, 0), out_ref, sems)


def join_tiles(groups, share, both_ref, mine_ref, other_ref, got_ref, *refs):
    *their_refs, out_ref, held_ref, block_ref = refs
    held, total, right, left = balance(both_ref, held_ref, block_ref, groups)
    group = lax.axis_index("grp")
    x, core = lax.div(group, 2), lax.rem(group, 2)
    (_, _, n), (_, _, m), (_, start, _) = runs_of(x, total, right, left, groups // 2)
    jobs = [
        (got_ref, 0, jnp.where(core == 0, n, 0), 0),
        (got_ref, 0, jnp.where(core == 0, 0, m), n),
    ]
    each = share // len(their_refs)
    for i, ref in enumerate(their_refs):
        jobs.append((ref, 0, jnp.clip(jnp.where(core == 0, m, n) - i * each, 0, each), jnp.where(core == 0, n, 0) + i * each))
    jobs += own_tiles(pick(held[0::2], x), core, start, share - n - m, mine_ref, other_ref, n + m)
    for source, tile, many, place in jobs:

        def move(i, carry, source=source, tile=tile, place=place):
            out_ref[tile_rows(place + i), :] = source[tile_rows(tile + i), :]
            return carry

        lax.fori_loop(0, many, move, 0)


def multiply(ny, *refs):
    refs, (b_ref, out_ref, a_ref) = refs[:-3], refs[-3:]
    group, y = lax.axis_index("grp"), lax.axis_index("row")
    x, core = lax.div(group, 2), lax.rem(group, 2)
    at = 0
    for ref in refs:
        _, n, octet, each = ref.shape
        for k in range(2):
            a_ref[at : at + n * octet, k * each : (k + 1) * each] = ref[k].reshape(n * octet, each)
        at += n * octet
    first = pl.ds(pl.multiple_of(core * each, each), each)
    last = pl.ds(pl.multiple_of((1 - core) * each, each), each)
    out = jnp.dot(a_ref[:, :each], b_ref[first, :], preferred_element_type=jnp.float32)
    out += jnp.dot(a_ref[:, each:], b_ref[last, :], preferred_element_type=jnp.float32)
    at = row = 0
    for i, ref in enumerate(refs):
        _, n, octet, _ = ref.shape
        for j in range(2):
            d = lax.rem(lax.rem(y + i % 2, 2) + 2 * j - x + ny, ny)
            for g in range(n // 2):
                start = at + (2 * g + j) * octet
                out_ref[d, row + g * octet : row + (g + 1) * octet, :] = out[start : start + octet]
        at += n * octet
        row += n // 2 * octet if i % 2 else 0


def finish(nz, rows, mine_ref, other_ref, out_ref):
    core, z = lax.rem(lax.axis_index("grp"), 2), lax.axis_index("col")
    h = rows // 2
    last = nz // 2 * rows - h
    for q in range(nz // 2):
        r = lax.rem(core * (nz // 2) + q - z + nz, nz)
        ends = jnp.logical_or(r == 0, r == nz // 2)
        above = r < nz // 2
        step = jnp.where(above, r, nz - r)
        for part in range(2):
            start = jnp.where(r == 0, 0, jnp.where(r == nz // 2, last, h + rows * (step - 1) + part * h))
            holder = jnp.where(ends, part, jnp.where(above, 1, 0))
            rows_in = pl.ds(pl.multiple_of(start, h), h)
            for ref, here in ((mine_ref, holder == core), (other_ref, holder != core)):

                @pl.when(here)
                def _(ref=ref, q=q, part=part, rows_in=rows_in):
                    out_ref[q * rows + part * h : q * rows + (part + 1) * h, :] = ref[rows_in, :]


def near_chips(p, up, down):
    h = p.shape[1] // 2
    a = lax.ppermute(jnp.concatenate([p[2, :h], p[1, h:]]), "grp", up)
    return a, lax.ppermute(jnp.concatenate([p[2, h:], p[3, :h]]), "grp", down)


def nothing(*refs):
    pass


def collect(*arrays):
    shapes = tuple(jax.ShapeDtypeStruct(array.shape, array.dtype) for array in arrays)
    return pl.pallas_call(
        nothing,
        out_shape=shapes,
        in_specs=[ANY] * len(arrays),
        out_specs=(ANY,) * len(arrays),
        input_output_aliases={i: i for i in range(len(arrays))},
        cost_estimate=pl.CostEstimate(flops=3000000000, bytes_accessed=0, transcendentals=0),
        compiler_params=pltpu.CompilerParams(vmem_limit_bytes=2**20),
    )(*arrays)


def body(amplitudes, integrals, block_tiles, assign):
    groups = assign.shape[0]
    _, rows, cap = amplitudes.shape
    cols = integrals.shape[2]
    ny, nz = lax.axis_size("row"), lax.axis_size("col")
    share = 24
    wide = share * TP
    octet = rows // groups
    small = [pltpu.SMEM((groups,), jnp.int32)] * 2
    swap = [(g, g ^ 1) for g in range(groups)]
    up = [(g, (g + 2) % groups) for g in range(groups)]
    down = [(g, (g - 2) % groups) for g in range(groups)]
    opposite = [(g, (g + 4) % groups) for g in range(groups)]
    apart = [(g, (g + 2 - 4 * (g % 2)) % groups) for g in range(groups)]
    along = [(g * nz + z, g * nz + (z + 1 - 2 * (g % 2)) % nz) for g in range(groups) for z in range(nz)]
    beside = [(g * ny + y, g * ny + (y - 1 + 2 * (g % 2)) % ny) for g in range(groups) for y in range(ny)]
    pairs = [[g * ny + y for g in range(groups) for y in (p, p + 2)] for p in range(2)]
    limit = pltpu.CompilerParams(vmem_limit_bytes=32 * 2**20)
    core = lax.rem(lax.axis_index("grp"), 2)
    barrier = lax.optimization_barrier

    both = jnp.stack([block_tiles, assign])
    mine = integrals[0]
    other = lax.ppermute(mine, "grp", swap)
    moved = lax.all_to_all(amplitudes[0].reshape(groups, octet, cap), "grp", 0, 0, tiled=True)
    shift = (cap // TP).bit_length()
    little = pltpu.CompilerParams(vmem_limit_bytes=8 * 2**20)
    listed = pl.pallas_call(
        functools.partial(list_tiles, groups, share, shift),
        out_shape=jax.ShapeDtypeStruct((groups // 2 * share,), jnp.int32),
        in_specs=[SMEM],
        out_specs=SMEM,
        scratch_shapes=small,
        compiler_params=little,
    )(both)
    packed = jax.ShapeDtypeStruct((2 * groups, octet, wide // 2), jnp.bfloat16)
    packed = pl.pallas_call(
        functools.partial(pack_amplitudes, groups, share, shift),
        out_shape=packed,
        in_specs=[SMEM, VMEM],
        out_specs=pl.BlockSpec(memory_space=pltpu.HBM),
        scratch_shapes=[pltpu.VMEM(packed.shape, packed.dtype), pltpu.SemaphoreType.DMA((groups // 2,))],
        compiler_params=little,
    )(listed, moved)
    pair = lax.all_to_all(packed, ("grp", "row"), 0, 0, axis_index_groups=pairs, tiled=True)

    tiles = jax.ShapeDtypeStruct((wide, cols), jnp.bfloat16)
    scratch = small + [pltpu.SemaphoreType.DMA((share,))]
    sent = pl.pallas_call(
        functools.partial(send_tiles, groups, share),
        out_shape=tiles,
        in_specs=[SMEM, ANY, ANY],
        out_specs=VMEM,
        scratch_shapes=scratch,
        compiler_params=limit,
    )(both, mine, other)
    pair, sent = barrier((pair, sent))
    got = lax.ppermute(sent, "grp", apart)
    def half_of(block):
        h = block.shape[1] // 2
        return jnp.where(core == 0, block[:, :h], block[:, h:])

    def z_step(block):
        return lax.ppermute(block, ("grp", "col"), along)

    def y_step(block):
        return lax.ppermute(block, ("grp", "row"), beside)

    pair_too = lax.ppermute(pair, "grp", swap)
    block = half_of(jnp.stack([pair, pair_too]))
    order = [block]
    block, near = barrier((jnp.stack([z_step(pair), z_step(pair_too)]), y_step(block)))
    order += [near]
    for s in range(1, nz // 2 - 1):
        order += [block]
        block, near = z_step(block), y_step(block)
        if s < nz // 2 - 2:
            block, near = barrier((block, near))
        if s == nz // 2 - 3:
            block, near, got = barrier((block, near, got))
        order += [near]
    theirs = [lax.ppermute(part, "grp", swap) for part in jnp.split(got, 2)]
    end = z_step(half_of(block))
    order += [block, y_step(block), end, y_step(end)]

    held = pl.pallas_call(
        functools.partial(join_tiles, groups, share),
        out_shape=tiles,
        in_specs=[SMEM] + [VMEM] * (3 + len(theirs)),
        out_specs=VMEM,
        scratch_shapes=small,
        compiler_params=limit,
    )(both, mine, other, got, *theirs)

    def sums(parts):
        n = sum(part.shape[1] for part in parts) * octet
        return pl.pallas_call(
            functools.partial(multiply, ny),
            out_shape=jax.ShapeDtypeStruct((ny, n // 4, cols), jnp.float32),
            in_specs=[VMEM] * (len(parts) + 1),
            out_specs=VMEM,
            scratch_shapes=[pltpu.VMEM((n, wide), jnp.bfloat16)],
            compiler_params=limit,
        )(*parts, held)

    early, late = sums(order[:6]), order[6:]
    a, b = near_chips(early, up, down)
    a, b = collect(a, b)
    *late, a, b = barrier((*late, a, b))
    late = sums(late)
    h, n = early.shape[1] // 2, late.shape[1]
    c = lax.ppermute(late[2], "grp", opposite)
    a2 = lax.ppermute(jnp.concatenate([late[1], early[1, :h] + a[:h]]), "grp", up)
    b2 = lax.ppermute(jnp.concatenate([late[3], early[3, h:] + b[:h]]), "grp", down)
    early = early[0] + jnp.concatenate([a2[n:], a[h:]]) + jnp.concatenate([b[h:], b2[n:]])
    done = jnp.concatenate([early, late[0] + a2[:n] + b2[:n] + c])
    return pl.pallas_call(
        functools.partial(finish, nz, rows),
        out_shape=jax.ShapeDtypeStruct((nz // 2 * rows, cols), jnp.float32),
        in_specs=[VMEM, VMEM],
        out_specs=VMEM,
        compiler_params=pltpu.CompilerParams(vmem_limit_bytes=8 * 2**20),
    )(done, lax.ppermute(done, "grp", swap))


def solution(mesh):
    in_specs = (P("grp", ("row", "col"), None), P("grp", None, ("row", "col")), P(), P())
    out_specs = P("grp", ("row", "col"))
    return jax.shard_map(body, mesh=mesh, in_specs=in_specs, out_specs=out_specs, check_vma=False)
```

```python
import functools

import jax
import jax.numpy as jnp
from jax import lax
from jax.experimental import pallas as pl
from jax.experimental.pallas import tpu as pltpu
from jax.sharding import PartitionSpec as P

TP = 128
ANY = pl.BlockSpec(memory_space=pl.ANY)
SMEM = pl.BlockSpec(memory_space=pltpu.SMEM)
VMEM = pl.BlockSpec(memory_space=pltpu.VMEM)


def balance(both_ref, held_ref, block_ref, groups):
    for b in range(groups):
        held_ref[both_ref[1, b]] = both_ref[0, b]
        block_ref[both_ref[1, b]] = b
    chips = groups // 2
    held = [held_ref[s] for s in range(groups)]
    total = [held[2 * x] + held[2 * x + 1] for x in range(chips)]
    share = 0
    for x in range(chips):
        share = share + total[x]
    share = share // chips
    running, prefix = 0, []
    for x in range(chips):
        running = running + total[x] - share
        prefix.append(running)
    high = functools.reduce(jnp.maximum, prefix)
    low = functools.reduce(jnp.minimum, prefix)
    middle = lax.shift_right_arithmetic(high + low, jnp.int32(1))
    flow = [p - middle for p in prefix]
    right = [jnp.maximum(flow[x], 0) for x in range(chips)]
    left = [jnp.maximum(-flow[(x - 1) % chips], 0) for x in range(chips)]
    return held, total, right, left


def pick(values, index):
    out = values[0]
    for i in range(1, len(values)):
        out = jnp.where(index == i, values[i], out)
    return out


def runs_of(x, total, right, left, chips):
    if isinstance(x, int):
        xl, xr = (x - 1) % chips, (x + 1) % chips
        n, m, t, k = right[xl], left[xr], total[xl], left[x]
    else:
        xl, xr = lax.rem(x + chips - 1, chips), lax.rem(x + 1, chips)
        n, m, t, k = pick(right, xl), pick(left, xr), pick(total, xl), pick(left, x)
    return (xl, t - n, n), (xr, 0, m), (x, k, None)


def list_tiles(groups, share, shift, both_ref, out_ref, held_ref, block_ref):
    held, total, right, left = balance(both_ref, held_ref, block_ref, groups)
    blocks = [block_ref[s] << shift for s in range(groups)]
    for x in range(groups // 2):
        place = x * share
        for chip, start, count in runs_of(x, total, right, left, groups // 2):
            if count is None:
                count = (x + 1) * share - place
            n0 = jnp.clip(held[2 * chip] - start, 0, count)
            second = jnp.maximum(start - held[2 * chip], 0)
            for first, many in ((blocks[2 * chip] + start, n0), (blocks[2 * chip + 1] + second, count - n0)):

                def note(i, carry, first=first, place=place):
                    out_ref[place + i] = first + i
                    return carry

                lax.fori_loop(0, many, note, 0)
                place = place + many


def pack_amplitudes(groups, share, shift, list_ref, src_ref, out_ref, packed_ref, sems):
    each = share // 2
    copies = []
    for x in range(groups // 2):
        for p in range(share):
            entry = list_ref[x * share + p]
            tile = pl.multiple_of((entry & ((1 << shift) - 1)) * TP, TP)
            data = src_ref[lax.shift_right_logical(entry, jnp.int32(shift)), :, pl.ds(tile, TP)]
            at = p % each * TP
            for j in range(2):
                packed_ref[4 * x + p // each * 2 + j, :, at : at + TP] = data
        part = pl.ds(4 * x, 4)
        copies.append(pltpu.make_async_copy(packed_ref.at[part], out_ref.at[part], sems.at[x]))
        copies[-1].start()
    for copy in copies:
        copy.wait()


def tile_rows(index):
    return pl.ds(pl.multiple_of(index * TP, TP), TP)


def run_copies(jobs, out_ref, sems):
    for phase in range(2):
        for source, tile, many, place in jobs:

            def move(i, carry, source=source, tile=tile, place=place):
                copy = pltpu.make_async_copy(source.at[tile_rows(tile + i)], out_ref.at[tile_rows(place + i)], sems.at[place + i])
                copy.start() if phase == 0 else copy.wait()
                return carry

            lax.fori_loop(0, many, move, 0)


def own_tiles(border, core, start, count, mine_ref, other_ref, place):
    lower = jnp.clip(border - start, 0, count)
    jobs = []
    for upper, tile, many, at in ((0, start, lower, place), (1, jnp.maximum(start - border, 0), count - lower, place + lower)):
        jobs.append((mine_ref, tile, jnp.where(core == upper, many, 0), at))
        jobs.append((other_ref, tile, jnp.where(core != upper, many, 0), at))
    return jobs


def send_tiles(groups, share, both_ref, mine_ref, other_ref, out_ref, held_ref, block_ref, sems):
    held, total, right, left = balance(both_ref, held_ref, block_ref, groups)
    group = lax.axis_index("grp")
    x, core = lax.div(group, 2), lax.rem(group, 2)
    go_right, go_left = pick(right, x), pick(left, x)
    start = jnp.where(core == 0, pick(total, x) - go_right, 0)
    count = jnp.where(core == 0, go_right, go_left)
    run_copies(own_tiles(pick(held[0::2], x), core, start, count, mine_ref, other_ref, 0), out_ref, sems)


def join_tiles(groups, share, both_ref, mine_ref, other_ref, got_ref, *refs):
    *their_refs, out_ref, held_ref, block_ref = refs
    held, total, right, left = balance(both_ref, held_ref, block_ref, groups)
    group = lax.axis_index("grp")
    x, core = lax.div(group, 2), lax.rem(group, 2)
    (_, _, n), (_, _, m), (_, start, _) = runs_of(x, total, right, left, groups // 2)
    jobs = [
        (got_ref, 0, jnp.where(core == 0, n, 0), 0),
        (got_ref, 0, jnp.where(core == 0, 0, m), n),
    ]
    each = share // len(their_refs)
    for i, ref in enumerate(their_refs):
        jobs.append((ref, 0, jnp.clip(jnp.where(core == 0, m, n) - i * each, 0, each), jnp.where(core == 0, n, 0) + i * each))
    jobs += own_tiles(pick(held[0::2], x), core, start, share - n - m, mine_ref, other_ref, n + m)
    for source, tile, many, place in jobs:

        def move(i, carry, source=source, tile=tile, place=place):
            out_ref[tile_rows(place + i), :] = source[tile_rows(tile + i), :]
            return carry

        lax.fori_loop(0, many, move, 0)


def multiply(ny, *refs):
    refs, (b_ref, out_ref, a_ref) = refs[:-3], refs[-3:]
    group, y = lax.axis_index("grp"), lax.axis_index("row")
    x, core = lax.div(group, 2), lax.rem(group, 2)
    at = 0
    for ref in refs:
        _, n, octet, each = ref.shape
        for k in range(2):
            a_ref[at : at + n * octet, k * each : (k + 1) * each] = ref[k].reshape(n * octet, each)
        at += n * octet
    first = pl.ds(pl.multiple_of(core * each, each), each)
    last = pl.ds(pl.multiple_of((1 - core) * each, each), each)
    out = jnp.dot(a_ref[:, :each], b_ref[first, :], preferred_element_type=jnp.float32)
    out += jnp.dot(a_ref[:, each:], b_ref[last, :], preferred_element_type=jnp.float32)
    at = row = 0
    for i, ref in enumerate(refs):
        _, n, octet, _ = ref.shape
        for j in range(2):
            d = lax.rem(lax.rem(y + i % 2, 2) + 2 * j - x + ny, ny)
            for g in range(n // 2):
                start = at + (2 * g + j) * octet
                out_ref[d, row + g * octet : row + (g + 1) * octet, :] = out[start : start + octet]
        at += n * octet
        row += n // 2 * octet if i % 2 else 0


def finish(nz, rows, mine_ref, other_ref, out_ref):
    core, z = lax.rem(lax.axis_index("grp"), 2), lax.axis_index("col")
    h = rows // 2
    last = nz // 2 * rows - h
    for q in range(nz // 2):
        r = lax.rem(core * (nz // 2) + q - z + nz, nz)
        ends = jnp.logical_or(r == 0, r == nz // 2)
        above = r < nz // 2
        step = jnp.where(above, r, nz - r)
        for part in range(2):
            start = jnp.where(r == 0, 0, jnp.where(r == nz // 2, last, h + rows * (step - 1) + part * h))
            holder = jnp.where(ends, part, jnp.where(above, 1, 0))
            rows_in = pl.ds(pl.multiple_of(start, h), h)
            for ref, here in ((mine_ref, holder == core), (other_ref, holder != core)):

                @pl.when(here)
                def _(ref=ref, q=q, part=part, rows_in=rows_in):
                    out_ref[q * rows + part * h : q * rows + (part + 1) * h, :] = ref[rows_in, :]


def near_chips(p, up, down):
    h = p.shape[1] // 2
    a = lax.ppermute(jnp.concatenate([p[2, :h], p[1, h:]]), "grp", up)
    return a, lax.ppermute(jnp.concatenate([p[2, h:], p[3, :h]]), "grp", down)


def nothing(*refs):
    pass


def collect(*arrays):
    shapes = tuple(jax.ShapeDtypeStruct(array.shape, array.dtype) for array in arrays)
    return pl.pallas_call(
        nothing,
        out_shape=shapes,
        in_specs=[ANY] * len(arrays),
        out_specs=(ANY,) * len(arrays),
        input_output_aliases={i: i for i in range(len(arrays))},
        cost_estimate=pl.CostEstimate(flops=3000000000, bytes_accessed=0, transcendentals=0),
        compiler_params=pltpu.CompilerParams(vmem_limit_bytes=2**20),
    )(*arrays)


def body(amplitudes, integrals, block_tiles, assign):
    groups = assign.shape[0]
    _, rows, cap = amplitudes.shape
    cols = integrals.shape[2]
    ny, nz = lax.axis_size("row"), lax.axis_size("col")
    share = 24
    wide = share * TP
    octet = rows // groups
    small = [pltpu.SMEM((groups,), jnp.int32)] * 2
    swap = [(g, g ^ 1) for g in range(groups)]
    up = [(g, (g + 2) % groups) for g in range(groups)]
    down = [(g, (g - 2) % groups) for g in range(groups)]
    opposite = [(g, (g + 4) % groups) for g in range(groups)]
    apart = [(g, (g + 2 - 4 * (g % 2)) % groups) for g in range(groups)]
    along = [(g * nz + z, g * nz + (z + 1 - 2 * (g % 2)) % nz) for g in range(groups) for z in range(nz)]
    beside = [(g * ny + y, g * ny + (y - 1 + 2 * (g % 2)) % ny) for g in range(groups) for y in range(ny)]
    pairs = [[g * ny + y for g in range(groups) for y in (p, p + 2)] for p in range(2)]
    limit = pltpu.CompilerParams(vmem_limit_bytes=32 * 2**20)
    core = lax.rem(lax.axis_index("grp"), 2)
    barrier = lax.optimization_barrier

    both = jnp.stack([block_tiles, assign])
    mine = integrals[0]
    other = lax.ppermute(mine, "grp", swap)
    moved = lax.all_to_all(amplitudes[0].reshape(groups, octet, cap), "grp", 0, 0, tiled=True)
    shift = (cap // TP).bit_length()
    little = pltpu.CompilerParams(vmem_limit_bytes=8 * 2**20)
    listed = pl.pallas_call(
        functools.partial(list_tiles, groups, share, shift),
        out_shape=jax.ShapeDtypeStruct((groups // 2 * share,), jnp.int32),
        in_specs=[SMEM],
        out_specs=SMEM,
        scratch_shapes=small,
        compiler_params=little,
    )(both)
    packed = jax.ShapeDtypeStruct((2 * groups, octet, wide // 2), jnp.bfloat16)
    packed = pl.pallas_call(
        functools.partial(pack_amplitudes, groups, share, shift),
        out_shape=packed,
        in_specs=[SMEM, VMEM],
        out_specs=pl.BlockSpec(memory_space=pltpu.HBM),
        scratch_shapes=[pltpu.VMEM(packed.shape, packed.dtype), pltpu.SemaphoreType.DMA((groups // 2,))],
        compiler_params=little,
    )(listed, moved)
    pair = lax.all_to_all(packed, ("grp", "row"), 0, 0, axis_index_groups=pairs, tiled=True)

    tiles = jax.ShapeDtypeStruct((wide, cols), jnp.bfloat16)
    scratch = small + [pltpu.SemaphoreType.DMA((share,))]
    sent = pl.pallas_call(
        functools.partial(send_tiles, groups, share),
        out_shape=tiles,
        in_specs=[SMEM, ANY, ANY],
        out_specs=VMEM,
        scratch_shapes=scratch,
        compiler_params=limit,
    )(both, mine, other)
    pair, sent = barrier((pair, sent))
    got = lax.ppermute(sent, "grp", apart)
    def half_of(block):
        h = block.shape[1] // 2
        return jnp.where(core == 0, block[:, :h], block[:, h:])

    def z_step(block):
        return lax.ppermute(block, ("grp", "col"), along)

    def y_step(block):
        return lax.ppermute(block, ("grp", "row"), beside)

    pair_too = lax.ppermute(pair, "grp", swap)
    block = half_of(jnp.stack([pair, pair_too]))
    order = [block]
    block, near = barrier((jnp.stack([z_step(pair), z_step(pair_too)]), y_step(block)))
    order += [near]
    for s in range(1, nz // 2 - 1):
        order += [block]
        block, near = z_step(block), y_step(block)
        if s < nz // 2 - 2:
            block, near = barrier((block, near))
        if s == nz // 2 - 3:
            block, near, got = barrier((block, near, got))
        order += [near]
    theirs = [lax.ppermute(part, "grp", swap) for part in jnp.split(got, 2)]
    end = z_step(half_of(block))
    order += [block, y_step(block), end, y_step(end)]

    held = pl.pallas_call(
        functools.partial(join_tiles, groups, share),
        out_shape=tiles,
        in_specs=[SMEM] + [VMEM] * (3 + len(theirs)),
        out_specs=VMEM,
        scratch_shapes=small,
        compiler_params=limit,
    )(both, mine, other, got, *theirs)

    def sums(parts):
        n = sum(part.shape[1] for part in parts) * octet
        return pl.pallas_call(
            functools.partial(multiply, ny),
            out_shape=jax.ShapeDtypeStruct((ny, n // 4, cols), jnp.float32),
            in_specs=[VMEM] * (len(parts) + 1),
            out_specs=VMEM,
            scratch_shapes=[pltpu.VMEM((n, wide), jnp.bfloat16)],
            compiler_params=limit,
        )(*parts, held)

    early, late = sums(order[:6]), order[6:]
    a, b = near_chips(early, up, down)
    a, b = collect(a, b)
    *late, a, b = barrier((*late, a, b))
    late = sums(late)
    h, n = early.shape[1] // 2, late.shape[1]
    (c,) = collect(lax.ppermute(late[2], "grp", opposite))
    a2 = lax.ppermute(jnp.concatenate([late[1], early[1, :h] + a[:h]]), "grp", up)
    b2 = lax.ppermute(jnp.concatenate([late[3], early[3, h:] + b[:h]]), "grp", down)
    early = early[0] + jnp.concatenate([a2[n:], a[h:]]) + jnp.concatenate([b[h:], b2[n:]])
    done = jnp.concatenate([early, late[0] + a2[:n] + b2[:n] + c])
    return pl.pallas_call(
        functools.partial(finish, nz, rows),
        out_shape=jax.ShapeDtypeStruct((nz // 2 * rows, cols), jnp.float32),
        in_specs=[VMEM, VMEM],
        out_specs=VMEM,
        compiler_params=pltpu.CompilerParams(vmem_limit_bytes=8 * 2**20),
    )(done, lax.ppermute(done, "grp", swap))


def solution(mesh):
    in_specs = (P("grp", ("row", "col"), None), P("grp", None, ("row", "col")), P(), P())
    out_specs = P("grp", ("row", "col"))
    return jax.shard_map(body, mesh=mesh, in_specs=in_specs, out_specs=out_specs, check_vma=False)
```

```python
import functools

import jax
import jax.numpy as jnp
from jax import lax
from jax.experimental import pallas as pl
from jax.experimental.pallas import tpu as pltpu
from jax.sharding import PartitionSpec as P

TP = 128
ANY = pl.BlockSpec(memory_space=pl.ANY)
SMEM = pl.BlockSpec(memory_space=pltpu.SMEM)
VMEM = pl.BlockSpec(memory_space=pltpu.VMEM)


def balance(both_ref, held_ref, block_ref, groups):
    for b in range(groups):
        held_ref[both_ref[1, b]] = both_ref[0, b]
        block_ref[both_ref[1, b]] = b
    chips = groups // 2
    held = [held_ref[s] for s in range(groups)]
    total = [held[2 * x] + held[2 * x + 1] for x in range(chips)]
    share = 0
    for x in range(chips):
        share = share + total[x]
    share = share // chips
    running, prefix = 0, []
    for x in range(chips):
        running = running + total[x] - share
        prefix.append(running)
    high = functools.reduce(jnp.maximum, prefix)
    low = functools.reduce(jnp.minimum, prefix)
    middle = lax.shift_right_arithmetic(high + low, jnp.int32(1))
    flow = [p - middle for p in prefix]
    right = [jnp.maximum(flow[x], 0) for x in range(chips)]
    left = [jnp.maximum(-flow[(x - 1) % chips], 0) for x in range(chips)]
    return held, total, right, left


def pick(values, index):
    out = values[0]
    for i in range(1, len(values)):
        out = jnp.where(index == i, values[i], out)
    return out


def runs_of(x, total, right, left, chips):
    if isinstance(x, int):
        xl, xr = (x - 1) % chips, (x + 1) % chips
        n, m, t, k = right[xl], left[xr], total[xl], left[x]
    else:
        xl, xr = lax.rem(x + chips - 1, chips), lax.rem(x + 1, chips)
        n, m, t, k = pick(right, xl), pick(left, xr), pick(total, xl), pick(left, x)
    return (xl, t - n, n), (xr, 0, m), (x, k, None)


def list_tiles(groups, share, shift, both_ref, out_ref, held_ref, block_ref):
    held, total, right, left = balance(both_ref, held_ref, block_ref, groups)
    blocks = [block_ref[s] << shift for s in range(groups)]
    for x in range(groups // 2):
        place = x * share
        for chip, start, count in runs_of(x, total, right, left, groups // 2):
            if count is None:
                count = (x + 1) * share - place
            n0 = jnp.clip(held[2 * chip] - start, 0, count)
            second = jnp.maximum(start - held[2 * chip], 0)
            for first, many in ((blocks[2 * chip] + start, n0), (blocks[2 * chip + 1] + second, count - n0)):

                def note(i, carry, first=first, place=place):
                    out_ref[place + i] = first + i
                    return carry

                lax.fori_loop(0, many, note, 0)
                place = place + many


def pack_amplitudes(groups, share, shift, list_ref, src_ref, out_ref, packed_ref, sems):
    each = share // 2
    copies = []
    for x in range(groups // 2):
        for p in range(share):
            entry = list_ref[x * share + p]
            tile = pl.multiple_of((entry & ((1 << shift) - 1)) * TP, TP)
            data = src_ref[lax.shift_right_logical(entry, jnp.int32(shift)), :, pl.ds(tile, TP)]
            at = p % each * TP
            for j in range(2):
                packed_ref[4 * x + p // each * 2 + j, :, at : at + TP] = data
        part = pl.ds(4 * x, 4)
        copies.append(pltpu.make_async_copy(packed_ref.at[part], out_ref.at[part], sems.at[x]))
        copies[-1].start()
    for copy in copies:
        copy.wait()


def tile_rows(index):
    return pl.ds(pl.multiple_of(index * TP, TP), TP)


def run_copies(jobs, out_ref, sems):
    for phase in range(2):
        for source, tile, many, place in jobs:

            def move(i, carry, source=source, tile=tile, place=place):
                copy = pltpu.make_async_copy(source.at[tile_rows(tile + i)], out_ref.at[tile_rows(place + i)], sems.at[place + i])
                copy.start() if phase == 0 else copy.wait()
                return carry

            lax.fori_loop(0, many, move, 0)


def own_tiles(border, core, start, count, mine_ref, other_ref, place):
    lower = jnp.clip(border - start, 0, count)
    jobs = []
    for upper, tile, many, at in ((0, start, lower, place), (1, jnp.maximum(start - border, 0), count - lower, place + lower)):
        jobs.append((mine_ref, tile, jnp.where(core == upper, many, 0), at))
        jobs.append((other_ref, tile, jnp.where(core != upper, many, 0), at))
    return jobs


def send_tiles(groups, share, both_ref, mine_ref, other_ref, out_ref, held_ref, block_ref, sems):
    held, total, right, left = balance(both_ref, held_ref, block_ref, groups)
    group = lax.axis_index("grp")
    x, core = lax.div(group, 2), lax.rem(group, 2)
    go_right, go_left = pick(right, x), pick(left, x)
    start = jnp.where(core == 0, pick(total, x) - go_right, 0)
    count = jnp.where(core == 0, go_right, go_left)
    run_copies(own_tiles(pick(held[0::2], x), core, start, count, mine_ref, other_ref, 0), out_ref, sems)


def join_tiles(groups, share, both_ref, mine_ref, other_ref, got_ref, *refs):
    *their_refs, out_ref, held_ref, block_ref = refs
    held, total, right, left = balance(both_ref, held_ref, block_ref, groups)
    group = lax.axis_index("grp")
    x, core = lax.div(group, 2), lax.rem(group, 2)
    (_, _, n), (_, _, m), (_, start, _) = runs_of(x, total, right, left, groups // 2)
    jobs = [
        (got_ref, 0, jnp.where(core == 0, n, 0), 0),
        (got_ref, 0, jnp.where(core == 0, 0, m), n),
    ]
    each = share // len(their_refs)
    for i, ref in enumerate(their_refs):
        jobs.append((ref, 0, jnp.clip(jnp.where(core == 0, m, n) - i * each, 0, each), jnp.where(core == 0, n, 0) + i * each))
    jobs += own_tiles(pick(held[0::2], x), core, start, share - n - m, mine_ref, other_ref, n + m)
    for source, tile, many, place in jobs:

        def move(i, carry, source=source, tile=tile, place=place):
            out_ref[tile_rows(place + i), :] = source[tile_rows(tile + i), :]
            return carry

        lax.fori_loop(0, many, move, 0)


def multiply(ny, *refs):
    refs, (b_ref, out_ref, a_ref) = refs[:-3], refs[-3:]
    group, y = lax.axis_index("grp"), lax.axis_index("row")
    x, core = lax.div(group, 2), lax.rem(group, 2)
    at = 0
    for ref in refs:
        _, n, octet, each = ref.shape
        for k in range(2):
            a_ref[at : at + n * octet, k * each : (k + 1) * each] = ref[k].reshape(n * octet, each)
        at += n * octet
    first = pl.ds(pl.multiple_of(core * each, each), each)
    last = pl.ds(pl.multiple_of((1 - core) * each, each), each)
    out = jnp.dot(a_ref[:, :each], b_ref[first, :], preferred_element_type=jnp.float32)
    out += jnp.dot(a_ref[:, each:], b_ref[last, :], preferred_element_type=jnp.float32)
    at = row = 0
    for i, ref in enumerate(refs):
        _, n, octet, _ = ref.shape
        for j in range(2):
            d = lax.rem(lax.rem(y + i % 2, 2) + 2 * j - x + ny, ny)
            for g in range(n // 2):
                start = at + (2 * g + j) * octet
                out_ref[d, row + g * octet : row + (g + 1) * octet, :] = out[start : start + octet]
        at += n * octet
        row += n // 2 * octet if i % 2 else 0


def finish(nz, rows, mine_ref, other_ref, out_ref):
    core, z = lax.rem(lax.axis_index("grp"), 2), lax.axis_index("col")
    h = rows // 2
    last = nz // 2 * rows - h
    for q in range(nz // 2):
        r = lax.rem(core * (nz // 2) + q - z + nz, nz)
        ends = jnp.logical_or(r == 0, r == nz // 2)
        above = r < nz // 2
        step = jnp.where(above, r, nz - r)
        for part in range(2):
            start = jnp.where(r == 0, 0, jnp.where(r == nz // 2, last, h + rows * (step - 1) + part * h))
            holder = jnp.where(ends, part, jnp.where(above, 1, 0))
            rows_in = pl.ds(pl.multiple_of(start, h), h)
            for ref, here in ((mine_ref, holder == core), (other_ref, holder != core)):

                @pl.when(here)
                def _(ref=ref, q=q, part=part, rows_in=rows_in):
                    out_ref[q * rows + part * h : q * rows + (part + 1) * h, :] = ref[rows_in, :]


def near_chips(p, up, down):
    h = p.shape[1] // 2
    a = lax.ppermute(jnp.concatenate([p[2, :h], p[1, h:]]), "grp", up)
    return a, lax.ppermute(jnp.concatenate([p[2, h:], p[3, :h]]), "grp", down)


def body(amplitudes, integrals, block_tiles, assign):
    groups = assign.shape[0]
    _, rows, cap = amplitudes.shape
    cols = integrals.shape[2]
    ny, nz = lax.axis_size("row"), lax.axis_size("col")
    share = 24
    wide = share * TP
    octet = rows // groups
    small = [pltpu.SMEM((groups,), jnp.int32)] * 2
    swap = [(g, g ^ 1) for g in range(groups)]
    up = [(g, (g + 2) % groups) for g in range(groups)]
    down = [(g, (g - 2) % groups) for g in range(groups)]
    opposite = [(g, (g + 4) % groups) for g in range(groups)]
    apart = [(g, (g + 2 - 4 * (g % 2)) % groups) for g in range(groups)]
    along = [(g * nz + z, g * nz + (z + 1 - 2 * (g % 2)) % nz) for g in range(groups) for z in range(nz)]
    beside = [(g * ny + y, g * ny + (y - 1 + 2 * (g % 2)) % ny) for g in range(groups) for y in range(ny)]
    pairs = [[g * ny + y for g in range(groups) for y in (p, p + 2)] for p in range(2)]
    limit = pltpu.CompilerParams(vmem_limit_bytes=32 * 2**20)
    core = lax.rem(lax.axis_index("grp"), 2)
    barrier = lax.optimization_barrier

    both = jnp.stack([block_tiles, assign])
    mine = integrals[0]
    other = lax.ppermute(mine, "grp", swap)
    moved = lax.all_to_all(amplitudes[0].reshape(groups, octet, cap), "grp", 0, 0, tiled=True)
    shift = (cap // TP).bit_length()
    little = pltpu.CompilerParams(vmem_limit_bytes=8 * 2**20)
    listed = pl.pallas_call(
        functools.partial(list_tiles, groups, share, shift),
        out_shape=jax.ShapeDtypeStruct((groups // 2 * share,), jnp.int32),
        in_specs=[SMEM],
        out_specs=SMEM,
        scratch_shapes=small,
        compiler_params=little,
    )(both)
    packed = jax.ShapeDtypeStruct((2 * groups, octet, wide // 2), jnp.bfloat16)
    packed = pl.pallas_call(
        functools.partial(pack_amplitudes, groups, share, shift),
        out_shape=packed,
        in_specs=[SMEM, VMEM],
        out_specs=pl.BlockSpec(memory_space=pltpu.HBM),
        scratch_shapes=[pltpu.VMEM(packed.shape, packed.dtype), pltpu.SemaphoreType.DMA((groups // 2,))],
        compiler_params=pltpu.CompilerParams(vmem_limit_bytes=60 * 2**20),
    )(listed, moved)
    pair = lax.all_to_all(packed, ("grp", "row"), 0, 0, axis_index_groups=pairs, tiled=True)

    tiles = jax.ShapeDtypeStruct((wide, cols), jnp.bfloat16)
    scratch = small + [pltpu.SemaphoreType.DMA((share,))]
    sent = pl.pallas_call(
        functools.partial(send_tiles, groups, share),
        out_shape=tiles,
        in_specs=[SMEM, ANY, ANY],
        out_specs=VMEM,
        scratch_shapes=scratch,
        compiler_params=limit,
    )(both, mine, other)
    pair, sent = barrier((pair, sent))
    got = lax.ppermute(sent, "grp", apart)
    def half_of(block):
        h = block.shape[1] // 2
        return jnp.where(core == 0, block[:, :h], block[:, h:])

    def z_step(block):
        return lax.ppermute(block, ("grp", "col"), along)

    def y_step(block):
        return lax.ppermute(block, ("grp", "row"), beside)

    pair_too = lax.ppermute(pair, "grp", swap)
    block = half_of(jnp.stack([pair, pair_too]))
    order = [block]
    block, near = barrier((jnp.stack([z_step(pair), z_step(pair_too)]), y_step(block)))
    order += [near]
    for s in range(1, nz // 2 - 1):
        order += [block]
        block, near = z_step(block), y_step(block)
        if s < nz // 2 - 2:
            block, near = barrier((block, near))
        if s == nz // 2 - 3:
            block, near, got = barrier((block, near, got))
        order += [near]
    theirs = [lax.ppermute(part, "grp", swap) for part in jnp.split(got, 2)]
    end = z_step(half_of(block))
    order += [block, y_step(block), end, y_step(end)]

    held = pl.pallas_call(
        functools.partial(join_tiles, groups, share),
        out_shape=tiles,
        in_specs=[SMEM] + [VMEM] * (3 + len(theirs)),
        out_specs=VMEM,
        scratch_shapes=small,
        compiler_params=limit,
    )(both, mine, other, got, *theirs)

    def sums(parts):
        n = sum(part.shape[1] for part in parts) * octet
        return pl.pallas_call(
            functools.partial(multiply, ny),
            out_shape=jax.ShapeDtypeStruct((ny, n // 4, cols), jnp.float32),
            in_specs=[VMEM] * (len(parts) + 1),
            out_specs=VMEM,
            scratch_shapes=[pltpu.VMEM((n, wide), jnp.bfloat16)],
            compiler_params=limit,
        )(*parts, held)

    early, late = sums(order[:6]), order[6:]
    a, b = near_chips(early, up, down)
    *late, a, b = barrier((*late, a, b))
    late = sums(late)
    h, n = early.shape[1] // 2, late.shape[1]
    c = lax.ppermute(late[2], "grp", opposite)
    a2 = lax.ppermute(jnp.concatenate([late[1], early[1, :h] + a[:h]]), "grp", up)
    b2 = lax.ppermute(jnp.concatenate([late[3], early[3, h:] + b[:h]]), "grp", down)
    early = early[0] + jnp.concatenate([a2[n:], a[h:]]) + jnp.concatenate([b[h:], b2[n:]])
    done = jnp.concatenate([early, late[0] + a2[:n] + b2[:n] + c])
    return pl.pallas_call(
        functools.partial(finish, nz, rows),
        out_shape=jax.ShapeDtypeStruct((nz // 2 * rows, cols), jnp.float32),
        in_specs=[VMEM, VMEM],
        out_specs=VMEM,
        compiler_params=pltpu.CompilerParams(vmem_limit_bytes=8 * 2**20),
    )(done, lax.ppermute(done, "grp", swap))


def solution(mesh):
    in_specs = (P("grp", ("row", "col"), None), P("grp", None, ("row", "col")), P(), P())
    out_specs = P("grp", ("row", "col"))
    return jax.shard_map(body, mesh=mesh, in_specs=in_specs, out_specs=out_specs, check_vma=False)
```
